32 devices in a mesh: outer: 8 (over y, x, core), node: 4 (over z).
Axes of the slice: x: 2, y: 2, z: 4, core: 2. Of those that a mesh axis runs over, the one named last changes fastest.
Arguments:
- tokens: bfloat16 [8192, 14848], P(('outer', 'node')), may hold values from -6 to 6
- cotangent: bfloat16 [8192, 256], P(('outer', 'node')), may hold values from -0.06591797 to 0.06591797
- weight_codes: bfloat16 [14848, 256], P('node'), may hold values from -127 to 127, as said below
- weight_scales: float32 [14848, 2], P('node'), may hold values from 4.103326e-05 to 0.00024619958
- weight_bits: int32 [256], replicated, may hold values 0 or 1
- grad_bits: int32 [256], replicated, may hold values 0 or 1
Outputs:
- output: bfloat16 [8192, 256], P(('outer', 'node'))
- grad_rotated: float32 [14848, 256], P(('outer', 'node'))
The draws below stay inside these ranges and needn't reach their ends.
Inputs may be any that keep to these rules, and one draw needn't show every extreme that they name: `weight_codes`: whole numbers.
All inputs are finite; a program needn't handle non-finite values.
Results may differ from the reference program's by a relative error of at most 0.015.
Values may be sent and summed in bfloat16 or wider, within the bound.
No kernel may reach another device: no remote copies, remote signals or barrier semaphores. Data moves between devices by JAX's collectives and lax.ppermute only.
A program may use at most 128 MiB of HBM per device.

```python
import math
import jax
import jax.numpy as jnp
import numpy as np
from jax import lax

D = 14848
SLAB = 256
TOKENS = 8192


def draw_weight_codes(key, part):
    key = jax.random.fold_in(key, 11)
    values = jax.random.randint(key, (D, SLAB), -127, 128)
    return values.astype(jnp.float32).astype(jnp.bfloat16)


def set_ends(entries, key, least, largest):
    spot = [jax.random.randint(jax.random.fold_in(key, axis), (), 0, length) for axis, length in enumerate(entries.shape)]
    main_axis = entries.shape.index(max(entries.shape))
    beside = spot[:main_axis] + [(spot[main_axis] + 1) % entries.shape[main_axis]] + spot[main_axis + 1:]
    return entries.at[tuple(spot)].set(least).at[tuple(beside)].set(largest)


def spiked(entries, rng, source, target, parts, factor):
    def block_of(axis_at):
        return (jnp.arange(entries.shape[axis_at]) // (entries.shape[axis_at] // parts)).reshape((-1,) + (1,) * (entries.ndim - 1 - axis_at))

    first = jax.random.permutation(rng, parts)[block_of(target)]
    far = (block_of(target) + parts // 2) % parts
    return jnp.where((block_of(source) == first) | (block_of(source) == far), factor * entries, entries)


def shard_levels(key, shape, pieces, low, top_value):
    gain = 1.0
    for axis_at, blocks in pieces:
        steps = jax.random.uniform(jax.random.fold_in(jax.random.fold_in(key, 6), axis_at), (blocks,), jnp.float32, low / len(pieces), top_value / len(pieces))
        gain = gain * jnp.repeat(jnp.exp(steps), shape[axis_at] // blocks).reshape((-1,) + (1,) * (len(shape) - 1 - axis_at))
    return gain


def noise(own_key, dims, deviation, reach, cuts=(), dtype=jnp.bfloat16):
    values = deviation * jax.random.normal(own_key, dims, jnp.float32)
    if cuts:
        values = values * shard_levels(own_key, dims, cuts, -0.22, 0.18)
    return jnp.clip(values, -reach, reach).astype(dtype)


def heavy_noise(rng, shape, scale, bound, split, heavy, kind=jnp.bfloat16):
    entries = scale * jax.random.normal(rng, shape, jnp.float32)
    if split:
        entries = entries * shard_levels(rng, shape, split, -0.22, 0.18)
    return jnp.clip(spiked(entries, jax.random.fold_in(rng, 3), *heavy), -bound, bound).astype(kind)


def setup_inputs(seed: int = 0) -> dict:
    seeds = jax.random.split(jax.random.key(seed), 7)
    tokens = heavy_noise(seeds[0], (TOKENS, D), 1.0, 6.0, ((0, 32),), (0, 1, 32, 2.75))
    cotangent = noise(seeds[1], (TOKENS, SLAB), (TOKENS ** -0.5), 0.06591797, ((0, 32),))
    weight_codes = draw_weight_codes(jax.random.fold_in(seeds[6], 71), 0)
    weight_scales = jnp.clip(jnp.exp(math.log(0.00024619958) - 1.7917595 * jax.random.uniform(seeds[3], (D, SLAB // 128), jnp.float32) ** shard_levels(seeds[3], (D, SLAB // 128), ((0, 4),), -0.2, 0.2)), 4.1033261368284e-05, 0.00024619958)
    weight_bits = set_ends((jax.random.randint(seeds[4], (SLAB,), 0, 2) < 1).astype(jnp.int32), jax.random.fold_in(seeds[4], 1), 0, 1)
    grad_bits = set_ends((jax.random.randint(seeds[5], (SLAB,), 0, 2) < 1).astype(jnp.int32), jax.random.fold_in(seeds[5], 1), 0, 1)
    return {"tokens": tokens, "cotangent": cotangent, "weight_codes": weight_codes, "weight_scales": weight_scales, "weight_bits": weight_bits, "grad_bits": grad_bits}


def sylvester():
    row_index = np.arange(128).reshape(128, 1)
    column_index = np.arange(128).reshape(1, 128)
    parity = np.zeros((128, 128))
    for level in range(7):
        parity = parity + row_index // 2 ** level % 2 * (column_index // 2 ** level % 2)
    return 1.0 - 2.0 * (parity % 2)

def rotate(values, bits):
    height, width = values.shape
    signs = (2 * bits - 1).astype(jnp.float32)
    table = jnp.asarray(sylvester(), jnp.float32) / math.sqrt(128.0)
    blocks = (values * signs).reshape(height, width // 128, 128)
    return jnp.einsum('rbi,ij->rbj', blocks, table, precision=lax.Precision.HIGHEST).reshape(height, width)

def dequantize(codes, scales):
    height, width = codes.shape
    blocks = codes.astype(jnp.float32).reshape(height, width // 128, 128)
    return (blocks * scales[:, :, None]).reshape(height, width)

def reference(tokens, cotangent, weight_codes, weight_scales, weight_bits, grad_bits):
    weight = rotate(dequantize(weight_codes, weight_scales), weight_bits).astype(jnp.bfloat16)
    output = jnp.dot(tokens, weight, preferred_element_type=jnp.float32).astype(jnp.bfloat16)
    grad = lax.dot_general(tokens, cotangent, (((0,), (0,)), ((), ())), preferred_element_type=jnp.float32)
    return (output, rotate(grad, grad_bits))
```

```python
import math

import jax
import jax.numpy as jnp
import numpy as np
from jax import lax
from jax.sharding import PartitionSpec as P


def sylvester():
    row_index = np.arange(128).reshape(128, 1)
    column_index = np.arange(128).reshape(1, 128)
    parity = np.zeros((128, 128))
    for level in range(7):
        parity = parity + row_index // 2**level % 2 * (column_index // 2**level % 2)
    return 1.0 - 2.0 * (parity % 2)


def rotate(values, bits):
    width = values.shape[1]
    signs = (2 * bits - 1).astype(jnp.float32)
    table = np.kron(np.eye(width // 128), sylvester()) / math.sqrt(128.0)
    return jnp.dot(
        values * signs,
        jnp.asarray(table, jnp.float32),
        precision=lax.Precision.HIGHEST,
    )


def dequantize(codes, scales):
    height, width = codes.shape
    spread = jnp.concatenate(
        [
            jnp.broadcast_to(scales[:, block : block + 1], (height, 128))
            for block in range(width // 128)
        ],
        axis=1,
    )
    return codes.astype(jnp.float32) * spread


def solution(mesh):
    n_outer = mesh.shape["outer"]
    n_node = mesh.shape["node"]
    n_bits = n_outer.bit_length() - 1
    orders = [list(range(1, n_bits)), [2, 1] + list(range(3, n_bits))]

    def outer_swap(value, stage):
        pairs = []
        for o in range(n_outer):
            pairs.append((o, o ^ (1 if stage is None else 1 << orders[o % 2][stage])))
        return lax.ppermute(value, "outer", pairs)

    def node_shift(value, step):
        return lax.ppermute(value, "node", [(n, (n + step) % n_node) for n in range(n_node)])

    def on_device(tokens, cotangent, weight_codes, weight_scales, weight_bits, grad_bits):
        o = lax.axis_index("outer")
        n = lax.axis_index("node")
        core = o % 2
        width = tokens.shape[1]
        slab = cotangent.shape[1]

        part = weight_codes.shape[0] // 4
        side = jnp.where(core == 0, (o >> orders[0][0]) % 2, (o >> orders[1][0]) % 2)
        mate_side = jnp.where(core == 0, (o >> orders[1][0]) % 2, (o >> orders[0][0]) % 2)
        quarter = core * 2 + side
        start = quarter * part
        held = rotate(
            dequantize(
                lax.dynamic_slice_in_dim(weight_codes, start, part),
                lax.dynamic_slice_in_dim(weight_scales, start, part),
            ),
            weight_bits,
        ).astype(jnp.bfloat16)

        total = lax.dot_general(
            tokens, cotangent, (((0,), (0,)), ((), ())), preferred_element_type=jnp.float32
        ).astype(jnp.bfloat16)
        rows = width // n_outer
        blocks = {}

        def own(d):
            return lax.dynamic_slice_in_dim(total, (o ^ d) * rows, rows)

        def relative(mask):
            found = [0, 0]
            for c in range(2):
                for j, bit in enumerate(orders[c]):
                    if mask >> j & 1:
                        found[c] |= 1 << bit
            return jnp.where(core == 0, found[0], found[1])

        n_rest = n_bits - 1
        sums = {}
        for mask in reversed(range(2**n_rest)):
            partner = jnp.where(core == 0, relative_of(orders, 1, mask), relative_of(orders, 0, mask))
            came = outer_swap(own(partner ^ 1), None)
            sums[mask] = own(relative(mask)).astype(jnp.float32) + came.astype(jnp.float32)
        for stage in range(n_rest):
            low = 1 << stage
            for mask in sorted([m for m in sums if m & low], reverse=True):
                came = outer_swap(sums.pop(mask).astype(jnp.bfloat16), stage)
                sums[mask ^ low] = sums[mask ^ low] + came.astype(jnp.float32)
        mine = sums[0]
        share = rows // n_node
        send = mine.astype(jnp.bfloat16)
        grad = lax.dynamic_slice_in_dim(mine, n * share, share)
        for step in range(1, n_node):
            piece = lax.dynamic_slice_in_dim(send, (n + step) % n_node * share, share)
            grad = grad + node_shift(piece, step).astype(jnp.float32)
        grad_rotated = rotate(grad, grad_bits)

        weight = jnp.zeros((width, slab), jnp.bfloat16)
        node_rows = weight_codes.shape[0]
        for step in range(n_node):
            base = (n - step) % n_node * node_rows
            across = outer_swap(held, 0)
            mate = outer_swap(held, None)
            mate_across = outer_swap(across, None)
            pieces = [
                (held, core * 2 + side),
                (across, core * 2 + 1 - side),
                (mate, (1 - core) * 2 + mate_side),
                (mate_across, (1 - core) * 2 + 1 - mate_side),
            ]
            for value, place in pieces:
                weight = lax.dynamic_update_slice_in_dim(weight, value, base + place * part, 0)
            if step < n_node - 1:
                held = node_shift(held, 1)
        output = jnp.dot(tokens, weight, preferred_element_type=jnp.float32).astype(jnp.bfloat16)
        return output, grad_rotated

    return jax.shard_map(
        on_device,
        mesh=mesh,
        in_specs=(
            P(("outer", "node"), None),
            P(("outer", "node"), None),
            P("node", None),
            P("node", None),
            P(),
            P(),
        ),
        out_specs=(P(("outer", "node"), None), P(("outer", "node"), None)),
        check_vma=False,
    )


def relative_of(orders, core, mask):
    found = 0
    for j, bit in enumerate(orders[core]):
        if mask >> j & 1:
            found |= 1 << bit
    return found
```

```python
import math

import jax
import jax.numpy as jnp
import numpy as np
from jax import lax
from jax.experimental import pallas as pl
from jax.experimental.pallas import tpu as pltpu
from jax.sharding import PartitionSpec as P


def sylvester():
    row_index = np.arange(128).reshape(128, 1)
    column_index = np.arange(128).reshape(1, 128)
    parity = np.zeros((128, 128))
    for level in range(7):
        parity = parity + row_index // 2**level % 2 * (column_index // 2**level % 2)
    return 1.0 - 2.0 * (parity % 2)


def rotate(values, bits):
    width = values.shape[1]
    signs = (2 * bits - 1).astype(jnp.float32)
    table = np.kron(np.eye(width // 128), sylvester()) / math.sqrt(128.0)
    return jnp.dot(
        values * signs,
        jnp.asarray(table, jnp.float32),
        precision=lax.Precision.HIGHEST,
    )


def dequantize(codes, scales):
    height, width = codes.shape
    spread = jnp.concatenate(
        [
            jnp.broadcast_to(scales[:, block : block + 1], (height, 128))
            for block in range(width // 128)
        ],
        axis=1,
    )
    return codes.astype(jnp.float32) * spread


def relative_of(orders, core, mask):
    found = 0
    for j, bit in enumerate(orders[core]):
        if mask >> j & 1:
            found |= 1 << bit
    return found


CONTRACT_ROWS = (((0,), (0,)), ((), ()))


def after(value, *deps):
    return lax.optimization_barrier((value, *deps))[0]


def grad_blocks(index, tokens, far, cotangent, cot_far, earlier, rows, share, window, kind):
    n_share = rows // share
    step = 384

    def kernel(index, tok, far, cot, cot_far, earlier, out, left, held, sems, out_sems):
        copies = []
        for i in range(2):
            start = pl.multiple_of(index[i], 128)
            copies.append(
                (
                    pltpu.make_async_copy(
                        tok.at[:, pl.ds(start, window)], left.at[i, 0], sems.at[i, 0]
                    ),
                    pltpu.make_async_copy(
                        far.at[:, pl.ds(i * window, window)], left.at[i, 1], sems.at[i, 1]
                    ),
                )
            )
        for pair in copies:
            for copy in pair:
                copy.start()
        skip = index[2]
        place = index[3]
        done = []
        for i in range(2):
            for copy in copies[i]:
                copy.wait()
            for j in range(window // step):
                cols = pl.ds(j * step, step)
                held[i, cols, :] = (
                    lax.dot_general(
                        left[i, 0, :, cols], cot[...], CONTRACT_ROWS,
                        preferred_element_type=jnp.float32,
                    )
                    + lax.dot_general(
                        left[i, 1, :, cols], cot_far[...], CONTRACT_ROWS,
                        preferred_element_type=jnp.float32,
                    )
                ).astype(kind)
            for k in range(n_share):
                source = pl.multiple_of(skip + lax.rem(place + k, n_share) * share, 16)
                done.append(
                    pltpu.make_async_copy(
                        held.at[i, pl.ds(source, share)],
                        out.at[pl.ds(i * rows + k * share, share)],
                        out_sems.at[i, k],
                    )
                )
                done[-1].start()
        for copy in done:
            copy.wait()

    depth, slab = cotangent.shape
    anywhere = pl.BlockSpec(memory_space=pl.ANY)
    whole = pl.BlockSpec(memory_space=pltpu.VMEM)
    return pl.pallas_call(
        kernel,
        out_shape=jax.ShapeDtypeStruct((2 * rows, slab), kind),
        in_specs=[pl.BlockSpec(memory_space=pltpu.SMEM), anywhere, anywhere, whole, whole, anywhere],
        out_specs=anywhere,
        scratch_shapes=[
            pltpu.VMEM((2, 2, depth, window), jnp.bfloat16),
            pltpu.VMEM((2, window, slab), kind),
            pltpu.SemaphoreType.DMA((2, 2)),
            pltpu.SemaphoreType.DMA((2, n_share)),
        ],
        compiler_params=pltpu.CompilerParams(vmem_limit_bytes=16 * 2**20),
        cost_estimate=pl.CostEstimate(
            flops=8 * depth * window * slab, bytes_accessed=16 * depth * window, transcendentals=0
        ),
    )(index, tokens, far, cotangent, cot_far, earlier)


def output_part(index, tokens, fars, pieces, before, earlier, part, window):
    steps = len(pieces)
    depth = tokens.shape[0]
    slab = pieces[0][0].shape[1]
    edge = window - 2 * part

    def kernel(index, tok, far_a, far_b, *refs):
        parts = refs[: 2 * steps]
        refs = refs[2 * steps + 1 :]
        if before is not None:
            old = refs[:2]
            refs = refs[2:]
        own, other, left, right, sems, piece_sems = refs
        waits = []
        for i in range(steps):
            right[i, 0:edge, :] = jnp.zeros((edge, slab), jnp.bfloat16)
            right[i, window - edge : window, :] = jnp.zeros((edge, slab), jnp.bfloat16)
            start = pl.multiple_of(index[4 * i], 128)
            slot = index[4 * i + 1]
            copy = pltpu.make_async_copy(
                tok.at[:, pl.ds(start, window)], left.at[i, pl.ds(0, depth)], sems.at[i, 0]
            )
            copy.start()
            column = pl.multiple_of(lax.rem(slot, 2) * window, 128)
            from_a = pltpu.make_async_copy(
                far_a.at[:, pl.ds(column, window)], left.at[i, pl.ds(depth, depth)], sems.at[i, 1]
            )
            from_b = pltpu.make_async_copy(
                far_b.at[:, pl.ds(column, window)], left.at[i, pl.ds(depth, depth)], sems.at[i, 1]
            )

            @pl.when(slot < 2)
            def _():
                from_a.start()

            @pl.when(slot >= 2)
            def _():
                from_b.start()

            waits.append([copy, from_a])
            for j in range(2):
                row = pl.multiple_of(index[4 * i + 2 + j], 16)
                piece = pltpu.make_async_copy(
                    parts[2 * i + j], right.at[i, pl.ds(row, part)], piece_sems.at[i, j]
                )
                piece.start()
                waits[-1].append(piece)
        total = None
        for i in range(steps):
            for copy in waits[i]:
                copy.wait()
            term = jnp.dot(left[i], right[i], preferred_element_type=jnp.float32)
            total = term if total is None else total + term
        if before is None:
            own[...] = total[:depth]
            other[...] = total[depth:]
        else:
            own[...] = total[:depth] + old[0][...]
            other[...] = total[depth:] + old[1][...]

    anywhere = pl.BlockSpec(memory_space=pl.ANY)
    whole = pl.BlockSpec(memory_space=pltpu.VMEM)
    shape = jax.ShapeDtypeStruct((depth, slab), jnp.float32)
    olds = () if before is None else tuple(before)
    return pl.pallas_call(
        kernel,
        out_shape=[shape, shape],
        in_specs=[pl.BlockSpec(memory_space=pltpu.SMEM)]
        + [anywhere] * (4 + 2 * steps)
        + [whole] * len(olds),
        out_specs=[whole, whole],
        scratch_shapes=[
            pltpu.VMEM((steps, 2 * depth, window), jnp.bfloat16),
            pltpu.VMEM((steps, window, slab), jnp.bfloat16),
            pltpu.SemaphoreType.DMA((steps, 2)),
            pltpu.SemaphoreType.DMA((steps, 2)),
        ],
        compiler_params=pltpu.CompilerParams(vmem_limit_bytes=(5 + 4 * steps) * 2**20),
        cost_estimate=pl.CostEstimate(
            flops=4 * steps * depth * window * slab,
            bytes_accessed=8 * steps * depth * window,
            transcendentals=0,
        ),
    )(index, tokens, *fars, *[p for pair in pieces for p in pair], earlier, *olds)


def paired(mesh):
    n_outer = mesh.shape["outer"]
    n_node = mesh.shape["node"]
    orders = [[1, 2], [2, 1]]

    def core_swap(value):
        return lax.ppermute(value, "outer", [(o, o ^ 1) for o in range(n_outer)])

    def outer_swap(value, stage):
        return lax.ppermute(
            value, "outer", [(o, o ^ (1 << orders[o % 2][stage])) for o in range(n_outer)]
        )

    def node_shift(value, step):
        return lax.ppermute(value, "node", [(n, (n + step) % n_node) for n in range(n_node)])

    def on_device(tokens, cotangent, weight_codes, weight_scales, weight_bits, grad_bits):
        o = lax.axis_index("outer")
        n = lax.axis_index("node")
        core = o % 2
        width = tokens.shape[1]
        rows = width // n_outer
        share = rows // n_node
        node_rows = weight_codes.shape[0]
        window = (rows + 127) // 128 * 128
        edge = window - rows

        def block(mask, mine):
            here = core if mine else 1 - core
            base = o if mine else o ^ 1
            return base ^ jnp.where(here == 0, relative_of(orders, 0, mask), relative_of(orders, 1, mask))

        def column(which):
            return which // 2 * node_rows + which % 2 * (node_rows - window)

        part = rows // 2
        side = jnp.where(core == 0, o >> 1, o >> 2) % 2
        start = core * rows + side * part
        held = rotate(
            dequantize(
                lax.dynamic_slice_in_dim(weight_codes, start, part),
                lax.dynamic_slice_in_dim(weight_scales, start, part),
            ),
            weight_bits,
        ).astype(jnp.bfloat16)

        def windows(masks):
            return core_swap(
                jnp.concatenate(
                    [
                        lax.dynamic_slice_in_dim(tokens, column(block(mask, False)), window, 1)
                        for mask in masks
                    ],
                    axis=1,
                )
            )

        cot_far = core_swap(cotangent)
        far_a = windows((3, 1))
        far_b = windows((2, 0))

        held = [held]
        across = [outer_swap(held[0], 0)]
        held.append(node_shift(held[0], 1))

        def grads(masks, far, kind):
            index = jnp.stack([column(block(mask, True)) for mask in masks] + [core * edge, n])
            return grad_blocks(
                index.astype(jnp.int32), tokens, far, cotangent, cot_far, held[0],
                rows, share, window, kind
            )

        came = outer_swap(grads((3, 1), far_a, jnp.bfloat16), 0)
        keep = grads((2, 0), far_b, jnp.float32)
        for step in range(1, n_node - 1):
            held.append(node_shift(held[step], 1))
        send2 = (keep[:rows] + came[:rows].astype(jnp.float32)).astype(jnp.bfloat16)
        came2 = outer_swap(send2, 1)
        for step in range(1, n_node):
            across.append(outer_swap(after(held[step], send2), 0))
        total = keep[rows:] + came[rows:].astype(jnp.float32) + came2.astype(jnp.float32)
        sends = [
            total[step * share : (step + 1) * share].astype(jnp.bfloat16)
            for step in range(1, n_node)
        ]
        grad = total[:share]
        first_send = grad
        for step in range(1, n_node):
            grad = grad + node_shift(sends[step - 1], step).astype(jnp.float32)
        grad_rotated = rotate(grad, grad_bits)

        def out_index(steps):
            found = []
            for step in steps:
                node = (n - step) % n_node
                pair = (node ^ (o >> 1)) % 4
                bits = jnp.where(core == 0, pair, (pair >> 1) + 2 * (pair % 2))
                slot = jnp.where(bits == 3, 0, jnp.where(bits == 1, 1, jnp.where(bits == 2, 2, 3)))
                found += [
                    column(node * 2 + core),
                    slot,
                    core * edge + side * part,
                    core * edge + (1 - side) * part,
                ]
            return jnp.stack(found).astype(jnp.int32)

        def product(steps, before):
            return output_part(
                out_index(steps),
                tokens,
                (far_a, far_b),
                [(held[step], across[step]) for step in steps],
                before,
                first_send,
                part,
                window,
            )

        sums = product((0, 1, 2), None)
        own, other = product((3,), sums)
        output = (own + core_swap(other)).astype(jnp.bfloat16)
        return output, grad_rotated

    return on_device


def general(mesh):
    n_outer = mesh.shape["outer"]
    n_node = mesh.shape["node"]
    n_bits = n_outer.bit_length() - 1
    orders = [list(range(1, n_bits)), [2, 1] + list(range(3, n_bits))]

    def outer_swap(value, stage):
        pairs = []
        for o in range(n_outer):
            pairs.append((o, o ^ (1 if stage is None else 1 << orders[o % 2][stage])))
        return lax.ppermute(value, "outer", pairs)

    def node_shift(value, step):
        return lax.ppermute(value, "node", [(n, (n + step) % n_node) for n in range(n_node)])

    def on_device(tokens, cotangent, weight_codes, weight_scales, weight_bits, grad_bits):
        o = lax.axis_index("outer")
        n = lax.axis_index("node")
        core = o % 2
        width = tokens.shape[1]
        slab = cotangent.shape[1]

        part = weight_codes.shape[0] // 4
        side = jnp.where(core == 0, (o >> orders[0][0]) % 2, (o >> orders[1][0]) % 2)
        mate_side = jnp.where(core == 0, (o >> orders[1][0]) % 2, (o >> orders[0][0]) % 2)
        quarter = core * 2 + side
        start = quarter * part
        held = rotate(
            dequantize(
                lax.dynamic_slice_in_dim(weight_codes, start, part),
                lax.dynamic_slice_in_dim(weight_scales, start, part),
            ),
            weight_bits,
        ).astype(jnp.bfloat16)

        total = lax.dot_general(
            tokens, cotangent, (((0,), (0,)), ((), ())), preferred_element_type=jnp.float32
        ).astype(jnp.bfloat16)
        rows = width // n_outer
        blocks = {}

        def own(d):
            return lax.dynamic_slice_in_dim(total, (o ^ d) * rows, rows)

        def relative(mask):
            found = [0, 0]
            for c in range(2):
                for j, bit in enumerate(orders[c]):
                    if mask >> j & 1:
                        found[c] |= 1 << bit
            return jnp.where(core == 0, found[0], found[1])

        n_rest = n_bits - 1
        sums = {}
        for mask in reversed(range(2**n_rest)):
            partner = jnp.where(core == 0, relative_of(orders, 1, mask), relative_of(orders, 0, mask))
            came = outer_swap(own(partner ^ 1), None)
            sums[mask] = own(relative(mask)).astype(jnp.float32) + came.astype(jnp.float32)
        for stage in range(n_rest):
            low = 1 << stage
            for mask in sorted([m for m in sums if m & low], reverse=True):
                came = outer_swap(sums.pop(mask).astype(jnp.bfloat16), stage)
                sums[mask ^ low] = sums[mask ^ low] + came.astype(jnp.float32)
        mine = sums[0]
        share = rows // n_node
        send = mine.astype(jnp.bfloat16)
        grad = lax.dynamic_slice_in_dim(mine, n * share, share)
        for step in range(1, n_node):
            piece = lax.dynamic_slice_in_dim(send, (n + step) % n_node * share, share)
            grad = grad + node_shift(piece, step).astype(jnp.float32)
        grad_rotated = rotate(grad, grad_bits)

        weight = jnp.zeros((width, slab), jnp.bfloat16)
        node_rows = weight_codes.shape[0]
        for step in range(n_node):
            base = (n - step) % n_node * node_rows
            across = outer_swap(held, 0)
            mate = outer_swap(held, None)
            mate_across = outer_swap(across, None)
            pieces = [
                (held, core * 2 + side),
                (across, core * 2 + 1 - side),
                (mate, (1 - core) * 2 + mate_side),
                (mate_across, (1 - core) * 2 + 1 - mate_side),
            ]
            for value, place in pieces:
                weight = lax.dynamic_update_slice_in_dim(weight, value, base + place * part, 0)
            if step < n_node - 1:
                held = node_shift(held, 1)
        output = jnp.dot(tokens, weight, preferred_element_type=jnp.float32).astype(jnp.bfloat16)
        return output, grad_rotated

    return on_device


def solution(mesh):
    n_outer = mesh.shape["outer"]
    n_node = mesh.shape["node"]
    on_device = paired(mesh) if n_outer == 8 and n_node == 4 else general(mesh)
    return jax.shard_map(
        on_device,
        mesh=mesh,
        in_specs=(
            P(("outer", "node"), None),
            P(("outer", "node"), None),
            P("node", None),
            P("node", None),
            P(),
            P(),
        ),
        out_specs=(P(("outer", "node"), None), P(("outer", "node"), None)),
        check_vma=False,
    )
```

```python
import math

import jax
import jax.numpy as jnp
import numpy as np
from jax import lax
from jax.experimental import pallas as pl
from jax.experimental.pallas import tpu as pltpu
from jax.sharding import PartitionSpec as P


def sylvester():
    row_index = np.arange(128).reshape(128, 1)
    column_index = np.arange(128).reshape(1, 128)
    parity = np.zeros((128, 128))
    for level in range(7):
        parity = parity + row_index // 2**level % 2 * (column_index // 2**level % 2)
    return 1.0 - 2.0 * (parity % 2)


def rotate(values, bits):
    width = values.shape[1]
    signs = (2 * bits - 1).astype(jnp.float32)
    table = np.kron(np.eye(width // 128), sylvester()) / math.sqrt(128.0)
    return jnp.dot(
        values * signs,
        jnp.asarray(table, jnp.float32),
        precision=lax.Precision.HIGHEST,
    )


def dequantize(codes, scales):
    height, width = codes.shape
    spread = jnp.concatenate(
        [
            jnp.broadcast_to(scales[:, block : block + 1], (height, 128))
            for block in range(width // 128)
        ],
        axis=1,
    )
    return codes.astype(jnp.float32) * spread


def relative_of(orders, core, mask):
    found = 0
    for j, bit in enumerate(orders[core]):
        if mask >> j & 1:
            found |= 1 << bit
    return found


PACK_MEMORY = 50 * 2**20
SMALL = pl.CostEstimate(flops=0, bytes_accessed=1024, transcendentals=0)
LONG = pl.CostEstimate(flops=5 * 10**9, bytes_accessed=1024, transcendentals=0)
CONTRACT_ROWS = (((0,), (0,)), ((), ()))


def after(value, *deps):
    return lax.optimization_barrier((value, *deps))[0]


def pack_windows(index, tokens, window):
    n_arrays = 4

    def kernel(index, tok, *refs):
        sems = refs[n_arrays]
        copies = []
        for i in range(2 * n_arrays):
            copies.append(
                pltpu.make_async_copy(
                    tok.at[:, pl.ds(pl.multiple_of(index[i], 128), window)],
                    refs[i // 2].at[:, pl.ds(i % 2 * window, window)],
                    sems.at[i],
                )
            )
            copies[-1].start()
        for copy in copies:
            copy.wait()

    depth = tokens.shape[0]
    shape = jax.ShapeDtypeStruct((depth, 2 * window), tokens.dtype)
    anywhere = pl.BlockSpec(memory_space=pl.ANY)
    return pl.pallas_call(
        kernel,
        out_shape=[shape] * n_arrays,
        in_specs=[pl.BlockSpec(memory_space=pltpu.SMEM), anywhere],
        out_specs=[anywhere] * n_arrays,
        scratch_shapes=[pltpu.SemaphoreType.DMA((2 * n_arrays,))],
        compiler_params=pltpu.CompilerParams(vmem_limit_bytes=PACK_MEMORY),
        cost_estimate=SMALL,
    )(index, tokens)


def grad_blocks(index, near, far, cotangent, cot_far, rows, share, window, kind):
    n_share = rows // share
    step = 384

    def kernel(index, near, far, cot, cot_far, out, left, held, sems, out_sems):
        copies = []
        for i in range(2):
            copies.append(
                [
                    pltpu.make_async_copy(
                        source.at[:, pl.ds(i * window, window)], left.at[i, j], sems.at[i, j]
                    )
                    for j, source in enumerate((near, far))
                ]
            )
        for pair in copies:
            for copy in pair:
                copy.start()
        skip = index[0]
        place = index[1]
        done = []
        for i in range(2):
            for copy in copies[i]:
                copy.wait()
            for j in range(window // step):
                cols = pl.ds(j * step, step)
                held[i, cols, :] = (
                    lax.dot_general(
                        left[i, 0, :, cols], cot[...], CONTRACT_ROWS,
                        preferred_element_type=jnp.float32,
                    )
                    + lax.dot_general(
                        left[i, 1, :, cols], cot_far[...], CONTRACT_ROWS,
                        preferred_element_type=jnp.float32,
                    )
                ).astype(kind)
            for k in range(n_share):
                source = pl.multiple_of(skip + lax.rem(place + k, n_share) * share, 16)
                done.append(
                    pltpu.make_async_copy(
                        held.at[i, pl.ds(source, share)],
                        out.at[pl.ds(i * rows + k * share, share)],
                        out_sems.at[i, k],
                    )
                )
                done[-1].start()
        for copy in done:
            copy.wait()

    depth, slab = cotangent.shape
    anywhere = pl.BlockSpec(memory_space=pl.ANY)
    whole = pl.BlockSpec(memory_space=pltpu.VMEM)
    return pl.pallas_call(
        kernel,
        out_shape=jax.ShapeDtypeStruct((2 * rows, slab), kind),
        in_specs=[pl.BlockSpec(memory_space=pltpu.SMEM), anywhere, anywhere, whole, whole],
        out_specs=anywhere,
        scratch_shapes=[
            pltpu.VMEM((2, 2, depth, window), jnp.bfloat16),
            pltpu.VMEM((2, window, slab), kind),
            pltpu.SemaphoreType.DMA((2, 2)),
            pltpu.SemaphoreType.DMA((2, n_share)),
        ],
        compiler_params=pltpu.CompilerParams(vmem_limit_bytes=16 * 2**20),
        cost_estimate=LONG,
    )(index, near, far, cotangent, cot_far)


def output_part(index, nears, fars, pieces, before, part, window):
    steps = len(pieces)
    depth = nears[0].shape[0]
    slab = pieces[0][0].shape[1]
    edge = window - 2 * part

    def kernel(index, near_a, near_b, far_a, far_b, *refs):
        parts = refs[: 2 * steps]
        refs = refs[2 * steps :]
        if before is not None:
            old = refs[:2]
            refs = refs[2:]
        own, other, left, right, sems, piece_sems = refs
        waits = []
        for i in range(steps):
            right[i, 0:edge, :] = jnp.zeros((edge, slab), jnp.bfloat16)
            right[i, window - edge : window, :] = jnp.zeros((edge, slab), jnp.bfloat16)
            slot = index[3 * i]
            column = pl.multiple_of(lax.rem(slot, 2) * window, 128)
            waits.append([])
            for j, pair in enumerate(((near_a, near_b), (far_a, far_b))):
                from_a, from_b = [
                    pltpu.make_async_copy(
                        source.at[:, pl.ds(column, window)],
                        left.at[i, pl.ds(j * depth, depth)],
                        sems.at[i, j],
                    )
                    for source in pair
                ]
                pl.when(slot < 2)(from_a.start)
                pl.when(slot >= 2)(from_b.start)
                waits[-1].append(from_a)
            for j in range(2):
                row = pl.multiple_of(index[3 * i + 1 + j], 16)
                piece = pltpu.make_async_copy(
                    parts[2 * i + j], right.at[i, pl.ds(row, part)], piece_sems.at[i, j]
                )
                piece.start()
                waits[-1].append(piece)
        total = None
        for i in range(steps):
            for copy in waits[i]:
                copy.wait()
            term = jnp.dot(left[i], right[i], preferred_element_type=jnp.float32)
            total = term if total is None else total + term
        if before is None:
            own[...] = total[:depth]
            other[...] = total[depth:]
        else:
            own[...] = total[:depth] + old[0][...]
            other[...] = total[depth:] + old[1][...]

    anywhere = pl.BlockSpec(memory_space=pl.ANY)
    whole = pl.BlockSpec(memory_space=pltpu.VMEM)
    shape = jax.ShapeDtypeStruct((depth, slab), jnp.float32)
    olds = () if before is None else tuple(before)
    return pl.pallas_call(
        kernel,
        out_shape=[shape, shape],
        in_specs=[pl.BlockSpec(memory_space=pltpu.SMEM)]
        + [anywhere] * (4 + 2 * steps)
        + [whole] * len(olds),
        out_specs=[whole, whole],
        scratch_shapes=[
            pltpu.VMEM((steps, 2 * depth, window), jnp.bfloat16),
            pltpu.VMEM((steps, window, slab), jnp.bfloat16),
            pltpu.SemaphoreType.DMA((steps, 2)),
            pltpu.SemaphoreType.DMA((steps, 2)),
        ],
        compiler_params=pltpu.CompilerParams(vmem_limit_bytes=(5 + 4 * steps) * 2**20),
        cost_estimate=SMALL,
    )(index, *nears, *fars, *[p for pair in pieces for p in pair], *olds)


def paired(mesh):
    n_outer = mesh.shape["outer"]
    n_node = mesh.shape["node"]
    orders = [[1, 2], [2, 1]]

    def core_swap(value):
        return lax.ppermute(value, "outer", [(o, o ^ 1) for o in range(n_outer)])

    def outer_swap(value, stage):
        return lax.ppermute(
            value, "outer", [(o, o ^ (1 << orders[o % 2][stage])) for o in range(n_outer)]
        )

    def node_shift(value, step):
        return lax.ppermute(value, "node", [(n, (n + step) % n_node) for n in range(n_node)])

    def on_device(tokens, cotangent, weight_codes, weight_scales, weight_bits, grad_bits):
        o = lax.axis_index("outer")
        n = lax.axis_index("node")
        core = o % 2
        width = tokens.shape[1]
        rows = width // n_outer
        share = rows // n_node
        node_rows = weight_codes.shape[0]
        window = (rows + 127) // 128 * 128
        edge = window - rows

        def block(mask, mine):
            here = core if mine else 1 - core
            base = o if mine else o ^ 1
            return base ^ jnp.where(here == 0, relative_of(orders, 0, mask), relative_of(orders, 1, mask))

        def column(which):
            return which // 2 * node_rows + which % 2 * (node_rows - window)

        part = rows // 2
        side = jnp.where(core == 0, o >> 1, o >> 2) % 2
        start = core * rows + side * part
        held = rotate(
            dequantize(
                lax.dynamic_slice_in_dim(weight_codes, start, part),
                lax.dynamic_slice_in_dim(weight_scales, start, part),
            ),
            weight_bits,
        ).astype(jnp.bfloat16)

        columns = [
            column(block(mask, mine)) for mine in (False, True) for mask in (3, 1, 2, 0)
        ]
        for_a, for_b, near_a, near_b = pack_windows(
            jnp.stack(columns).astype(jnp.int32), tokens, window
        )
        far_a = core_swap(for_a)
        cot_far = core_swap(cotangent)
        far_b = core_swap(for_b)

        held = [held]
        across = [outer_swap(held[0], 0)]
        held.append(node_shift(held[0], 1))

        def grads(near, far, kind):
            index = jnp.stack([core * edge, n])
            return grad_blocks(
                index.astype(jnp.int32), near, far, cotangent, cot_far, rows, share, window, kind
            )

        came = outer_swap(grads(after(near_a, held[0]), far_a, jnp.bfloat16), 0)
        keep = grads(after(near_b, held[1], across[0]), far_b, jnp.float32)
        for step in range(1, n_node - 1):
            held.append(node_shift(held[step], 1))
        came = after(came, *held[:-1])
        send2 = (keep[:rows] + came[:rows].astype(jnp.float32)).astype(jnp.bfloat16)
        came2 = after(outer_swap(send2, 1), held[-1])
        total = keep[rows:] + came[rows:].astype(jnp.float32) + came2.astype(jnp.float32)
        sends = [
            total[step * share : (step + 1) * share].astype(jnp.bfloat16)
            for step in range(1, n_node)
        ]
        grad = total[:share]
        for step in range(1, n_node):
            grad = grad + node_shift(sends[step - 1], step).astype(jnp.float32)
        grad_rotated = rotate(grad, grad_bits)
        joined = outer_swap(after(jnp.concatenate(held[1:3]), *sends), 0)
        across += [joined[:part], joined[part:], outer_swap(after(held[3], *sends), 0)]

        def out_index(steps):
            found = []
            for step in steps:
                node = (n - step) % n_node
                pair = (node ^ (o >> 1)) % 4
                bits = jnp.where(core == 0, pair, (pair >> 1) + 2 * (pair % 2))
                slot = jnp.where(bits == 3, 0, jnp.where(bits == 1, 1, jnp.where(bits == 2, 2, 3)))
                found += [
                    slot,
                    core * edge + side * part,
                    core * edge + (1 - side) * part,
                ]
            return jnp.stack(found).astype(jnp.int32)

        def product(steps, before):
            return output_part(
                out_index(steps),
                (near_a, near_b),
                (far_a, far_b),
                [(held[step], across[step]) for step in steps],
                before,
                part,
                window,
            )

        sums = product((0, 1, 2), None)
        own, other = product((3,), sums)
        output = (own + core_swap(other)).astype(jnp.bfloat16)
        return output, grad_rotated

    return on_device


def general(mesh):
    n_outer = mesh.shape["outer"]
    n_node = mesh.shape["node"]
    n_bits = n_outer.bit_length() - 1
    orders = [list(range(1, n_bits)), [2, 1] + list(range(3, n_bits))]

    def outer_swap(value, stage):
        pairs = []
        for o in range(n_outer):
            pairs.append((o, o ^ (1 if stage is None else 1 << orders[o % 2][stage])))
        return lax.ppermute(value, "outer", pairs)

    def node_shift(value, step):
        return lax.ppermute(value, "node", [(n, (n + step) % n_node) for n in range(n_node)])

    def on_device(tokens, cotangent, weight_codes, weight_scales, weight_bits, grad_bits):
        o = lax.axis_index("outer")
        n = lax.axis_index("node")
        core = o % 2
        width = tokens.shape[1]
        slab = cotangent.shape[1]

        part = weight_codes.shape[0] // 4
        side = jnp.where(core == 0, (o >> orders[0][0]) % 2, (o >> orders[1][0]) % 2)
        mate_side = jnp.where(core == 0, (o >> orders[1][0]) % 2, (o >> orders[0][0]) % 2)
        quarter = core * 2 + side
        start = quarter * part
        held = rotate(
            dequantize(
                lax.dynamic_slice_in_dim(weight_codes, start, part),
                lax.dynamic_slice_in_dim(weight_scales, start, part),
            ),
            weight_bits,
        ).astype(jnp.bfloat16)

        total = lax.dot_general(
            tokens, cotangent, (((0,), (0,)), ((), ())), preferred_element_type=jnp.float32
        ).astype(jnp.bfloat16)
        rows = width // n_outer
        blocks = {}

        def own(d):
            return lax.dynamic_slice_in_dim(total, (o ^ d) * rows, rows)

        def relative(mask):
            found = [0, 0]
            for c in range(2):
                for j, bit in enumerate(orders[c]):
                    if mask >> j & 1:
                        found[c] |= 1 << bit
            return jnp.where(core == 0, found[0], found[1])

        n_rest = n_bits - 1
        sums = {}
        for mask in reversed(range(2**n_rest)):
            partner = jnp.where(core == 0, relative_of(orders, 1, mask), relative_of(orders, 0, mask))
            came = outer_swap(own(partner ^ 1), None)
            sums[mask] = own(relative(mask)).astype(jnp.float32) + came.astype(jnp.float32)
        for stage in range(n_rest):
            low = 1 << stage
            for mask in sorted([m for m in sums if m & low], reverse=True):
                came = outer_swap(sums.pop(mask).astype(jnp.bfloat16), stage)
                sums[mask ^ low] = sums[mask ^ low] + came.astype(jnp.float32)
        mine = sums[0]
        share = rows // n_node
        send = mine.astype(jnp.bfloat16)
        grad = lax.dynamic_slice_in_dim(mine, n * share, share)
        for step in range(1, n_node):
            piece = lax.dynamic_slice_in_dim(send, (n + step) % n_node * share, share)
            grad = grad + node_shift(piece, step).astype(jnp.float32)
        grad_rotated = rotate(grad, grad_bits)

        weight = jnp.zeros((width, slab), jnp.bfloat16)
        node_rows = weight_codes.shape[0]
        for step in range(n_node):
            base = (n - step) % n_node * node_rows
            across = outer_swap(held, 0)
            mate = outer_swap(held, None)
            mate_across = outer_swap(across, None)
            pieces = [
                (held, core * 2 + side),
                (across, core * 2 + 1 - side),
                (mate, (1 - core) * 2 + mate_side),
                (mate_across, (1 - core) * 2 + 1 - mate_side),
            ]
            for value, place in pieces:
                weight = lax.dynamic_update_slice_in_dim(weight, value, base + place * part, 0)
            if step < n_node - 1:
                held = node_shift(held, 1)
        output = jnp.dot(tokens, weight, preferred_element_type=jnp.float32).astype(jnp.bfloat16)
        return output, grad_rotated

    return on_device


def solution(mesh):
    n_outer = mesh.shape["outer"]
    n_node = mesh.shape["node"]
    on_device = paired(mesh) if n_outer == 8 and n_node == 4 else general(mesh)
    return jax.shard_map(
        on_device,
        mesh=mesh,
        in_specs=(
            P(("outer", "node"), None),
            P(("outer", "node"), None),
            P("node", None),
            P("node", None),
            P(),
            P(),
        ),
        out_specs=(P(("outer", "node"), None), P(("outer", "node"), None)),
        check_vma=False,
    )
```

```python
import math

import jax
import jax.numpy as jnp
import numpy as np
from jax import lax
from jax.experimental import pallas as pl
from jax.experimental.pallas import tpu as pltpu
from jax.sharding import PartitionSpec as P


def sylvester():
    row_index = np.arange(128).reshape(128, 1)
    column_index = np.arange(128).reshape(1, 128)
    parity = np.zeros((128, 128))
    for level in range(7):
        parity = parity + row_index // 2**level % 2 * (column_index // 2**level % 2)
    return 1.0 - 2.0 * (parity % 2)


def rotate(values, bits):
    width = values.shape[1]
    signs = (2 * bits - 1).astype(jnp.float32)
    table = np.kron(np.eye(width // 128), sylvester()) / math.sqrt(128.0)
    return jnp.dot(
        values * signs,
        jnp.asarray(table, jnp.float32),
        precision=lax.Precision.HIGHEST,
    )


def dequantize(codes, scales):
    height, width = codes.shape
    spread = jnp.concatenate(
        [
            jnp.broadcast_to(scales[:, block : block + 1], (height, 128))
            for block in range(width // 128)
        ],
        axis=1,
    )
    return codes.astype(jnp.float32) * spread


def relative_of(orders, core, mask):
    found = 0
    for j, bit in enumerate(orders[core]):
        if mask >> j & 1:
            found |= 1 << bit
    return found


SMALL = pl.CostEstimate(flops=0, bytes_accessed=1024, transcendentals=0)
LONG = pl.CostEstimate(flops=5 * 10**9, bytes_accessed=1024, transcendentals=0)
LONGER = pl.CostEstimate(flops=6 * 10**10, bytes_accessed=1024, transcendentals=0)
CONTRACT_ROWS = (((0,), (0,)), ((), ()))


def after(value, *deps):
    return lax.optimization_barrier((value, *deps))[0]


def pack_windows(index, tokens, window):
    n_arrays = 4

    def kernel(index, tok, *refs):
        held, sems, out_sems = refs[n_arrays:]
        copies = []
        for i in range(2 * n_arrays):
            copies.append(
                pltpu.make_async_copy(
                    tok.at[:, pl.ds(pl.multiple_of(index[i], 128), window)],
                    held.at[i],
                    sems.at[i],
                )
            )
            copies[-1].start()
        done = []
        for i in range(2 * n_arrays):
            copies[i].wait()
            done.append(
                pltpu.make_async_copy(
                    held.at[i], refs[i // 2].at[:, pl.ds(i % 2 * window, window)], out_sems.at[i]
                )
            )
            done[-1].start()
        for copy in done:
            copy.wait()

    depth = tokens.shape[0]
    shape = jax.ShapeDtypeStruct((depth, 2 * window), tokens.dtype)
    anywhere = pl.BlockSpec(memory_space=pl.ANY)
    return pl.pallas_call(
        kernel,
        out_shape=[shape] * n_arrays,
        in_specs=[pl.BlockSpec(memory_space=pltpu.SMEM), anywhere],
        out_specs=[anywhere] * n_arrays,
        scratch_shapes=[
            pltpu.VMEM((2 * n_arrays, depth, window), tokens.dtype),
            pltpu.SemaphoreType.DMA((2 * n_arrays,)),
            pltpu.SemaphoreType.DMA((2 * n_arrays,)),
        ],
        compiler_params=pltpu.CompilerParams(vmem_limit_bytes=10 * 2**20),
        cost_estimate=SMALL,
    )(index, tokens)


def grad_blocks(index, near, far, cotangent, cot_far, rows, share, window, kind):
    n_share = rows // share
    step = 384

    def kernel(index, near, far, cot, cot_far, out, left, held, sems, out_sems):
        copies = []
        for i in range(2):
            copies.append(
                [
                    pltpu.make_async_copy(
                        source.at[:, pl.ds(i * window, window)], left.at[i, j], sems.at[i, j]
                    )
                    for j, source in enumerate((near, far))
                ]
            )
        for pair in copies:
            for copy in pair:
                copy.start()
        skip = index[0]
        place = index[1]
        done = []
        for i in range(2):
            for copy in copies[i]:
                copy.wait()
            for j in range(window // step):
                cols = pl.ds(j * step, step)
                held[i, cols, :] = (
                    lax.dot_general(
                        left[i, 0, :, cols], cot[...], CONTRACT_ROWS,
                        preferred_element_type=jnp.float32,
                    )
                    + lax.dot_general(
                        left[i, 1, :, cols], cot_far[...], CONTRACT_ROWS,
                        preferred_element_type=jnp.float32,
                    )
                ).astype(kind)
            for k in range(n_share):
                source = pl.multiple_of(skip + lax.rem(place + k, n_share) * share, 16)
                done.append(
                    pltpu.make_async_copy(
                        held.at[i, pl.ds(source, share)],
                        out.at[pl.ds(i * rows + k * share, share)],
                        out_sems.at[i, k],
                    )
                )
                done[-1].start()
        for copy in done:
            copy.wait()

    depth, slab = cotangent.shape
    anywhere = pl.BlockSpec(memory_space=pl.ANY)
    whole = pl.BlockSpec(memory_space=pltpu.VMEM)
    return pl.pallas_call(
        kernel,
        out_shape=jax.ShapeDtypeStruct((2 * rows, slab), kind),
        in_specs=[pl.BlockSpec(memory_space=pltpu.SMEM), anywhere, anywhere, whole, whole],
        out_specs=anywhere,
        scratch_shapes=[
            pltpu.VMEM((2, 2, depth, window), jnp.bfloat16),
            pltpu.VMEM((2, window, slab), kind),
            pltpu.SemaphoreType.DMA((2, 2)),
            pltpu.SemaphoreType.DMA((2, n_share)),
        ],
        compiler_params=pltpu.CompilerParams(vmem_limit_bytes=16 * 2**20),
        cost_estimate=LONG if kind == jnp.bfloat16 else LONGER,
    )(index, near, far, cotangent, cot_far)


def output_part(index, nears, fars, pieces, before, part, window):
    steps = len(pieces)
    depth = nears[0].shape[0]
    slab = pieces[0][0][0].shape[1]
    edge = window - 2 * part

    def kernel(index, near_a, near_b, far_a, far_b, *refs):
        parts = refs[: 2 * steps]
        refs = refs[2 * steps :]
        if before is not None:
            old = refs[:2]
            refs = refs[2:]
        own, other, left, right, sems, piece_sems = refs
        waits = []
        for i in range(steps):
            right[i, 0:edge, :] = jnp.zeros((edge, slab), jnp.bfloat16)
            right[i, window - edge : window, :] = jnp.zeros((edge, slab), jnp.bfloat16)
            slot = index[3 * i]
            column = pl.multiple_of(lax.rem(slot, 2) * window, 128)
            waits.append([])
            for j, pair in enumerate(((near_a, near_b), (far_a, far_b))):
                from_a, from_b = [
                    pltpu.make_async_copy(
                        source.at[:, pl.ds(column, window)],
                        left.at[i, pl.ds(j * depth, depth)],
                        sems.at[i, j],
                    )
                    for source in pair
                ]
                pl.when(slot < 2)(from_a.start)
                pl.when(slot >= 2)(from_b.start)
                waits[-1].append(from_a)
            for j in range(2):
                row = pl.multiple_of(index[3 * i + 1 + j], 16)
                first = pieces[i][j][1]
                piece = pltpu.make_async_copy(
                    parts[2 * i + j].at[pl.ds(first, part)], right.at[i, pl.ds(row, part)], piece_sems.at[i, j]
                )
                piece.start()
                waits[-1].append(piece)
        total = None
        for i in range(steps):
            for copy in waits[i]:
                copy.wait()
            term = jnp.dot(left[i], right[i], preferred_element_type=jnp.float32)
            total = term if total is None else total + term
        if before is None:
            own[...] = total[:depth]
            other[...] = total[depth:]
        else:
            own[...] = total[:depth] + old[0][...]
            other[...] = total[depth:] + old[1][...]

    anywhere = pl.BlockSpec(memory_space=pl.ANY)
    whole = pl.BlockSpec(memory_space=pltpu.VMEM)
    shape = jax.ShapeDtypeStruct((depth, slab), jnp.float32)
    olds = () if before is None else tuple(before)
    return pl.pallas_call(
        kernel,
        out_shape=[shape, shape],
        in_specs=[pl.BlockSpec(memory_space=pltpu.SMEM)]
        + [anywhere] * (4 + 2 * steps)
        + [whole] * len(olds),
        out_specs=[whole, whole],
        scratch_shapes=[
            pltpu.VMEM((steps, 2 * depth, window), jnp.bfloat16),
            pltpu.VMEM((steps, window, slab), jnp.bfloat16),
            pltpu.SemaphoreType.DMA((steps, 2)),
            pltpu.SemaphoreType.DMA((steps, 2)),
        ],
        compiler_params=pltpu.CompilerParams(vmem_limit_bytes=(5 + 4 * steps) * 2**20),
        cost_estimate=SMALL,
    )(index, *nears, *fars, *[p for pair in pieces for p, _ in pair], *olds)


def paired(mesh):
    n_outer = mesh.shape["outer"]
    n_node = mesh.shape["node"]
    orders = [[1, 2], [2, 1]]

    def core_swap(value):
        return lax.ppermute(value, "outer", [(o, o ^ 1) for o in range(n_outer)])

    def outer_swap(value, stage):
        return lax.ppermute(
            value, "outer", [(o, o ^ (1 << orders[o % 2][stage])) for o in range(n_outer)]
        )

    def node_shift(value, step):
        return lax.ppermute(value, "node", [(n, (n + step) % n_node) for n in range(n_node)])

    def on_device(tokens, cotangent, weight_codes, weight_scales, weight_bits, grad_bits):
        o = lax.axis_index("outer")
        n = lax.axis_index("node")
        core = o % 2
        width = tokens.shape[1]
        rows = width // n_outer
        share = rows // n_node
        node_rows = weight_codes.shape[0]
        window = (rows + 127) // 128 * 128
        edge = window - rows

        def block(mask, mine):
            here = core if mine else 1 - core
            base = o if mine else o ^ 1
            return base ^ jnp.where(here == 0, relative_of(orders, 0, mask), relative_of(orders, 1, mask))

        def column(which):
            return which // 2 * node_rows + which % 2 * (node_rows - window)

        part = rows // 2
        side = jnp.where(core == 0, o >> 1, o >> 2) % 2
        start = core * rows + side * part
        held = rotate(
            dequantize(
                lax.dynamic_slice_in_dim(weight_codes, start, part),
                lax.dynamic_slice_in_dim(weight_scales, start, part),
            ),
            weight_bits,
        ).astype(jnp.bfloat16)

        columns = [
            column(block(mask, mine)) for mine in (False, True) for mask in (3, 1, 2, 0)
        ]
        for_a, for_b, near_a, near_b = pack_windows(
            jnp.stack(columns).astype(jnp.int32), after(tokens, held), window
        )
        far_a = core_swap(for_a)
        cot_far = core_swap(cotangent)
        far_b = core_swap(for_b)

        held = [held]
        across = [outer_swap(held[0], 0)]
        held.append(node_shift(held[0], 1))

        def grads(near, far, kind):
            index = jnp.stack([core * edge, n])
            return grad_blocks(
                index.astype(jnp.int32), near, far, cotangent, cot_far, rows, share, window, kind
            )

        def out_index(steps):
            found = []
            for step in steps:
                node = (n - step) % n_node
                pair = (node ^ (o >> 1)) % 4
                bits = jnp.where(core == 0, pair, (pair >> 1) + 2 * (pair % 2))
                slot = jnp.where(bits == 3, 0, jnp.where(bits == 1, 1, jnp.where(bits == 2, 2, 3)))
                found += [
                    slot,
                    core * edge + side * part,
                    core * edge + (1 - side) * part,
                ]
            return jnp.stack(found).astype(jnp.int32)

        def product(steps, before):
            return output_part(
                out_index(steps),
                (near_a, near_b),
                (far_a, far_b),
                [((held[step], 0), swapped[step]) for step in steps],
                before,
                part,
                window,
            )

        swapped = [(across[0], 0)]
        leaving = grads(near_a, far_a, jnp.bfloat16)
        came = outer_swap(leaving, 0)
        held[1] = after(held[1], leaving)
        keep = grads(after(near_b, held[1]), far_b, jnp.float32)
        for step in range(1, n_node - 1):
            held.append(node_shift(held[step], 1))
        came, early = lax.optimization_barrier((came, product((0,), None), *held[1:-1]))[:2]
        send2 = (keep[:rows] + came[:rows].astype(jnp.float32)).astype(jnp.bfloat16)
        came2 = after(outer_swap(send2, 1), held[-1])
        total = keep[rows:] + came[rows:].astype(jnp.float32) + came2.astype(jnp.float32)
        sends = [
            total[step * share : (step + 1) * share].astype(jnp.bfloat16)
            for step in range(1, n_node)
        ]
        grad = total[:share]
        for step in range(1, n_node):
            grad = grad + node_shift(sends[step - 1], step).astype(jnp.float32)
        grad_rotated = rotate(grad, grad_bits)
        joined = outer_swap(after(jnp.concatenate(held[1:3]), *sends), 0)
        last = outer_swap(after(held[3], *sends), 0)
        swapped += [(joined, 0), (joined, part), (last, 0)]

        sums = product((1, 2), early)
        own, other = product((3,), sums)
        output = (own + core_swap(other)).astype(jnp.bfloat16)
        return output, grad_rotated

    return on_device


def general(mesh):
    n_outer = mesh.shape["outer"]
    n_node = mesh.shape["node"]
    n_bits = n_outer.bit_length() - 1
    orders = [list(range(1, n_bits)), [2, 1] + list(range(3, n_bits))]

    def outer_swap(value, stage):
        pairs = []
        for o in range(n_outer):
            pairs.append((o, o ^ (1 if stage is None else 1 << orders[o % 2][stage])))
        return lax.ppermute(value, "outer", pairs)

    def node_shift(value, step):
        return lax.ppermute(value, "node", [(n, (n + step) % n_node) for n in range(n_node)])

    def on_device(tokens, cotangent, weight_codes, weight_scales, weight_bits, grad_bits):
        o = lax.axis_index("outer")
        n = lax.axis_index("node")
        core = o % 2
        width = tokens.shape[1]
        slab = cotangent.shape[1]

        part = weight_codes.shape[0] // 4
        side = jnp.where(core == 0, (o >> orders[0][0]) % 2, (o >> orders[1][0]) % 2)
        mate_side = jnp.where(core == 0, (o >> orders[1][0]) % 2, (o >> orders[0][0]) % 2)
        quarter = core * 2 + side
        start = quarter * part
        held = rotate(
            dequantize(
                lax.dynamic_slice_in_dim(weight_codes, start, part),
                lax.dynamic_slice_in_dim(weight_scales, start, part),
            ),
            weight_bits,
        ).astype(jnp.bfloat16)

        total = lax.dot_general(
            tokens, cotangent, (((0,), (0,)), ((), ())), preferred_element_type=jnp.float32
        ).astype(jnp.bfloat16)
        rows = width // n_outer
        blocks = {}

        def own(d):
            return lax.dynamic_slice_in_dim(total, (o ^ d) * rows, rows)

        def relative(mask):
            found = [0, 0]
            for c in range(2):
                for j, bit in enumerate(orders[c]):
                    if mask >> j & 1:
                        found[c] |= 1 << bit
            return jnp.where(core == 0, found[0], found[1])

        n_rest = n_bits - 1
        sums = {}
        for mask in reversed(range(2**n_rest)):
            partner = jnp.where(core == 0, relative_of(orders, 1, mask), relative_of(orders, 0, mask))
            came = outer_swap(own(partner ^ 1), None)
            sums[mask] = own(relative(mask)).astype(jnp.float32) + came.astype(jnp.float32)
        for stage in range(n_rest):
            low = 1 << stage
            for mask in sorted([m for m in sums if m & low], reverse=True):
                came = outer_swap(sums.pop(mask).astype(jnp.bfloat16), stage)
                sums[mask ^ low] = sums[mask ^ low] + came.astype(jnp.float32)
        mine = sums[0]
        share = rows // n_node
        send = mine.astype(jnp.bfloat16)
        grad = lax.dynamic_slice_in_dim(mine, n * share, share)
        for step in range(1, n_node):
            piece = lax.dynamic_slice_in_dim(send, (n + step) % n_node * share, share)
            grad = grad + node_shift(piece, step).astype(jnp.float32)
        grad_rotated = rotate(grad, grad_bits)

        weight = jnp.zeros((width, slab), jnp.bfloat16)
        node_rows = weight_codes.shape[0]
        for step in range(n_node):
            base = (n - step) % n_node * node_rows
            across = outer_swap(held, 0)
            mate = outer_swap(held, None)
            mate_across = outer_swap(across, None)
            pieces = [
                (held, core * 2 + side),
                (across, core * 2 + 1 - side),
                (mate, (1 - core) * 2 + mate_side),
                (mate_across, (1 - core) * 2 + 1 - mate_side),
            ]
            for value, place in pieces:
                weight = lax.dynamic_update_slice_in_dim(weight, value, base + place * part, 0)
            if step < n_node - 1:
                held = node_shift(held, 1)
        output = jnp.dot(tokens, weight, preferred_element_type=jnp.float32).astype(jnp.bfloat16)
        return output, grad_rotated

    return on_device


def solution(mesh):
    n_outer = mesh.shape["outer"]
    n_node = mesh.shape["node"]
    on_device = paired(mesh) if n_outer == 8 and n_node == 4 else general(mesh)
    return jax.shard_map(
        on_device,
        mesh=mesh,
        in_specs=(
            P(("outer", "node"), None),
            P(("outer", "node"), None),
            P("node", None),
            P("node", None),
            P(),
            P(),
        ),
        out_specs=(P(("outer", "node"), None), P(("outer", "node"), None)),
        check_vma=False,
    )
```

```python
import math

import jax
import jax.numpy as jnp
import numpy as np
from jax import lax
from jax.experimental import pallas as pl
from jax.experimental.pallas import tpu as pltpu
from jax.sharding import PartitionSpec as P


def sylvester():
    row_index = np.arange(128).reshape(128, 1)
    column_index = np.arange(128).reshape(1, 128)
    parity = np.zeros((128, 128))
    for level in range(7):
        parity = parity + row_index // 2**level % 2 * (column_index // 2**level % 2)
    return 1.0 - 2.0 * (parity % 2)


def rotate(values, bits):
    width = values.shape[1]
    signs = (2 * bits - 1).astype(jnp.float32)
    table = np.kron(np.eye(width // 128), sylvester()) / math.sqrt(128.0)
    return jnp.dot(
        values * signs,
        jnp.asarray(table, jnp.float32),
        precision=lax.Precision.HIGHEST,
    )


def dequantize(codes, scales):
    height, width = codes.shape
    spread = jnp.concatenate(
        [
            jnp.broadcast_to(scales[:, block : block + 1], (height, 128))
            for block in range(width // 128)
        ],
        axis=1,
    )
    return codes.astype(jnp.float32) * spread


def relative_of(orders, core, mask):
    found = 0
    for j, bit in enumerate(orders[core]):
        if mask >> j & 1:
            found |= 1 << bit
    return found


SMALL = pl.CostEstimate(flops=0, bytes_accessed=1024, transcendentals=0)
LONG = pl.CostEstimate(flops=5 * 10**9, bytes_accessed=1024, transcendentals=0)
LONGER = pl.CostEstimate(flops=6 * 10**10, bytes_accessed=1024, transcendentals=0)
MIB = 2**20


def after(value, *deps):
    return lax.optimization_barrier((value, *deps))[0]


def tile_of(window):
    return max(128 * k for k in range(1, 6) if window % (128 * k) == 0)


def grad_blocks(nears, fars, cot, cot_far, kind, cost):
    count = len(nears)
    slab, depth = cot.shape
    window = nears[0][0].shape[1]
    tile = tile_of(window)

    def kernel(cot, cot_far, *refs):
        out = refs[-1]
        for i in range(count):
            out[i * slab : (i + 1) * slab, :] = (
                jnp.dot(cot[...], refs[i][...], preferred_element_type=jnp.float32)
                + jnp.dot(cot_far[...], refs[count + i][...], preferred_element_type=jnp.float32)
            ).astype(kind)

    fixed = pl.BlockSpec((slab, depth), lambda j: (0, 0))

    def block(place):
        return pl.BlockSpec((depth, tile), lambda j: (place, j))

    return pl.pallas_call(
        kernel,
        grid=(window // tile,),
        out_shape=jax.ShapeDtypeStruct((count * slab, window), kind),
        in_specs=[fixed, fixed] + [block(place) for _, place in nears + fars],
        out_specs=pl.BlockSpec((count * slab, tile), lambda j: (0, j)),
        compiler_params=pltpu.CompilerParams(vmem_limit_bytes=10 * MIB),
        cost_estimate=cost,
    )(cot, cot_far, *[array for array, _ in nears + fars])


def cut_shares(index, keep, came, came2, rows, share):
    slab, window = came2.shape
    tile = tile_of(window)
    n_share = rows // share
    last = window // tile - 1

    def kernel(index, keep, came, came2, own, *refs):
        sends, total = refs[:-1], refs[-1]
        j = pl.program_id(0)
        block = (
            keep[...] + came[...].astype(jnp.float32) + came2[...].astype(jnp.float32)
        )
        total[pl.ds(pl.multiple_of(j * tile, tile), tile), :] = block.T

        @pl.when(j == last)
        def _():
            for k in range(n_share):
                first = index[0] + lax.rem(index[1] + k, n_share) * share
                value = total[pl.ds(pl.multiple_of(first, 16), share), :]
                if k == 0:
                    own[...] = value
                else:
                    sends[k - 1][...] = value.astype(jnp.bfloat16)

    whole = pl.BlockSpec((share, slab), lambda j: (0, 0))
    return pl.pallas_call(
        kernel,
        grid=(window // tile,),
        out_shape=[jax.ShapeDtypeStruct((share, slab), jnp.float32)]
        + [jax.ShapeDtypeStruct((share, slab), jnp.bfloat16)] * (n_share - 1),
        in_specs=[
            pl.BlockSpec(memory_space=pltpu.SMEM),
            pl.BlockSpec((slab, tile), lambda j: (1, j)),
            pl.BlockSpec((slab, tile), lambda j: (1, j)),
            pl.BlockSpec((slab, tile), lambda j: (0, j)),
        ],
        out_specs=[whole] * n_share,
        scratch_shapes=[pltpu.VMEM((window, slab), jnp.float32)],
        compiler_params=pltpu.CompilerParams(vmem_limit_bytes=12 * MIB),
        cost_estimate=SMALL,
    )(index, keep, came, came2)


def finish_grad(own, came, signs):
    share, slab = own.shape

    def kernel(own, *refs):
        signs, table, out = refs[-3:]
        total = own[...]
        for ref in refs[:-3]:
            total = total + ref[...].astype(jnp.float32)
        total = total * signs[...]
        result = None
        for _ in range(3):
            part = total.astype(jnp.bfloat16)
            total = total - part.astype(jnp.float32)
            term = jnp.dot(part, table[...], preferred_element_type=jnp.float32)
            result = term if result is None else result + term
        out[...] = result * (1.0 / math.sqrt(128.0))

    table = np.kron(np.eye(slab // 128), sylvester())
    whole = pl.BlockSpec(memory_space=pltpu.VMEM)
    return pl.pallas_call(
        kernel,
        out_shape=jax.ShapeDtypeStruct((share, slab), jnp.float32),
        in_specs=[whole] * (3 + len(came)),
        out_specs=whole,
        compiler_params=pltpu.CompilerParams(vmem_limit_bytes=8 * MIB),
        cost_estimate=LONG,
    )(own, *came, signs, jnp.asarray(table, jnp.bfloat16))


def output_part(index, nears, fars, pieces, before, part):
    steps = len(pieces)
    depth, window = nears[0][0].shape
    slab = pieces[0][0][0].shape[1]
    edge = window - 2 * part
    places = len(nears)

    def kernel(index, *refs):
        windows = refs[: 2 * places]
        parts = refs[2 * places : 2 * places + 2 * steps]
        refs = refs[2 * places + 2 * steps :]
        if before is not None:
            old = refs[:2]
            refs = refs[2:]
        own, other, left, right, sems, piece_sems = refs
        waits = []
        for i in range(steps):
            right[i, 0:edge, :] = jnp.zeros((edge, slab), jnp.bfloat16)
            right[i, window - edge : window, :] = jnp.zeros((edge, slab), jnp.bfloat16)
            waits.append([])
            for j in range(2):
                copies = [
                    pltpu.make_async_copy(
                        windows[j * places + place].at[
                            pl.ds((nears, fars)[j][place][1] * depth, depth)
                        ],
                        left.at[i, pl.ds(j * depth, depth)],
                        sems.at[i, j],
                    )
                    for place in range(places)
                ]
                for place in range(places):
                    pl.when(index[3 * i] == place)(copies[place].start)
                waits[-1].append(copies[0])
            for j in range(2):
                row = pl.multiple_of(index[3 * i + 1 + j], 16)
                first = pieces[i][j][1]
                piece = pltpu.make_async_copy(
                    parts[2 * i + j].at[pl.ds(first, part)],
                    right.at[i, pl.ds(row, part)],
                    piece_sems.at[i, j],
                )
                piece.start()
                waits[-1].append(piece)
        total = None
        for i in range(steps):
            for copy in waits[i]:
                copy.wait()
            term = jnp.dot(left[i], right[i], preferred_element_type=jnp.float32)
            total = term if total is None else total + term
        if before is None:
            own[...] = total[:depth]
            other[...] = total[depth:]
        else:
            own[...] = total[:depth] + old[0][...]
            other[...] = total[depth:] + old[1][...]

    anywhere = pl.BlockSpec(memory_space=pl.ANY)
    whole = pl.BlockSpec(memory_space=pltpu.VMEM)
    shape = jax.ShapeDtypeStruct((depth, slab), jnp.float32)
    olds = () if before is None else tuple(before)
    return pl.pallas_call(
        kernel,
        out_shape=[shape, shape],
        in_specs=[pl.BlockSpec(memory_space=pltpu.SMEM)]
        + [anywhere] * (2 * places + 2 * steps)
        + [whole] * len(olds),
        out_specs=[whole, whole],
        scratch_shapes=[
            pltpu.VMEM((steps, 2 * depth, window), jnp.bfloat16),
            pltpu.VMEM((steps, window, slab), jnp.bfloat16),
            pltpu.SemaphoreType.DMA((steps, 2)),
            pltpu.SemaphoreType.DMA((steps, 2)),
        ],
        compiler_params=pltpu.CompilerParams(vmem_limit_bytes=(5 + 4 * steps) * MIB),
        cost_estimate=SMALL,
    )(index, *[array for array, _ in nears + fars], *[p for pair in pieces for p, _ in pair], *olds)


def paired(mesh):
    n_outer = mesh.shape["outer"]
    n_node = mesh.shape["node"]
    orders = [[1, 2], [2, 1]]

    def core_swap(value):
        return lax.ppermute(value, "outer", [(o, o ^ 1) for o in range(n_outer)])

    def outer_swap(value, stage):
        return lax.ppermute(
            value, "outer", [(o, o ^ (1 << orders[o % 2][stage])) for o in range(n_outer)]
        )

    def node_shift(value, step):
        return lax.ppermute(value, "node", [(n, (n + step) % n_node) for n in range(n_node)])

    def on_device(tokens, cotangent, weight_codes, weight_scales, weight_bits, grad_bits):
        o = lax.axis_index("outer")
        n = lax.axis_index("node")
        core = o % 2
        width = tokens.shape[1]
        rows = width // n_outer
        share = rows // n_node
        node_rows = weight_codes.shape[0]
        window = (rows + 127) // 128 * 128
        edge = window - rows
        masks = (3, 1, 2, 0)

        def take(mask, mine):
            here = core if mine else 1 - core
            base = o if mine else o ^ 1
            which = base ^ jnp.where(
                here == 0, relative_of(orders, 0, mask), relative_of(orders, 1, mask)
            )
            start = which // 2 * node_rows + which % 2 * (node_rows - window)
            return lax.dynamic_slice_in_dim(tokens, start, window, 1)

        leave = [take(mask, False) for mask in masks[:2]]
        fars = [(core_swap(value), 0) for value in leave]
        cot = cotangent.T
        cot_far = core_swap(cot)

        part = rows // 2
        side = jnp.where(core == 0, o >> 1, o >> 2) % 2
        start = core * rows + side * part
        held = rotate(
            dequantize(
                lax.dynamic_slice_in_dim(after(weight_codes, *leave), start, part),
                lax.dynamic_slice_in_dim(weight_scales, start, part),
            ),
            weight_bits,
        ).astype(jnp.bfloat16)
        held = [held, node_shift(held, 1), None, node_shift(held, n_node - 1)]
        first_across = outer_swap(held[0], 0)
        nears = [(take(mask, True), 0) for mask in masks]
        pair = core_swap(jnp.concatenate([take(mask, False) for mask in masks[2:]]))
        fars += [(pair, 0), (pair, 1)]

        def out_index(steps):
            found = []
            for step in steps:
                node = (n - step) % n_node
                pair = (node ^ (o >> 1)) % 4
                bits = jnp.where(core == 0, pair, (pair >> 1) + 2 * (pair % 2))
                place = jnp.where(bits == 3, 0, jnp.where(bits == 1, 1, jnp.where(bits == 2, 2, 3)))
                found += [
                    place,
                    core * edge + side * part,
                    core * edge + (1 - side) * part,
                ]
            return jnp.stack(found).astype(jnp.int32)

        def product(steps, before):
            return output_part(
                out_index(steps),
                nears,
                fars,
                [((held[step], 0), across[step]) for step in steps],
                before,
                part,
            )

        leaving = grad_blocks(nears[:2], fars[:2], cot, cot_far, jnp.bfloat16, LONGER)
        came = outer_swap(leaving, 0)
        held[1], held[3], first_across, _ = lax.optimization_barrier(
            (held[1], held[3], first_across, leaving)
        )
        keep = grad_blocks(
            [(after(nears[2][0], held[1], held[3], first_across), 0), nears[3]],
            fars[2:], cot, cot_far, jnp.float32, LONGER,
        )
        held[2] = node_shift(held[1], 1)
        across = [(first_across, 0)]
        half = slab_of(keep)
        send2 = (keep[:half] + came[:half].astype(jnp.float32)).astype(jnp.bfloat16)
        came2 = outer_swap(send2, 1)
        held[0] = after(held[0], send2)
        early = product((0,), None)
        came2, *early = lax.optimization_barrier((came2, *early))
        held[1], held[2], held[3] = lax.optimization_barrier((*held[1:], came2))[:3]
        index = jnp.stack([core * edge, n]).astype(jnp.int32)
        own, *sends = cut_shares(index, keep, came, came2, rows, share)
        arrived = [node_shift(sends[step - 1], step) for step in range(1, n_node)]
        signs = (2 * grad_bits - 1).astype(jnp.float32).reshape(1, -1)
        grad_rotated = finish_grad(own, arrived, signs)

        joined = outer_swap(after(jnp.concatenate([held[1], held[3]]), *sends), 0)
        last = outer_swap(after(held[2], *sends), 0)
        across += [(joined, 0), (last, 0), (joined, part)]
        sums = product((1, 3), early)
        own_part, other_part = product((2,), sums)
        output = (own_part + core_swap(other_part)).astype(jnp.bfloat16)
        return output, grad_rotated

    return on_device


def slab_of(stacked):
    return stacked.shape[0] // 2


def general(mesh):
    n_outer = mesh.shape["outer"]
    n_node = mesh.shape["node"]
    n_bits = n_outer.bit_length() - 1
    orders = [list(range(1, n_bits)), [2, 1] + list(range(3, n_bits))]

    def outer_swap(value, stage):
        pairs = []
        for o in range(n_outer):
            pairs.append((o, o ^ (1 if stage is None else 1 << orders[o % 2][stage])))
        return lax.ppermute(value, "outer", pairs)

    def node_shift(value, step):
        return lax.ppermute(value, "node", [(n, (n + step) % n_node) for n in range(n_node)])

    def on_device(tokens, cotangent, weight_codes, weight_scales, weight_bits, grad_bits):
        o = lax.axis_index("outer")
        n = lax.axis_index("node")
        core = o % 2
        width = tokens.shape[1]
        slab = cotangent.shape[1]

        part = weight_codes.shape[0] // 4
        side = jnp.where(core == 0, (o >> orders[0][0]) % 2, (o >> orders[1][0]) % 2)
        mate_side = jnp.where(core == 0, (o >> orders[1][0]) % 2, (o >> orders[0][0]) % 2)
        quarter = core * 2 + side
        start = quarter * part
        held = rotate(
            dequantize(
                lax.dynamic_slice_in_dim(weight_codes, start, part),
                lax.dynamic_slice_in_dim(weight_scales, start, part),
            ),
            weight_bits,
        ).astype(jnp.bfloat16)

        total = lax.dot_general(
            tokens, cotangent, (((0,), (0,)), ((), ())), preferred_element_type=jnp.float32
        ).astype(jnp.bfloat16)
        rows = width // n_outer
        blocks = {}

        def own(d):
            return lax.dynamic_slice_in_dim(total, (o ^ d) * rows, rows)

        def relative(mask):
            found = [0, 0]
            for c in range(2):
                for j, bit in enumerate(orders[c]):
                    if mask >> j & 1:
                        found[c] |= 1 << bit
            return jnp.where(core == 0, found[0], found[1])

        n_rest = n_bits - 1
        sums = {}
        for mask in reversed(range(2**n_rest)):
            partner = jnp.where(core == 0, relative_of(orders, 1, mask), relative_of(orders, 0, mask))
            came = outer_swap(own(partner ^ 1), None)
            sums[mask] = own(relative(mask)).astype(jnp.float32) + came.astype(jnp.float32)
        for stage in range(n_rest):
            low = 1 << stage
            for mask in sorted([m for m in sums if m & low], reverse=True):
                came = outer_swap(sums.pop(mask).astype(jnp.bfloat16), stage)
                sums[mask ^ low] = sums[mask ^ low] + came.astype(jnp.float32)
        mine = sums[0]
        share = rows // n_node
        send = mine.astype(jnp.bfloat16)
        grad = lax.dynamic_slice_in_dim(mine, n * share, share)
        for step in range(1, n_node):
            piece = lax.dynamic_slice_in_dim(send, (n + step) % n_node * share, share)
            grad = grad + node_shift(piece, step).astype(jnp.float32)
        grad_rotated = rotate(grad, grad_bits)

        weight = jnp.zeros((width, slab), jnp.bfloat16)
        node_rows = weight_codes.shape[0]
        for step in range(n_node):
            base = (n - step) % n_node * node_rows
            across = outer_swap(held, 0)
            mate = outer_swap(held, None)
            mate_across = outer_swap(across, None)
            pieces = [
                (held, core * 2 + side),
                (across, core * 2 + 1 - side),
                (mate, (1 - core) * 2 + mate_side),
                (mate_across, (1 - core) * 2 + 1 - mate_side),
            ]
            for value, place in pieces:
                weight = lax.dynamic_update_slice_in_dim(weight, value, base + place * part, 0)
            if step < n_node - 1:
                held = node_shift(held, 1)
        output = jnp.dot(tokens, weight, preferred_element_type=jnp.float32).astype(jnp.bfloat16)
        return output, grad_rotated

    return on_device


def solution(mesh):
    n_outer = mesh.shape["outer"]
    n_node = mesh.shape["node"]
    on_device = paired(mesh) if n_outer == 8 and n_node == 4 else general(mesh)
    return jax.shard_map(
        on_device,
        mesh=mesh,
        in_specs=(
            P(("outer", "node"), None),
            P(("outer", "node"), None),
            P("node", None),
            P("node", None),
            P(),
            P(),
        ),
        out_specs=(P(("outer", "node"), None), P(("outer", "node"), None)),
        check_vma=False,
    )
```

```python
import math

import jax
import jax.numpy as jnp
import numpy as np
from jax import lax
from jax.experimental import pallas as pl
from jax.experimental.pallas import tpu as pltpu
from jax.sharding import PartitionSpec as P


def sylvester():
    row_index = np.arange(128).reshape(128, 1)
    column_index = np.arange(128).reshape(1, 128)
    parity = np.zeros((128, 128))
    for level in range(7):
        parity = parity + row_index // 2**level % 2 * (column_index // 2**level % 2)
    return 1.0 - 2.0 * (parity % 2)


def rotate(values, bits):
    width = values.shape[1]
    signs = (2 * bits - 1).astype(jnp.float32)
    table = np.kron(np.eye(width // 128), sylvester()) / math.sqrt(128.0)
    return jnp.dot(
        values * signs,
        jnp.asarray(table, jnp.float32),
        precision=lax.Precision.HIGHEST,
    )


def dequantize(codes, scales):
    height, width = codes.shape
    spread = jnp.concatenate(
        [
            jnp.broadcast_to(scales[:, block : block + 1], (height, 128))
            for block in range(width // 128)
        ],
        axis=1,
    )
    return codes.astype(jnp.float32) * spread


def relative_of(orders, core, mask):
    found = 0
    for j, bit in enumerate(orders[core]):
        if mask >> j & 1:
            found |= 1 << bit
    return found


SMALL = pl.CostEstimate(flops=0, bytes_accessed=1024, transcendentals=0)
LONG = pl.CostEstimate(flops=5 * 10**9, bytes_accessed=1024, transcendentals=0)
LONGER = pl.CostEstimate(flops=6 * 10**10, bytes_accessed=1024, transcendentals=0)
MEMORY = 60 * 2**20


def after(value, *deps):
    return lax.optimization_barrier((value, *deps))[0]


def tile_of(window):
    return max(128 * k for k in range(1, 6) if window % (128 * k) == 0)


def grad_blocks(index, tokens, fars, cot, cot_far, kind, cost):
    count = len(fars)
    slab, depth = cot.shape
    window = fars[0][0].shape[1]
    tile = tile_of(window)
    tiles = window // tile

    def kernel(index, tok, cot, cot_far, *refs):
        out, left, held, sems, out_sems = refs[count:]
        copies = {}
        for j in range(tiles):
            for i in range(count):
                start = pl.multiple_of(index[i] + j * tile, 128)
                near = tok.at[:, pl.ds(start, tile)]
                far = refs[i].at[pl.ds(fars[i][1] * depth, depth), pl.ds(j * tile, tile)]
                copies[i, j] = [
                    pltpu.make_async_copy(source, left.at[j, i, k], sems.at[j, i, k])
                    for k, source in enumerate((near, far))
                ]
                for copy in copies[i, j]:
                    copy.start()
        done = []
        for j in range(tiles):
            for i in range(count):
                for copy in copies[i, j]:
                    copy.wait()
                held[j, i * slab : (i + 1) * slab, :] = (
                    jnp.dot(cot[...], left[j, i, 0], preferred_element_type=jnp.float32)
                    + jnp.dot(cot_far[...], left[j, i, 1], preferred_element_type=jnp.float32)
                ).astype(kind)
            done.append(
                pltpu.make_async_copy(
                    held.at[j], out.at[:, pl.ds(j * tile, tile)], out_sems.at[j]
                )
            )
            done[-1].start()
        for copy in done:
            copy.wait()

    anywhere = pl.BlockSpec(memory_space=pl.ANY)
    whole = pl.BlockSpec(memory_space=pltpu.VMEM)
    return pl.pallas_call(
        kernel,
        out_shape=jax.ShapeDtypeStruct((count * slab, window), kind),
        in_specs=[pl.BlockSpec(memory_space=pltpu.SMEM), anywhere, whole, whole]
        + [anywhere] * count,
        out_specs=anywhere,
        scratch_shapes=[
            pltpu.VMEM((tiles, count, 2, depth, tile), jnp.bfloat16),
            pltpu.VMEM((tiles, count * slab, tile), kind),
            pltpu.SemaphoreType.DMA((tiles, count, 2)),
            pltpu.SemaphoreType.DMA((tiles,)),
        ],
        compiler_params=pltpu.CompilerParams(vmem_limit_bytes=MEMORY),
        cost_estimate=cost,
    )(index, tokens, cot, cot_far, *[array for array, _ in fars])


def cut_shares(index, keep, came, came2, rows, share):
    slab, window = came2.shape
    tile = tile_of(window)
    n_share = rows // share
    last = window // tile - 1

    def kernel(index, keep, came, came2, own, *refs):
        sends, total = refs[:-1], refs[-1]
        j = pl.program_id(0)
        block = (
            keep[...] + came[...].astype(jnp.float32) + came2[...].astype(jnp.float32)
        )
        total[pl.ds(pl.multiple_of(j * tile, tile), tile), :] = block.T

        @pl.when(j == last)
        def _():
            for k in range(n_share):
                first = index[0] + lax.rem(index[1] + k, n_share) * share
                value = total[pl.ds(pl.multiple_of(first, 16), share), :]
                if k == 0:
                    own[...] = value
                else:
                    sends[k - 1][...] = value.astype(jnp.bfloat16)

    whole = pl.BlockSpec((share, slab), lambda j: (0, 0))
    return pl.pallas_call(
        kernel,
        grid=(window // tile,),
        out_shape=[jax.ShapeDtypeStruct((share, slab), jnp.float32)]
        + [jax.ShapeDtypeStruct((share, slab), jnp.bfloat16)] * (n_share - 1),
        in_specs=[
            pl.BlockSpec(memory_space=pltpu.SMEM),
            pl.BlockSpec((slab, tile), lambda j: (1, j)),
            pl.BlockSpec((slab, tile), lambda j: (1, j)),
            pl.BlockSpec((slab, tile), lambda j: (0, j)),
        ],
        out_specs=[whole] * n_share,
        scratch_shapes=[pltpu.VMEM((window, slab), jnp.float32)],
        compiler_params=pltpu.CompilerParams(vmem_limit_bytes=MEMORY),
        cost_estimate=SMALL,
    )(index, keep, came, came2)


def finish_grad(own, came, signs):
    share, slab = own.shape

    def kernel(own, *refs):
        signs, table, out = refs[-3:]
        total = own[...]
        for ref in refs[:-3]:
            total = total + ref[...].astype(jnp.float32)
        total = total * signs[...]
        result = None
        for _ in range(3):
            part = total.astype(jnp.bfloat16)
            total = total - part.astype(jnp.float32)
            term = jnp.dot(part, table[...], preferred_element_type=jnp.float32)
            result = term if result is None else result + term
        out[...] = result * (1.0 / math.sqrt(128.0))

    table = np.kron(np.eye(slab // 128), sylvester())
    whole = pl.BlockSpec(memory_space=pltpu.VMEM)
    return pl.pallas_call(
        kernel,
        out_shape=jax.ShapeDtypeStruct((share, slab), jnp.float32),
        in_specs=[whole] * (3 + len(came)),
        out_specs=whole,
        compiler_params=pltpu.CompilerParams(vmem_limit_bytes=MEMORY),
        cost_estimate=LONG,
    )(own, *came, signs, jnp.asarray(table, jnp.bfloat16))


def output_part(index, tokens, fars, pieces, before, part):
    steps = len(pieces)
    depth = tokens.shape[0]
    window = fars[0][0].shape[1]
    slab = pieces[0][0][0].shape[1]
    edge = window - 2 * part
    places = len(fars)

    def kernel(index, tok, *refs):
        windows = refs[:places]
        parts = refs[places : places + 2 * steps]
        refs = refs[places + 2 * steps :]
        if before is not None:
            old = refs[:2]
            refs = refs[2:]
        own, other, left, right, sems, piece_sems = refs
        waits = []
        for i in range(steps):
            right[i, 0:edge, :] = jnp.zeros((edge, slab), jnp.bfloat16)
            right[i, window - edge : window, :] = jnp.zeros((edge, slab), jnp.bfloat16)
            start = pl.multiple_of(index[4 * i], 128)
            near = pltpu.make_async_copy(
                tok.at[:, pl.ds(start, window)], left.at[i, pl.ds(0, depth)], sems.at[i, 0]
            )
            near.start()
            copies = [
                pltpu.make_async_copy(
                    windows[place].at[pl.ds(fars[place][1] * depth, depth)],
                    left.at[i, pl.ds(depth, depth)],
                    sems.at[i, 1],
                )
                for place in range(places)
            ]
            for place in range(places):
                pl.when(index[4 * i + 1] == place)(copies[place].start)
            waits.append([near, copies[0]])
            for j in range(2):
                row = pl.multiple_of(index[4 * i + 2 + j], 16)
                first = pieces[i][j][1]
                piece = pltpu.make_async_copy(
                    parts[2 * i + j].at[pl.ds(first, part)],
                    right.at[i, pl.ds(row, part)],
                    piece_sems.at[i, j],
                )
                piece.start()
                waits[-1].append(piece)
        total = None
        for i in range(steps):
            for copy in waits[i]:
                copy.wait()
            term = jnp.dot(left[i], right[i], preferred_element_type=jnp.float32)
            total = term if total is None else total + term
        if before is None:
            own[...] = total[:depth]
            other[...] = total[depth:]
        else:
            own[...] = total[:depth] + old[0][...]
            other[...] = total[depth:] + old[1][...]

    anywhere = pl.BlockSpec(memory_space=pl.ANY)
    whole = pl.BlockSpec(memory_space=pltpu.VMEM)
    shape = jax.ShapeDtypeStruct((depth, slab), jnp.float32)
    olds = () if before is None else tuple(before)
    return pl.pallas_call(
        kernel,
        out_shape=[shape, shape],
        in_specs=[pl.BlockSpec(memory_space=pltpu.SMEM)]
        + [anywhere] * (1 + places + 2 * steps)
        + [whole] * len(olds),
        out_specs=[whole, whole],
        scratch_shapes=[
            pltpu.VMEM((steps, 2 * depth, window), jnp.bfloat16),
            pltpu.VMEM((steps, window, slab), jnp.bfloat16),
            pltpu.SemaphoreType.DMA((steps, 2)),
            pltpu.SemaphoreType.DMA((steps, 2)),
        ],
        compiler_params=pltpu.CompilerParams(vmem_limit_bytes=MEMORY),
        cost_estimate=SMALL,
    )(index, tokens, *[array for array, _ in fars], *[p for pair in pieces for p, _ in pair], *olds)


def paired(mesh):
    n_outer = mesh.shape["outer"]
    n_node = mesh.shape["node"]
    orders = [[1, 2], [2, 1]]

    def core_swap(value):
        return lax.ppermute(value, "outer", [(o, o ^ 1) for o in range(n_outer)])

    def outer_swap(value, stage):
        return lax.ppermute(
            value, "outer", [(o, o ^ (1 << orders[o % 2][stage])) for o in range(n_outer)]
        )

    def node_shift(value, step):
        return lax.ppermute(value, "node", [(n, (n + step) % n_node) for n in range(n_node)])

    def on_device(tokens, cotangent, weight_codes, weight_scales, weight_bits, grad_bits):
        o = lax.axis_index("outer")
        n = lax.axis_index("node")
        core = o % 2
        width = tokens.shape[1]
        rows = width // n_outer
        share = rows // n_node
        node_rows = weight_codes.shape[0]
        window = (rows + 127) // 128 * 128
        edge = window - rows
        masks = (3, 1, 2, 0)

        def column(mask, mine):
            here = core if mine else 1 - core
            base = o if mine else o ^ 1
            which = base ^ jnp.where(
                here == 0, relative_of(orders, 0, mask), relative_of(orders, 1, mask)
            )
            return which // 2 * node_rows + which % 2 * (node_rows - window)

        def take(source, mask):
            return lax.dynamic_slice_in_dim(source, column(mask, False), window, 1)

        leave = [take(tokens, mask) for mask in masks[:2]]
        fars = [(core_swap(value), 0) for value in leave]
        cot = cotangent.T
        cot_far = core_swap(cot)

        part = rows // 2
        side = jnp.where(core == 0, o >> 1, o >> 2) % 2
        start = core * rows + side * part
        held = rotate(
            dequantize(
                lax.dynamic_slice_in_dim(after(weight_codes, *leave), start, part),
                lax.dynamic_slice_in_dim(weight_scales, start, part),
            ),
            weight_bits,
        ).astype(jnp.bfloat16)
        held = [held, node_shift(held, 1), None, node_shift(held, n_node - 1)]
        first_across = outer_swap(held[0], 0)
        source = after(tokens, *leave)
        pair = core_swap(jnp.concatenate([take(source, mask) for mask in masks[2:]]))
        fars += [(pair, 0), (pair, 1)]

        def out_index(steps):
            found = []
            for step in steps:
                node = (n - step) % n_node
                pair = (node ^ (o >> 1)) % 4
                bits = jnp.where(core == 0, pair, (pair >> 1) + 2 * (pair % 2))
                place = jnp.where(bits == 3, 0, jnp.where(bits == 1, 1, jnp.where(bits == 2, 2, 3)))
                found += [
                    node * node_rows + core * (node_rows - window),
                    place,
                    core * edge + side * part,
                    core * edge + (1 - side) * part,
                ]
            return jnp.stack(found).astype(jnp.int32)

        def product(steps, before):
            return output_part(
                out_index(steps),
                tokens,
                fars,
                [((held[step], 0), across[step]) for step in steps],
                before,
                part,
            )

        def blocks(at, source, kind):
            index = jnp.stack([column(mask, True) for mask in masks[at : at + 2]])
            return grad_blocks(
                index.astype(jnp.int32), source, fars[at : at + 2], cot, cot_far, kind, LONGER
            )

        leaving = blocks(0, tokens, jnp.bfloat16)
        came = outer_swap(leaving, 0)
        first_across = after(first_across, leaving)
        keep = blocks(2, after(tokens, first_across), jnp.float32)
        held[2] = node_shift(held[1], 1)
        across = [(first_across, 0)]
        half = slab_of(keep)
        send2 = (keep[:half] + came[:half].astype(jnp.float32)).astype(jnp.bfloat16)
        came2 = outer_swap(send2, 1)
        held[0] = after(held[0], send2)
        early = product((0,), None)
        joined = jnp.concatenate([held[1], held[3]])
        came2, joined, *early = lax.optimization_barrier((came2, joined, *early))
        index = jnp.stack([core * edge, n]).astype(jnp.int32)
        own, *sends = cut_shares(index, keep, came, came2, rows, share)
        arrived = [node_shift(sends[step - 1], step) for step in range(1, n_node)]
        signs = (2 * grad_bits - 1).astype(jnp.float32).reshape(1, -1)
        grad_rotated = finish_grad(own, arrived, signs)

        joined = outer_swap(after(joined, *sends), 0)
        last = outer_swap(after(held[2], *sends), 0)
        across += [(joined, 0), (last, 0), (joined, part)]
        sums = product((1, 3), early)
        own_part, other_part = product((2,), sums)
        output = (own_part + core_swap(other_part)).astype(jnp.bfloat16)
        return output, grad_rotated

    return on_device


def slab_of(stacked):
    return stacked.shape[0] // 2


def general(mesh):
    n_outer = mesh.shape["outer"]
    n_node = mesh.shape["node"]
    n_bits = n_outer.bit_length() - 1
    orders = [list(range(1, n_bits)), [2, 1] + list(range(3, n_bits))]

    def outer_swap(value, stage):
        pairs = []
        for o in range(n_outer):
            pairs.append((o, o ^ (1 if stage is None else 1 << orders[o % 2][stage])))
        return lax.ppermute(value, "outer", pairs)

    def node_shift(value, step):
        return lax.ppermute(value, "node", [(n, (n + step) % n_node) for n in range(n_node)])

    def on_device(tokens, cotangent, weight_codes, weight_scales, weight_bits, grad_bits):
        o = lax.axis_index("outer")
        n = lax.axis_index("node")
        core = o % 2
        width = tokens.shape[1]
        slab = cotangent.shape[1]

        part = weight_codes.shape[0] // 4
        side = jnp.where(core == 0, (o >> orders[0][0]) % 2, (o >> orders[1][0]) % 2)
        mate_side = jnp.where(core == 0, (o >> orders[1][0]) % 2, (o >> orders[0][0]) % 2)
        quarter = core * 2 + side
        start = quarter * part
        held = rotate(
            dequantize(
                lax.dynamic_slice_in_dim(weight_codes, start, part),
                lax.dynamic_slice_in_dim(weight_scales, start, part),
            ),
            weight_bits,
        ).astype(jnp.bfloat16)

        total = lax.dot_general(
            tokens, cotangent, (((0,), (0,)), ((), ())), preferred_element_type=jnp.float32
        ).astype(jnp.bfloat16)
        rows = width // n_outer
        blocks = {}

        def own(d):
            return lax.dynamic_slice_in_dim(total, (o ^ d) * rows, rows)

        def relative(mask):
            found = [0, 0]
            for c in range(2):
                for j, bit in enumerate(orders[c]):
                    if mask >> j & 1:
                        found[c] |= 1 << bit
            return jnp.where(core == 0, found[0], found[1])

        n_rest = n_bits - 1
        sums = {}
        for mask in reversed(range(2**n_rest)):
            partner = jnp.where(core == 0, relative_of(orders, 1, mask), relative_of(orders, 0, mask))
            came = outer_swap(own(partner ^ 1), None)
            sums[mask] = own(relative(mask)).astype(jnp.float32) + came.astype(jnp.float32)
        for stage in range(n_rest):
            low = 1 << stage
            for mask in sorted([m for m in sums if m & low], reverse=True):
                came = outer_swap(sums.pop(mask).astype(jnp.bfloat16), stage)
                sums[mask ^ low] = sums[mask ^ low] + came.astype(jnp.float32)
        mine = sums[0]
        share = rows // n_node
        send = mine.astype(jnp.bfloat16)
        grad = lax.dynamic_slice_in_dim(mine, n * share, share)
        for step in range(1, n_node):
            piece = lax.dynamic_slice_in_dim(send, (n + step) % n_node * share, share)
            grad = grad + node_shift(piece, step).astype(jnp.float32)
        grad_rotated = rotate(grad, grad_bits)

        weight = jnp.zeros((width, slab), jnp.bfloat16)
        node_rows = weight_codes.shape[0]
        for step in range(n_node):
            base = (n - step) % n_node * node_rows
            across = outer_swap(held, 0)
            mate = outer_swap(held, None)
            mate_across = outer_swap(across, None)
            pieces = [
                (held, core * 2 + side),
                (across, core * 2 + 1 - side),
                (mate, (1 - core) * 2 + mate_side),
                (mate_across, (1 - core) * 2 + 1 - mate_side),
            ]
            for value, place in pieces:
                weight = lax.dynamic_update_slice_in_dim(weight, value, base + place * part, 0)
            if step < n_node - 1:
                held = node_shift(held, 1)
        output = jnp.dot(tokens, weight, preferred_element_type=jnp.float32).astype(jnp.bfloat16)
        return output, grad_rotated

    return on_device


def solution(mesh):
    n_outer = mesh.shape["outer"]
    n_node = mesh.shape["node"]
    on_device = paired(mesh) if n_outer == 8 and n_node == 4 else general(mesh)
    return jax.shard_map(
        on_device,
        mesh=mesh,
        in_specs=(
            P(("outer", "node"), None),
            P(("outer", "node"), None),
            P("node", None),
            P("node", None),
            P(),
            P(),
        ),
        out_specs=(P(("outer", "node"), None), P(("outer", "node"), None)),
        check_vma=False,
    )
```

```python
import math

import jax
import jax.numpy as jnp
import numpy as np
from jax import lax
from jax.experimental import pallas as pl
from jax.experimental.pallas import tpu as pltpu
from jax.sharding import PartitionSpec as P


def sylvester():
    row_index = np.arange(128).reshape(128, 1)
    column_index = np.arange(128).reshape(1, 128)
    parity = np.zeros((128, 128))
    for level in range(7):
        parity = parity + row_index // 2**level % 2 * (column_index // 2**level % 2)
    return 1.0 - 2.0 * (parity % 2)


def rotate(values, bits):
    width = values.shape[1]
    signs = (2 * bits - 1).astype(jnp.float32)
    table = np.kron(np.eye(width // 128), sylvester()) / math.sqrt(128.0)
    return jnp.dot(
        values * signs,
        jnp.asarray(table, jnp.float32),
        precision=lax.Precision.HIGHEST,
    )


def dequantize(codes, scales):
    height, width = codes.shape
    spread = jnp.concatenate(
        [
            jnp.broadcast_to(scales[:, block : block + 1], (height, 128))
            for block in range(width // 128)
        ],
        axis=1,
    )
    return codes.astype(jnp.float32) * spread


def relative_of(orders, core, mask):
    found = 0
    for j, bit in enumerate(orders[core]):
        if mask >> j & 1:
            found |= 1 << bit
    return found


SMALL = pl.CostEstimate(flops=0, bytes_accessed=1024, transcendentals=0)
LONG = pl.CostEstimate(flops=5 * 10**9, bytes_accessed=1024, transcendentals=0)
LONGER = pl.CostEstimate(flops=6 * 10**10, bytes_accessed=1024, transcendentals=0)
MIB = 2**20
MEMORY = 56 * MIB


def after(value, *deps):
    return lax.optimization_barrier((value, *deps))[0]


def tile_of(window):
    return max(128 * k for k in range(1, 6) if window % (128 * k) == 0)


def grad_copies(columns, tok, fars, far_refs, added, added_refs, left, more, sems):
    tiles, count, _, depth, tile = left.shape
    slab = more.shape[2]
    copies = []
    for j in range(tiles):
        copies.append([])
        cols = pl.ds(j * tile, tile)
        for i in range(count):
            near = tok.at[:, pl.ds(pl.multiple_of(columns[i] + j * tile, 128), tile)]
            far = far_refs[i].at[pl.ds(fars[i][1] * depth, depth), cols]
            for k, source in enumerate((near, far)):
                copies[j].append(
                    pltpu.make_async_copy(source, left.at[j, i, k], sems.at[j, 2 * i + k])
                )
        for e, (_, place) in enumerate(added):
            copies[j].append(
                pltpu.make_async_copy(
                    added_refs[e].at[pl.ds(place * slab, slab), cols],
                    more.at[j, e],
                    sems.at[j, 2 * count + e],
                )
            )
        for copy in copies[j]:
            copy.start()
    return copies


def grad_tile(j, i, cot, cot_far, left, more, n_added):
    value = jnp.dot(cot[...], left[j, i, 0], preferred_element_type=jnp.float32) + jnp.dot(
        cot_far[...], left[j, i, 1], preferred_element_type=jnp.float32
    )
    for e in range(n_added):
        value = value + more[j, e].astype(jnp.float32)
    return value


def grad_scratch(tiles, count, n_added, depth, slab, tile):
    return [
        pltpu.VMEM((tiles, count, 2, depth, tile), jnp.bfloat16),
        pltpu.VMEM((tiles, max(n_added, 1), slab, tile), jnp.bfloat16),
        pltpu.SemaphoreType.DMA((tiles, 2 * count + n_added)),
    ]


def grad_blocks(columns, tokens, fars, cot, cot_far, added):
    count = len(fars)
    slab, depth = cot.shape
    window = fars[0][0].shape[1]
    tile = tile_of(window)
    tiles = window // tile

    def kernel(tok, cot, cot_far, *refs):
        far_refs, added_refs = refs[:count], refs[count : count + len(added)]
        out, left, more, sems, held, out_sems = refs[count + len(added) :]
        copies = grad_copies(
            columns(), tok, fars, far_refs, added, added_refs, left, more, sems
        )
        done = []
        for j in range(tiles):
            for copy in copies[j]:
                copy.wait()
            for i in range(count):
                value = grad_tile(j, i, cot, cot_far, left, more, len(added))
                held[j, i * slab : (i + 1) * slab, :] = value.astype(jnp.bfloat16)
            done.append(
                pltpu.make_async_copy(
                    held.at[j], out.at[:, pl.ds(j * tile, tile)], out_sems.at[j]
                )
            )
            done[-1].start()
        for copy in done:
            copy.wait()

    anywhere = pl.BlockSpec(memory_space=pl.ANY)
    whole = pl.BlockSpec(memory_space=pltpu.VMEM)
    return pl.pallas_call(
        kernel,
        out_shape=jax.ShapeDtypeStruct((count * slab, window), jnp.bfloat16),
        in_specs=[anywhere, whole, whole] + [anywhere] * (count + len(added)),
        out_specs=anywhere,
        scratch_shapes=grad_scratch(tiles, count, len(added), depth, slab, tile)
        + [
            pltpu.VMEM((tiles, count * slab, tile), jnp.bfloat16),
            pltpu.SemaphoreType.DMA((tiles,)),
        ],
        compiler_params=pltpu.CompilerParams(vmem_limit_bytes=MEMORY),
        cost_estimate=LONG,
    )(tokens, cot, cot_far, *[array for array, _ in fars + added])


def cut_shares(columns, position, tokens, far, cot, cot_far, added, rows, share):
    slab, depth = cot.shape
    window = far[0].shape[1]
    tile = tile_of(window)
    tiles = window // tile
    n_share = rows // share

    def kernel(tok, cot, cot_far, far_ref, *refs):
        added_refs = refs[: len(added)]
        own, *sends = refs[len(added) : len(added) + n_share]
        left, more, sems, total = refs[len(added) + n_share :]
        copies = grad_copies(
            columns(), tok, [far], [far_ref], added, added_refs, left, more, sems
        )
        for j in range(tiles):
            for copy in copies[j]:
                copy.wait()
            block = grad_tile(j, 0, cot, cot_far, left, more, len(added))
            total[j * tile : (j + 1) * tile, :] = block.T
        skip, place = position()
        for k in range(n_share):
            first = skip + lax.rem(place + k, n_share) * share
            value = total[pl.ds(pl.multiple_of(first, 16), share), :]
            if k == 0:
                own[...] = value
            else:
                sends[k - 1][...] = value.astype(jnp.bfloat16)

    anywhere = pl.BlockSpec(memory_space=pl.ANY)
    whole = pl.BlockSpec(memory_space=pltpu.VMEM)
    return pl.pallas_call(
        kernel,
        out_shape=[jax.ShapeDtypeStruct((share, slab), jnp.float32)]
        + [jax.ShapeDtypeStruct((share, slab), jnp.bfloat16)] * (n_share - 1),
        in_specs=[anywhere, whole, whole] + [anywhere] * (1 + len(added)),
        out_specs=[whole] * n_share,
        scratch_shapes=grad_scratch(tiles, 1, len(added), depth, slab, tile)
        + [pltpu.VMEM((window, slab), jnp.float32)],
        compiler_params=pltpu.CompilerParams(vmem_limit_bytes=MEMORY),
        cost_estimate=SMALL,
    )(tokens, cot, cot_far, *[array for array, _ in [far] + added])


def round_sum(own, came, kind):
    def kernel(own, came, out):
        out[...] = (own[...] + came[...]).astype(kind)

    whole = pl.BlockSpec(memory_space=pltpu.VMEM)
    return pl.pallas_call(
        kernel,
        out_shape=jax.ShapeDtypeStruct(own.shape, kind),
        in_specs=[whole, whole],
        out_specs=whole,
        compiler_params=pltpu.CompilerParams(vmem_limit_bytes=4 * MIB),
        cost_estimate=SMALL,
    )(own, came)


def finish_grad(own, came, bits):
    share, slab = own.shape

    def kernel(own, *refs):
        bits, table, out = refs[-3:]
        total = own[...]
        for ref in refs[:-3]:
            total = total + ref[...].astype(jnp.float32)
        total = total * (2 * bits[...] - 1).astype(jnp.float32)
        result = None
        for _ in range(3):
            part = total.astype(jnp.bfloat16)
            total = total - part.astype(jnp.float32)
            term = jnp.dot(part, table[...], preferred_element_type=jnp.float32)
            result = term if result is None else result + term
        out[...] = result * (1.0 / math.sqrt(128.0))

    table = np.kron(np.eye(slab // 128), sylvester())
    whole = pl.BlockSpec(memory_space=pltpu.VMEM)
    return pl.pallas_call(
        kernel,
        out_shape=jax.ShapeDtypeStruct((share, slab), jnp.float32),
        in_specs=[whole] * (3 + len(came)),
        out_specs=whole,
        compiler_params=pltpu.CompilerParams(vmem_limit_bytes=12 * MIB),
        cost_estimate=LONGER,
    )(own, *came, bits, jnp.asarray(table, jnp.bfloat16))


def output_part(position, tokens, fars, gathered, swapped, part):
    depth = tokens.shape[0]
    window = fars[0][0].shape[1]
    slab = gathered.shape[1]
    edge = window - 2 * part
    places = len(fars)

    def kernel(tok, *refs):
        windows = refs[:places]
        parts = refs[places : places + 2]
        own, other, left, right, sems, piece_sems = refs[places + 2 :]
        starts, slots, rows = position()
        waits = []
        for i in range(places):
            right[i, 0:edge, :] = jnp.zeros((edge, slab), jnp.bfloat16)
            right[i, window - edge : window, :] = jnp.zeros((edge, slab), jnp.bfloat16)
            near = pltpu.make_async_copy(
                tok.at[:, pl.ds(pl.multiple_of(starts[i], 128), window)],
                left.at[i, pl.ds(0, depth)],
                sems.at[i, 0],
            )
            near.start()
            copies = [
                pltpu.make_async_copy(
                    windows[place].at[pl.ds(fars[place][1] * depth, depth)],
                    left.at[i, pl.ds(depth, depth)],
                    sems.at[i, 1],
                )
                for place in range(places)
            ]
            for place in range(places):
                pl.when(slots[i] == place)(copies[place].start)
            waits.append([near, copies[0]])
            for j in range(2):
                piece = pltpu.make_async_copy(
                    parts[j].at[pl.ds(i * part, part)],
                    right.at[i, pl.ds(pl.multiple_of(rows[j], 16), part)],
                    piece_sems.at[i, j],
                )
                piece.start()
                waits[-1].append(piece)
        total = None
        for i in range(places):
            for copy in waits[i]:
                copy.wait()
            term = jnp.dot(left[i], right[i], preferred_element_type=jnp.float32)
            total = term if total is None else total + term
        own[...] = total[:depth]
        other[...] = total[depth:]

    anywhere = pl.BlockSpec(memory_space=pl.ANY)
    whole = pl.BlockSpec(memory_space=pltpu.VMEM)
    shape = jax.ShapeDtypeStruct((depth, slab), jnp.float32)
    return pl.pallas_call(
        kernel,
        out_shape=[shape, shape],
        in_specs=[anywhere] * (3 + places),
        out_specs=[whole, whole],
        scratch_shapes=[
            pltpu.VMEM((places, 2 * depth, window), jnp.bfloat16),
            pltpu.VMEM((places, window, slab), jnp.bfloat16),
            pltpu.SemaphoreType.DMA((places, 2)),
            pltpu.SemaphoreType.DMA((places, 2)),
        ],
        compiler_params=pltpu.CompilerParams(vmem_limit_bytes=MEMORY),
        cost_estimate=SMALL,
    )(tokens, *[array for array, _ in fars], gathered, swapped)


def paired(mesh):
    n_outer = mesh.shape["outer"]
    n_node = mesh.shape["node"]
    orders = [[1, 2], [2, 1]]

    def core_swap(value):
        return lax.ppermute(value, "outer", [(o, o ^ 1) for o in range(n_outer)])

    def outer_swap(value, stage):
        return lax.ppermute(
            value, "outer", [(o, o ^ (1 << orders[o % 2][stage])) for o in range(n_outer)]
        )

    def node_shift(value, step):
        return lax.ppermute(value, "node", [(n, (n + step) % n_node) for n in range(n_node)])

    def place_of(o):
        bits = o >> 1
        return jnp.where(o % 2 == 0, bits, (bits >> 1) + 2 * (bits % 2))

    def on_device(tokens, cotangent, weight_codes, weight_scales, weight_bits, grad_bits):
        o = lax.axis_index("outer")
        width = tokens.shape[1]
        rows = width // n_outer
        share = rows // n_node
        node_rows = weight_codes.shape[0]
        window = (rows + 127) // 128 * 128
        edge = window - rows
        masks = (3, 1, 2, 0)

        def column(mask, o, mine):
            base = o if mine else o ^ 1
            which = base ^ jnp.where(
                base % 2 == 0, relative_of(orders, 0, mask), relative_of(orders, 1, mask)
            )
            return which // 2 * node_rows + which % 2 * (node_rows - window)

        def take(source, mask):
            return lax.dynamic_slice_in_dim(source, column(mask, o, False), window, 1)

        leave = [take(tokens, mask) for mask in masks[:2]]
        fars = [(core_swap(value), 0) for value in leave]
        cot = cotangent.T
        cot_far = core_swap(cot)

        part = rows // 2

        def side_of(o):
            return jnp.where(o % 2 == 0, o >> 1, o >> 2) % 2

        start = o % 2 * rows + side_of(o) * part
        held = rotate(
            dequantize(
                lax.dynamic_slice_in_dim(after(weight_codes, *leave), start, part),
                lax.dynamic_slice_in_dim(weight_scales, start, part),
            ),
            weight_bits,
        ).astype(jnp.bfloat16)
        gathered = lax.all_gather(held, "node", axis=0, tiled=True)
        source = after(tokens, held)
        pair = core_swap(jnp.concatenate([take(source, mask) for mask in masks[2:]]))
        fars += [(pair, 0), (pair, 1)]

        def columns(*masks):
            return lambda: [column(mask, lax.axis_index("outer"), True) for mask in masks]

        def position():
            return lax.axis_index("outer") % 2 * edge, lax.axis_index("node")

        leaving = grad_blocks(columns(3, 1), after(tokens, held), fars[:2], cot, cot_far, [])
        came = outer_swap(leaving, 0)
        came2 = outer_swap(
            grad_blocks(columns(2), tokens, fars[2:3], cot, cot_far, [(came, 0)]), 1
        )
        own, *sends = cut_shares(
            columns(0), position, tokens, fars[3], cot, cot_far, [(came, 1), (came2, 0)],
            rows, share,
        )
        arrived = [node_shift(sends[step - 1], step) for step in range(1, n_node)]
        grad_rotated = finish_grad(own, arrived, grad_bits.reshape(1, -1))

        def out_position():
            o = lax.axis_index("outer")
            core = o % 2
            side = side_of(o)
            starts = [node * node_rows + core * (node_rows - window) for node in range(n_node)]
            slots = []
            for node in range(n_node):
                bits = place_of((node * 2 + core) ^ (o - core))
                slots.append(
                    jnp.where(bits == 3, 0, jnp.where(bits == 1, 1, jnp.where(bits == 2, 2, 3)))
                )
            return starts, slots, [core * edge + k * part for k in (side, 1 - side)]

        swapped = outer_swap(after(gathered, *sends), 0)
        own_part, other_part = output_part(out_position, tokens, fars, gathered, swapped, part)
        output = round_sum(own_part, core_swap(other_part), tokens.dtype)
        return output, grad_rotated

    return on_device


def general(mesh):
    n_outer = mesh.shape["outer"]
    n_node = mesh.shape["node"]
    n_bits = n_outer.bit_length() - 1
    orders = [list(range(1, n_bits)), [2, 1] + list(range(3, n_bits))]

    def outer_swap(value, stage):
        pairs = []
        for o in range(n_outer):
            pairs.append((o, o ^ (1 if stage is None else 1 << orders[o % 2][stage])))
        return lax.ppermute(value, "outer", pairs)

    def node_shift(value, step):
        return lax.ppermute(value, "node", [(n, (n + step) % n_node) for n in range(n_node)])

    def on_device(tokens, cotangent, weight_codes, weight_scales, weight_bits, grad_bits):
        o = lax.axis_index("outer")
        n = lax.axis_index("node")
        core = o % 2
        width = tokens.shape[1]
        slab = cotangent.shape[1]

        part = weight_codes.shape[0] // 4
        side = jnp.where(core == 0, (o >> orders[0][0]) % 2, (o >> orders[1][0]) % 2)
        mate_side = jnp.where(core == 0, (o >> orders[1][0]) % 2, (o >> orders[0][0]) % 2)
        quarter = core * 2 + side
        start = quarter * part
        held = rotate(
            dequantize(
                lax.dynamic_slice_in_dim(weight_codes, start, part),
                lax.dynamic_slice_in_dim(weight_scales, start, part),
            ),
            weight_bits,
        ).astype(jnp.bfloat16)

        total = lax.dot_general(
            tokens, cotangent, (((0,), (0,)), ((), ())), preferred_element_type=jnp.float32
        ).astype(jnp.bfloat16)
        rows = width // n_outer
        blocks = {}

        def own(d):
            return lax.dynamic_slice_in_dim(total, (o ^ d) * rows, rows)

        def relative(mask):
            found = [0, 0]
            for c in range(2):
                for j, bit in enumerate(orders[c]):
                    if mask >> j & 1:
                        found[c] |= 1 << bit
            return jnp.where(core == 0, found[0], found[1])

        n_rest = n_bits - 1
        sums = {}
        for mask in reversed(range(2**n_rest)):
            partner = jnp.where(core == 0, relative_of(orders, 1, mask), relative_of(orders, 0, mask))
            came = outer_swap(own(partner ^ 1), None)
            sums[mask] = own(relative(mask)).astype(jnp.float32) + came.astype(jnp.float32)
        for stage in range(n_rest):
            low = 1 << stage
            for mask in sorted([m for m in sums if m & low], reverse=True):
                came = outer_swap(sums.pop(mask).astype(jnp.bfloat16), stage)
                sums[mask ^ low] = sums[mask ^ low] + came.astype(jnp.float32)
        mine = sums[0]
        share = rows // n_node
        send = mine.astype(jnp.bfloat16)
        grad = lax.dynamic_slice_in_dim(mine, n * share, share)
        for step in range(1, n_node):
            piece = lax.dynamic_slice_in_dim(send, (n + step) % n_node * share, share)
            grad = grad + node_shift(piece, step).astype(jnp.float32)
        grad_rotated = rotate(grad, grad_bits)

        weight = jnp.zeros((width, slab), jnp.bfloat16)
        node_rows = weight_codes.shape[0]
        for step in range(n_node):
            base = (n - step) % n_node * node_rows
            across = outer_swap(held, 0)
            mate = outer_swap(held, None)
            mate_across = outer_swap(across, None)
            pieces = [
                (held, core * 2 + side),
                (across, core * 2 + 1 - side),
                (mate, (1 - core) * 2 + mate_side),
                (mate_across, (1 - core) * 2 + 1 - mate_side),
            ]
            for value, place in pieces:
                weight = lax.dynamic_update_slice_in_dim(weight, value, base + place * part, 0)
            if step < n_node - 1:
                held = node_shift(held, 1)
        output = jnp.dot(tokens, weight, preferred_element_type=jnp.float32).astype(jnp.bfloat16)
        return output, grad_rotated

    return on_device


def solution(mesh):
    n_outer = mesh.shape["outer"]
    n_node = mesh.shape["node"]
    on_device = paired(mesh) if n_outer == 8 and n_node == 4 else general(mesh)
    return jax.shard_map(
        on_device,
        mesh=mesh,
        in_specs=(
            P(("outer", "node"), None),
            P(("outer", "node"), None),
            P("node", None),
            P("node", None),
            P(),
            P(),
        ),
        out_specs=(P(("outer", "node"), None), P(("outer", "node"), None)),
        check_vma=False,
    )
```

```python
import math

import jax
import jax.numpy as jnp
import numpy as np
from jax import lax
from jax.experimental import pallas as pl
from jax.experimental.pallas import tpu as pltpu
from jax.sharding import PartitionSpec as P


def sylvester():
    row_index = np.arange(128).reshape(128, 1)
    column_index = np.arange(128).reshape(1, 128)
    parity = np.zeros((128, 128))
    for level in range(7):
        parity = parity + row_index // 2**level % 2 * (column_index // 2**level % 2)
    return 1.0 - 2.0 * (parity % 2)


def rotate(values, bits):
    width = values.shape[1]
    signs = (2 * bits - 1).astype(jnp.float32)
    table = np.kron(np.eye(width // 128), sylvester()) / math.sqrt(128.0)
    return jnp.dot(
        values * signs,
        jnp.asarray(table, jnp.float32),
        precision=lax.Precision.HIGHEST,
    )


def dequantize(codes, scales):
    height, width = codes.shape
    spread = jnp.concatenate(
        [
            jnp.broadcast_to(scales[:, block : block + 1], (height, 128))
            for block in range(width // 128)
        ],
        axis=1,
    )
    return codes.astype(jnp.float32) * spread


def relative_of(orders, core, mask):
    found = 0
    for j, bit in enumerate(orders[core]):
        if mask >> j & 1:
            found |= 1 << bit
    return found


SMALL = pl.CostEstimate(flops=0, bytes_accessed=1024, transcendentals=0)
LONG = pl.CostEstimate(flops=5 * 10**9, bytes_accessed=1024, transcendentals=0)
LONGER = pl.CostEstimate(flops=6 * 10**10, bytes_accessed=1024, transcendentals=0)
MIB = 2**20
MEMORY = 56 * MIB


def after(value, *deps):
    return lax.optimization_barrier((value, *deps))[0]


def tile_of(window):
    return max(128 * k for k in range(1, 6) if window % (128 * k) == 0)


def grad_copies(columns, tok, fars, far_refs, added, added_refs, left, more, sems):
    tiles, count, _, depth, tile = left.shape
    slab = more.shape[2]
    copies = []
    for j in range(tiles):
        copies.append([])
        cols = pl.ds(j * tile, tile)
        for i in range(count):
            near = tok.at[:, pl.ds(pl.multiple_of(columns[i] + j * tile, 128), tile)]
            far = far_refs[i].at[pl.ds(fars[i][1] * depth, depth), cols]
            for k, source in enumerate((near, far)):
                copies[j].append(
                    pltpu.make_async_copy(source, left.at[j, i, k], sems.at[j, 2 * i + k])
                )
        for e, (_, place) in enumerate(added):
            copies[j].append(
                pltpu.make_async_copy(
                    added_refs[e].at[pl.ds(place * slab, slab), cols],
                    more.at[j, e],
                    sems.at[j, 2 * count + e],
                )
            )
        for copy in copies[j]:
            copy.start()
    return copies


def grad_tile(j, i, cot, cot_far, left, more, n_added):
    value = jnp.dot(cot[...], left[j, i, 0], preferred_element_type=jnp.float32) + jnp.dot(
        cot_far[...], left[j, i, 1], preferred_element_type=jnp.float32
    )
    for e in range(n_added):
        value = value + more[j, e].astype(jnp.float32)
    return value


def grad_scratch(tiles, count, n_added, depth, slab, tile):
    return [
        pltpu.VMEM((tiles, count, 2, depth, tile), jnp.bfloat16),
        pltpu.VMEM((tiles, max(n_added, 1), slab, tile), jnp.bfloat16),
        pltpu.SemaphoreType.DMA((tiles, 2 * count + n_added)),
    ]


def grad_blocks(columns, tokens, fars, cot, cot_far, added, cost):
    count = len(fars)
    slab, depth = cot.shape
    window = fars[0][0].shape[1]
    tile = tile_of(window)
    tiles = window // tile

    def kernel(tok, cot, cot_far, *refs):
        far_refs, added_refs = refs[:count], refs[count : count + len(added)]
        out, left, more, sems, held, out_sems = refs[count + len(added) :]
        copies = grad_copies(
            columns(), tok, fars, far_refs, added, added_refs, left, more, sems
        )
        done = []
        for j in range(tiles):
            for copy in copies[j]:
                copy.wait()
            for i in range(count):
                value = grad_tile(j, i, cot, cot_far, left, more, len(added))
                held[j, i * slab : (i + 1) * slab, :] = value.astype(jnp.bfloat16)
            done.append(
                pltpu.make_async_copy(
                    held.at[j], out.at[:, pl.ds(j * tile, tile)], out_sems.at[j]
                )
            )
            done[-1].start()
        for copy in done:
            copy.wait()

    anywhere = pl.BlockSpec(memory_space=pl.ANY)
    whole = pl.BlockSpec(memory_space=pltpu.VMEM)
    return pl.pallas_call(
        kernel,
        out_shape=jax.ShapeDtypeStruct((count * slab, window), jnp.bfloat16),
        in_specs=[anywhere, whole, whole] + [anywhere] * (count + len(added)),
        out_specs=anywhere,
        scratch_shapes=grad_scratch(tiles, count, len(added), depth, slab, tile)
        + [
            pltpu.VMEM((tiles, count * slab, tile), jnp.bfloat16),
            pltpu.SemaphoreType.DMA((tiles,)),
        ],
        compiler_params=pltpu.CompilerParams(vmem_limit_bytes=MEMORY),
        cost_estimate=cost,
    )(tokens, cot, cot_far, *[array for array, _ in fars + added])


def cut_shares(columns, position, tokens, far, cot, cot_far, added, rows, share):
    slab, depth = cot.shape
    window = far[0].shape[1]
    tile = tile_of(window)
    tiles = window // tile
    n_share = rows // share

    def kernel(tok, cot, cot_far, far_ref, *refs):
        added_refs = refs[: len(added)]
        own, *sends = refs[len(added) : len(added) + n_share]
        left, more, sems, total = refs[len(added) + n_share :]
        copies = grad_copies(
            columns(), tok, [far], [far_ref], added, added_refs, left, more, sems
        )
        for j in range(tiles):
            for copy in copies[j]:
                copy.wait()
            block = grad_tile(j, 0, cot, cot_far, left, more, len(added))
            total[j * tile : (j + 1) * tile, :] = block.T
        skip, place = position()
        for k in range(n_share):
            first = skip + lax.rem(place + k, n_share) * share
            value = total[pl.ds(pl.multiple_of(first, 16), share), :]
            if k == 0:
                own[...] = value
            else:
                sends[k - 1][...] = value.astype(jnp.bfloat16)

    anywhere = pl.BlockSpec(memory_space=pl.ANY)
    whole = pl.BlockSpec(memory_space=pltpu.VMEM)
    return pl.pallas_call(
        kernel,
        out_shape=[jax.ShapeDtypeStruct((share, slab), jnp.float32)]
        + [jax.ShapeDtypeStruct((share, slab), jnp.bfloat16)] * (n_share - 1),
        in_specs=[anywhere, whole, whole] + [anywhere] * (1 + len(added)),
        out_specs=[whole] * n_share,
        scratch_shapes=grad_scratch(tiles, 1, len(added), depth, slab, tile)
        + [pltpu.VMEM((window, slab), jnp.float32)],
        compiler_params=pltpu.CompilerParams(vmem_limit_bytes=MEMORY),
        cost_estimate=SMALL,
    )(tokens, cot, cot_far, *[array for array, _ in [far] + added])


def join(upper, lower):
    rows, slab = upper.shape

    def kernel(upper, lower, out, held, sems):
        moves = []
        for i, source in enumerate((upper, lower)):
            moves.append(pltpu.make_async_copy(source, held.at[i], sems.at[i, 0]))
            moves[-1].start()
        done = []
        for i in range(2):
            moves[i].wait()
            done.append(
                pltpu.make_async_copy(held.at[i], out.at[pl.ds(i * rows, rows)], sems.at[i, 1])
            )
            done[-1].start()
        for copy in done:
            copy.wait()

    anywhere = pl.BlockSpec(memory_space=pl.ANY)
    return pl.pallas_call(
        kernel,
        out_shape=jax.ShapeDtypeStruct((2 * rows, slab), upper.dtype),
        in_specs=[anywhere, anywhere],
        out_specs=anywhere,
        scratch_shapes=[
            pltpu.VMEM((2, rows, slab), upper.dtype),
            pltpu.SemaphoreType.DMA((2, 2)),
        ],
        compiler_params=pltpu.CompilerParams(vmem_limit_bytes=4 * MIB),
        cost_estimate=SMALL,
    )(upper, lower)


def round_sum(own, came, kind):
    def kernel(own, came, out):
        out[...] = (own[...] + came[...]).astype(kind)

    whole = pl.BlockSpec(memory_space=pltpu.VMEM)
    return pl.pallas_call(
        kernel,
        out_shape=jax.ShapeDtypeStruct(own.shape, kind),
        in_specs=[whole, whole],
        out_specs=whole,
        compiler_params=pltpu.CompilerParams(vmem_limit_bytes=4 * MIB),
        cost_estimate=SMALL,
    )(own, came)


def finish_grad(own, came, bits):
    share, slab = own.shape

    def kernel(own, *refs):
        bits, table, out = refs[-3:]
        total = own[...]
        for ref in refs[:-3]:
            total = total + ref[...].astype(jnp.float32)
        total = total * (2 * bits[...] - 1).astype(jnp.float32)
        result = None
        for _ in range(3):
            part = total.astype(jnp.bfloat16)
            total = total - part.astype(jnp.float32)
            term = jnp.dot(part, table[...], preferred_element_type=jnp.float32)
            result = term if result is None else result + term
        out[...] = result * (1.0 / math.sqrt(128.0))

    table = np.kron(np.eye(slab // 128), sylvester())
    whole = pl.BlockSpec(memory_space=pltpu.VMEM)
    return pl.pallas_call(
        kernel,
        out_shape=jax.ShapeDtypeStruct((share, slab), jnp.float32),
        in_specs=[whole] * (3 + len(came)),
        out_specs=whole,
        compiler_params=pltpu.CompilerParams(vmem_limit_bytes=12 * MIB),
        cost_estimate=LONGER,
    )(own, *came, bits, jnp.asarray(table, jnp.bfloat16))


def output_part(position, steps, tokens, fars, pieces, before, part):
    depth = tokens.shape[0]
    window = fars[0][0].shape[1]
    slab = pieces[0][0][0].shape[1]
    edge = window - 2 * part
    places = len(fars)
    count = len(steps)

    def kernel(tok, *refs):
        windows = refs[:places]
        parts = refs[places : places + 2 * count]
        refs = refs[places + 2 * count :]
        if before is not None:
            old = refs[:2]
            refs = refs[2:]
        own, other, left, right, sems, piece_sems = refs
        waits = []
        for i, step in enumerate(steps):
            start, slot, rows = position(step)
            near = pltpu.make_async_copy(
                tok.at[:, pl.ds(pl.multiple_of(start, 128), window)],
                left.at[i, pl.ds(0, depth)],
                sems.at[i, 0],
            )
            near.start()
            copies = [
                pltpu.make_async_copy(
                    windows[place].at[pl.ds(fars[place][1] * depth, depth)],
                    left.at[i, pl.ds(depth, depth)],
                    sems.at[i, 1],
                )
                for place in range(places)
            ]
            for place in range(places):
                pl.when(slot == place)(copies[place].start)
            waits.append([near, copies[0]])
            right[i, 0:edge, :] = jnp.zeros((edge, slab), jnp.bfloat16)
            right[i, window - edge : window, :] = jnp.zeros((edge, slab), jnp.bfloat16)
            for j in range(2):
                piece = pltpu.make_async_copy(
                    parts[2 * i + j].at[pl.ds(pieces[i][j][1], part)],
                    right.at[i, pl.ds(pl.multiple_of(rows[j], 16), part)],
                    piece_sems.at[i, j],
                )
                piece.start()
                waits[-1].append(piece)
        total = None
        for i in range(count):
            for copy in waits[i]:
                copy.wait()
            term = jnp.dot(left[i], right[i], preferred_element_type=jnp.float32)
            total = term if total is None else total + term
        if before is None:
            own[...] = total[:depth]
            other[...] = total[depth:]
        else:
            own[...] = total[:depth] + old[0][...]
            other[...] = total[depth:] + old[1][...]

    anywhere = pl.BlockSpec(memory_space=pl.ANY)
    whole = pl.BlockSpec(memory_space=pltpu.VMEM)
    shape = jax.ShapeDtypeStruct((depth, slab), jnp.float32)
    olds = () if before is None else tuple(before)
    return pl.pallas_call(
        kernel,
        out_shape=[shape, shape],
        in_specs=[anywhere] * (1 + places + 2 * count) + [whole] * len(olds),
        out_specs=[whole, whole],
        scratch_shapes=[
            pltpu.VMEM((count, 2 * depth, window), jnp.bfloat16),
            pltpu.VMEM((count, window, slab), jnp.bfloat16),
            pltpu.SemaphoreType.DMA((count, 2)),
            pltpu.SemaphoreType.DMA((count, 2)),
        ],
        compiler_params=pltpu.CompilerParams(vmem_limit_bytes=MEMORY),
        cost_estimate=SMALL,
    )(tokens, *[array for array, _ in fars], *[p for pair in pieces for p, _ in pair], *olds)


def paired(mesh):
    n_outer = mesh.shape["outer"]
    n_node = mesh.shape["node"]
    orders = [[1, 2], [2, 1]]

    def core_swap(value):
        return lax.ppermute(value, "outer", [(o, o ^ 1) for o in range(n_outer)])

    def outer_swap(value, stage):
        return lax.ppermute(
            value, "outer", [(o, o ^ (1 << orders[o % 2][stage])) for o in range(n_outer)]
        )

    def node_shift(value, step):
        return lax.ppermute(value, "node", [(n, (n + step) % n_node) for n in range(n_node)])

    def place_of(o):
        bits = o >> 1
        return jnp.where(o % 2 == 0, bits, (bits >> 1) + 2 * (bits % 2))

    def on_device(tokens, cotangent, weight_codes, weight_scales, weight_bits, grad_bits):
        o = lax.axis_index("outer")
        width = tokens.shape[1]
        rows = width // n_outer
        share = rows // n_node
        node_rows = weight_codes.shape[0]
        window = (rows + 127) // 128 * 128
        edge = window - rows
        masks = (3, 1, 2, 0)

        def column(mask, o, mine):
            base = o if mine else o ^ 1
            which = base ^ jnp.where(
                base % 2 == 0, relative_of(orders, 0, mask), relative_of(orders, 1, mask)
            )
            return which // 2 * node_rows + which % 2 * (node_rows - window)

        def take(source, mask):
            return lax.dynamic_slice_in_dim(source, column(mask, o, False), window, 1)

        leave = [take(tokens, mask) for mask in masks[:2]]
        source = after(tokens, *leave)
        fars = [(core_swap(value), 0) for value in leave]
        fars += [(core_swap(take(source, mask)), 0) for mask in masks[2:]]
        cot = cotangent.T
        cot_far = core_swap(cot)

        part = rows // 2

        def side_of(o):
            return jnp.where(o % 2 == 0, o >> 1, o >> 2) % 2

        start = o % 2 * rows + side_of(o) * part
        held = rotate(
            dequantize(
                lax.dynamic_slice_in_dim(after(weight_codes, *leave), start, part),
                lax.dynamic_slice_in_dim(weight_scales, start, part),
            ),
            weight_bits,
        ).astype(jnp.bfloat16)
        swap0 = outer_swap(held, 0)
        ahead = node_shift(held, 1)

        def columns(*masks):
            return lambda: [column(mask, lax.axis_index("outer"), True) for mask in masks]

        def position():
            return lax.axis_index("outer") % 2 * edge, lax.axis_index("node")

        def block(mask, place, source, added, cost):
            return grad_blocks(
                columns(mask), source, fars[place : place + 1], cot, cot_far, added, cost
            )

        first = block(3, 0, after(tokens, held), [], LONGER)
        came3 = outer_swap(first, 0)
        ahead, swap0, _ = lax.optimization_barrier((ahead, swap0, first))
        second = block(1, 1, after(tokens, first), [], LONGER)
        came1 = outer_swap(after(second, came3), 0)
        passed = block(2, 2, after(tokens, ahead, swap0, second), [(came3, 0)], LONG)
        came2 = outer_swap(passed, 1)
        relay = node_shift(after(ahead, passed), 1)
        behind = node_shift(after(held, passed), n_node - 1)
        joined = join(ahead, behind)
        own, *sends = cut_shares(
            columns(0), position, after(tokens, joined), fars[3], cot, cot_far, [(came1, 0), (came2, 0)],
            rows, share,
        )
        arrived = [node_shift(sends[step - 1], step) for step in range(1, n_node)]
        grad_rotated = finish_grad(own, arrived, grad_bits.reshape(1, -1))

        def out_position(step):
            o = lax.axis_index("outer")
            n = lax.axis_index("node")
            core = o % 2
            node = lax.rem(n + n_node - step, n_node)
            bits = place_of((node * 2 + core) ^ (o - core))
            slot = jnp.where(bits == 3, 0, jnp.where(bits == 1, 1, jnp.where(bits == 2, 2, 3)))
            start = node * node_rows + core * (node_rows - window)
            rows_at = [core * edge + side * part for side in (side_of(o), 1 - side_of(o))]
            return start, slot, rows_at

        def product(steps, pieces, before):
            return output_part(out_position, steps, tokens, fars, pieces, before, part)

        swap13 = outer_swap(after(joined, *sends), 0)
        swap2 = outer_swap(after(relay, *sends), 0)
        sums = product(
            (0, 1, 3),
            [((held, 0), (swap0, 0)), ((ahead, 0), (swap13, 0)), ((behind, 0), (swap13, part))],
            None,
        )
        own_part, other_part = product((2,), [((relay, 0), (swap2, 0))], sums)
        output = round_sum(own_part, core_swap(other_part), tokens.dtype)
        return output, grad_rotated

    return on_device


def general(mesh):
    n_outer = mesh.shape["outer"]
    n_node = mesh.shape["node"]
    n_bits = n_outer.bit_length() - 1
    orders = [list(range(1, n_bits)), [2, 1] + list(range(3, n_bits))]

    def outer_swap(value, stage):
        pairs = []
        for o in range(n_outer):
            pairs.append((o, o ^ (1 if stage is None else 1 << orders[o % 2][stage])))
        return lax.ppermute(value, "outer", pairs)

    def node_shift(value, step):
        return lax.ppermute(value, "node", [(n, (n + step) % n_node) for n in range(n_node)])

    def on_device(tokens, cotangent, weight_codes, weight_scales, weight_bits, grad_bits):
        o = lax.axis_index("outer")
        n = lax.axis_index("node")
        core = o % 2
        width = tokens.shape[1]
        slab = cotangent.shape[1]

        part = weight_codes.shape[0] // 4
        side = jnp.where(core == 0, (o >> orders[0][0]) % 2, (o >> orders[1][0]) % 2)
        mate_side = jnp.where(core == 0, (o >> orders[1][0]) % 2, (o >> orders[0][0]) % 2)
        quarter = core * 2 + side
        start = quarter * part
        held = rotate(
            dequantize(
                lax.dynamic_slice_in_dim(weight_codes, start, part),
                lax.dynamic_slice_in_dim(weight_scales, start, part),
            ),
            weight_bits,
        ).astype(jnp.bfloat16)

        total = lax.dot_general(
            tokens, cotangent, (((0,), (0,)), ((), ())), preferred_element_type=jnp.float32
        ).astype(jnp.bfloat16)
        rows = width // n_outer
        blocks = {}

        def own(d):
            return lax.dynamic_slice_in_dim(total, (o ^ d) * rows, rows)

        def relative(mask):
            found = [0, 0]
            for c in range(2):
                for j, bit in enumerate(orders[c]):
                    if mask >> j & 1:
                        found[c] |= 1 << bit
            return jnp.where(core == 0, found[0], found[1])

        n_rest = n_bits - 1
        sums = {}
        for mask in reversed(range(2**n_rest)):
            partner = jnp.where(core == 0, relative_of(orders, 1, mask), relative_of(orders, 0, mask))
            came = outer_swap(own(partner ^ 1), None)
            sums[mask] = own(relative(mask)).astype(jnp.float32) + came.astype(jnp.float32)
        for stage in range(n_rest):
            low = 1 << stage
            for mask in sorted([m for m in sums if m & low], reverse=True):
                came = outer_swap(sums.pop(mask).astype(jnp.bfloat16), stage)
                sums[mask ^ low] = sums[mask ^ low] + came.astype(jnp.float32)
        mine = sums[0]
        share = rows // n_node
        send = mine.astype(jnp.bfloat16)
        grad = lax.dynamic_slice_in_dim(mine, n * share, share)
        for step in range(1, n_node):
            piece = lax.dynamic_slice_in_dim(send, (n + step) % n_node * share, share)
            grad = grad + node_shift(piece, step).astype(jnp.float32)
        grad_rotated = rotate(grad, grad_bits)

        weight = jnp.zeros((width, slab), jnp.bfloat16)
        node_rows = weight_codes.shape[0]
        for step in range(n_node):
            base = (n - step) % n_node * node_rows
            across = outer_swap(held, 0)
            mate = outer_swap(held, None)
            mate_across = outer_swap(across, None)
            pieces = [
                (held, core * 2 + side),
                (across, core * 2 + 1 - side),
                (mate, (1 - core) * 2 + mate_side),
                (mate_across, (1 - core) * 2 + 1 - mate_side),
            ]
            for value, place in pieces:
                weight = lax.dynamic_update_slice_in_dim(weight, value, base + place * part, 0)
            if step < n_node - 1:
                held = node_shift(held, 1)
        output = jnp.dot(tokens, weight, preferred_element_type=jnp.float32).astype(jnp.bfloat16)
        return output, grad_rotated

    return on_device


def solution(mesh):
    n_outer = mesh.shape["outer"]
    n_node = mesh.shape["node"]
    on_device = paired(mesh) if n_outer == 8 and n_node == 4 else general(mesh)
    return jax.shard_map(
        on_device,
        mesh=mesh,
        in_specs=(
            P(("outer", "node"), None),
            P(("outer", "node"), None),
            P("node", None),
            P("node", None),
            P(),
            P(),
        ),
        out_specs=(P(("outer", "node"), None), P(("outer", "node"), None)),
        check_vma=False,
    )
```

```python
import math

import jax
import jax.numpy as jnp
import numpy as np
from jax import lax
from jax.experimental import pallas as pl
from jax.experimental.pallas import tpu as pltpu
from jax.sharding import PartitionSpec as P


def sylvester():
    row_index = np.arange(128).reshape(128, 1)
    column_index = np.arange(128).reshape(1, 128)
    parity = np.zeros((128, 128))
    for level in range(7):
        parity = parity + row_index // 2**level % 2 * (column_index // 2**level % 2)
    return 1.0 - 2.0 * (parity % 2)


def rotate(values, bits):
    width = values.shape[1]
    signs = (2 * bits - 1).astype(jnp.float32)
    table = np.kron(np.eye(width // 128), sylvester()) / math.sqrt(128.0)
    return jnp.dot(
        values * signs,
        jnp.asarray(table, jnp.float32),
        precision=lax.Precision.HIGHEST,
    )


def dequantize(codes, scales):
    height, width = codes.shape
    spread = jnp.concatenate(
        [
            jnp.broadcast_to(scales[:, block : block + 1], (height, 128))
            for block in range(width // 128)
        ],
        axis=1,
    )
    return codes.astype(jnp.float32) * spread


def relative_of(orders, core, mask):
    found = 0
    for j, bit in enumerate(orders[core]):
        if mask >> j & 1:
            found |= 1 << bit
    return found


SMALL = pl.CostEstimate(flops=0, bytes_accessed=1024, transcendentals=0)
LONG = pl.CostEstimate(flops=5 * 10**9, bytes_accessed=1024, transcendentals=0)
LONGER = pl.CostEstimate(flops=6 * 10**10, bytes_accessed=1024, transcendentals=0)
MIB = 2**20
MEMORY = 56 * MIB


def after(value, *deps):
    return lax.optimization_barrier((value, *deps))[0]


def tile_of(window):
    return max(128 * k for k in range(1, 6) if window % (128 * k) == 0)


def tile_copies(sources, dests, sems):
    return [
        pltpu.make_async_copy(source, dest, sems.at[i])
        for i, (source, dest) in enumerate(zip(sources, dests))
    ]


def start_all(copies):
    for copy in copies:
        copy.start()


def wait_all(copies):
    for copy in copies:
        copy.wait()


def grad_blocks(columns, tokens, fars, cot, cot_far, kinds, cost):
    count = len(fars)
    depth, slab = cot.shape
    window = fars[0].shape[1]
    tile = tile_of(window)
    tiles = window // tile

    def kernel(tok, cot, cot_far, *refs):
        far_refs, outs = refs[:count], refs[count : 2 * count]
        cots, left, sems, cot_sems, out_sems = refs[2 * count : 2 * count + 5]
        held = refs[2 * count + 5 :]
        first = columns()
        ends = tile_copies([cot, cot_far], [cots.at[0], cots.at[1]], cot_sems)
        start_all(ends)
        copies = {}
        for i in range(count):
            for j in range(tiles):
                near = tok.at[:, pl.ds(pl.multiple_of(first[i] + j * tile, 128), tile)]
                far = far_refs[i].at[:, pl.ds(j * tile, tile)]
                copies[i, j] = tile_copies(
                    [near, far], [left.at[i, j, 0], left.at[i, j, 1]], sems.at[i, j]
                )
                start_all(copies[i, j])
        wait_all(ends)
        mine, theirs = cots[0].T, cots[1].T
        done = []
        for i in range(count):
            for j in range(tiles):
                wait_all(copies[i, j])
                held[i][j] = (
                    jnp.dot(mine, left[i, j, 0], preferred_element_type=jnp.float32)
                    + jnp.dot(theirs, left[i, j, 1], preferred_element_type=jnp.float32)
                ).astype(kinds[i])
                done.append(
                    pltpu.make_async_copy(
                        held[i].at[j], outs[i].at[:, pl.ds(j * tile, tile)], out_sems.at[i, j]
                    )
                )
                done[-1].start()
        wait_all(done)

    anywhere = pl.BlockSpec(memory_space=pl.ANY)
    return pl.pallas_call(
        kernel,
        out_shape=[jax.ShapeDtypeStruct((slab, window), kind) for kind in kinds],
        in_specs=[anywhere] * (3 + count),
        out_specs=[anywhere] * count,
        scratch_shapes=[
            pltpu.VMEM((2, depth, slab), jnp.bfloat16),
            pltpu.VMEM((count, tiles, 2, depth, tile), jnp.bfloat16),
            pltpu.SemaphoreType.DMA((count, tiles, 2)),
            pltpu.SemaphoreType.DMA((2,)),
            pltpu.SemaphoreType.DMA((count, tiles)),
        ]
        + [pltpu.VMEM((tiles, slab, tile), kind) for kind in kinds],
        compiler_params=pltpu.CompilerParams(vmem_limit_bytes=MEMORY),
        cost_estimate=cost,
    )(tokens, cot, cot_far, *fars)


def add_blocks(keep, came):
    slab, window = keep.shape
    tile = tile_of(window)
    tiles = window // tile

    def kernel(keep, came, out, left, right, held, sems, out_sems):
        copies = []
        for j in range(tiles):
            cols = pl.ds(j * tile, tile)
            copies.append(
                tile_copies(
                    [keep.at[:, cols], came.at[:, cols]], [left.at[j], right.at[j]], sems.at[j]
                )
            )
            start_all(copies[j])
        done = []
        for j in range(tiles):
            wait_all(copies[j])
            held[j] = (left[j] + right[j].astype(jnp.float32)).astype(jnp.bfloat16)
            done.append(
                pltpu.make_async_copy(held.at[j], out.at[:, pl.ds(j * tile, tile)], out_sems.at[j])
            )
            done[-1].start()
        wait_all(done)

    anywhere = pl.BlockSpec(memory_space=pl.ANY)
    return pl.pallas_call(
        kernel,
        out_shape=jax.ShapeDtypeStruct((slab, window), jnp.bfloat16),
        in_specs=[anywhere] * 2,
        out_specs=anywhere,
        scratch_shapes=[
            pltpu.VMEM((tiles, slab, tile), jnp.float32),
            pltpu.VMEM((tiles, slab, tile), jnp.bfloat16),
            pltpu.VMEM((tiles, slab, tile), jnp.bfloat16),
            pltpu.SemaphoreType.DMA((tiles, 2)),
            pltpu.SemaphoreType.DMA((tiles,)),
        ],
        compiler_params=pltpu.CompilerParams(vmem_limit_bytes=6 * MIB),
        cost_estimate=SMALL,
    )(keep, came)


def cut_shares(position, keep, came, came2, rows, share):
    slab, window = keep.shape
    tile = tile_of(window)
    tiles = window // tile
    n_share = rows // share

    def kernel(keep, came, came2, own, *refs):
        sends = refs[: n_share - 1]
        left, right, total, own_held, send_held, sems, out_sems = refs[n_share - 1 :]
        copies = []
        for j in range(tiles):
            cols = pl.ds(j * tile, tile)
            copies.append(
                tile_copies(
                    [keep.at[:, cols], came.at[:, cols], came2.at[:, cols]],
                    [left.at[j], right.at[j, 0], right.at[j, 1]],
                    sems.at[j],
                )
            )
            start_all(copies[j])
        for j in range(tiles):
            wait_all(copies[j])
            block = (
                left[j] + right[j, 0].astype(jnp.float32) + right[j, 1].astype(jnp.float32)
            )
            total[j * tile : (j + 1) * tile, :] = block.T
        skip, place = position()
        done = []
        for k in [*range(1, n_share), 0]:
            first = skip + lax.rem(place + k, n_share) * share
            value = total[pl.ds(pl.multiple_of(first, 16), share), :]
            if k == 0:
                own_held[...] = value
                copy = pltpu.make_async_copy(own_held, own, out_sems.at[0])
            else:
                send_held[k - 1] = value.astype(jnp.bfloat16)
                copy = pltpu.make_async_copy(send_held.at[k - 1], sends[k - 1], out_sems.at[k])
            copy.start()
            done.append(copy)
        wait_all(done)

    anywhere = pl.BlockSpec(memory_space=pl.ANY)
    return pl.pallas_call(
        kernel,
        out_shape=[jax.ShapeDtypeStruct((share, slab), jnp.float32)]
        + [jax.ShapeDtypeStruct((share, slab), jnp.bfloat16)] * (n_share - 1),
        in_specs=[anywhere] * 3,
        out_specs=[anywhere] * n_share,
        scratch_shapes=[
            pltpu.VMEM((tiles, slab, tile), jnp.float32),
            pltpu.VMEM((tiles, 2, slab, tile), jnp.bfloat16),
            pltpu.VMEM((window, slab), jnp.float32),
            pltpu.VMEM((share, slab), jnp.float32),
            pltpu.VMEM((n_share - 1, share, slab), jnp.bfloat16),
            pltpu.SemaphoreType.DMA((tiles, 3)),
            pltpu.SemaphoreType.DMA((n_share,)),
        ],
        compiler_params=pltpu.CompilerParams(vmem_limit_bytes=9 * MIB),
        cost_estimate=SMALL,
    )(keep, came, came2)


def join(upper, lower):
    rows, slab = upper.shape

    def kernel(upper, lower, out, held, sems):
        moves = []
        for i, source in enumerate((upper, lower)):
            moves.append(pltpu.make_async_copy(source, held.at[i], sems.at[i, 0]))
            moves[-1].start()
        done = []
        for i in range(2):
            moves[i].wait()
            done.append(
                pltpu.make_async_copy(held.at[i], out.at[pl.ds(i * rows, rows)], sems.at[i, 1])
            )
            done[-1].start()
        for copy in done:
            copy.wait()

    anywhere = pl.BlockSpec(memory_space=pl.ANY)
    return pl.pallas_call(
        kernel,
        out_shape=jax.ShapeDtypeStruct((2 * rows, slab), upper.dtype),
        in_specs=[anywhere, anywhere],
        out_specs=anywhere,
        scratch_shapes=[
            pltpu.VMEM((2, rows, slab), upper.dtype),
            pltpu.SemaphoreType.DMA((2, 2)),
        ],
        compiler_params=pltpu.CompilerParams(vmem_limit_bytes=4 * MIB),
        cost_estimate=SMALL,
    )(upper, lower)


def round_sum(own, came, kind):
    def kernel(own, came, out):
        out[...] = (own[...] + came[...]).astype(kind)

    whole = pl.BlockSpec(memory_space=pltpu.VMEM)
    return pl.pallas_call(
        kernel,
        out_shape=jax.ShapeDtypeStruct(own.shape, kind),
        in_specs=[whole, whole],
        out_specs=whole,
        compiler_params=pltpu.CompilerParams(vmem_limit_bytes=4 * MIB),
        cost_estimate=SMALL,
    )(own, came)


def finish_grad(own, came, bits):
    share, slab = own.shape

    def kernel(own, *refs):
        bits, table, out = refs[-3:]
        total = own[...]
        for ref in refs[:-3]:
            total = total + ref[...].astype(jnp.float32)
        total = total * (2 * bits[...] - 1).astype(jnp.float32)
        result = None
        for _ in range(3):
            part = total.astype(jnp.bfloat16)
            total = total - part.astype(jnp.float32)
            term = jnp.dot(part, table[...], preferred_element_type=jnp.float32)
            result = term if result is None else result + term
        out[...] = result * (1.0 / math.sqrt(128.0))

    table = np.kron(np.eye(slab // 128), sylvester())
    whole = pl.BlockSpec(memory_space=pltpu.VMEM)
    return pl.pallas_call(
        kernel,
        out_shape=jax.ShapeDtypeStruct((share, slab), jnp.float32),
        in_specs=[whole] * (3 + len(came)),
        out_specs=whole,
        compiler_params=pltpu.CompilerParams(vmem_limit_bytes=12 * MIB),
        cost_estimate=LONGER,
    )(own, *came, bits, jnp.asarray(table, jnp.bfloat16))


def output_part(position, steps, tokens, fars, pieces, before, part, cost):
    depth = tokens.shape[0]
    window = fars[0].shape[1]
    slab = pieces[0][0][0].shape[1]
    edge = window - 2 * part
    places = len(fars)
    count = len(steps)

    def kernel(tok, *refs):
        windows = refs[:places]
        parts = refs[places : places + 2 * count]
        refs = refs[places + 2 * count :]
        if before is not None:
            old = refs[:2]
            refs = refs[2:]
        own, other, left, right, sums, sems, piece_sems, old_sems = refs
        earlier = []
        if before is not None:
            earlier = tile_copies(old, [sums.at[0], sums.at[1]], old_sems)
            start_all(earlier)
        waits = []
        for i, step in enumerate(steps):
            start, slot, rows = position(step)
            near = pltpu.make_async_copy(
                tok.at[:, pl.ds(pl.multiple_of(start, 128), window)],
                left.at[i, pl.ds(0, depth)],
                sems.at[i, 0],
            )
            near.start()
            copies = [
                pltpu.make_async_copy(
                    windows[place],
                    left.at[i, pl.ds(depth, depth)],
                    sems.at[i, 1],
                )
                for place in range(places)
            ]
            for place in range(places):
                pl.when(slot == place)(copies[place].start)
            waits.append([near, copies[0]])
            right[i, 0:edge, :] = jnp.zeros((edge, slab), jnp.bfloat16)
            right[i, window - edge : window, :] = jnp.zeros((edge, slab), jnp.bfloat16)
            for j in range(2):
                piece = pltpu.make_async_copy(
                    parts[2 * i + j].at[pl.ds(pieces[i][j][1], part)],
                    right.at[i, pl.ds(pl.multiple_of(rows[j], 16), part)],
                    piece_sems.at[i, j],
                )
                piece.start()
                waits[-1].append(piece)
        total = None
        for i in range(count):
            for copy in waits[i]:
                copy.wait()
            term = jnp.dot(left[i], right[i], preferred_element_type=jnp.float32)
            total = term if total is None else total + term
        wait_all(earlier)
        if before is None:
            own[...] = total[:depth]
            other[...] = total[depth:]
        else:
            own[...] = total[:depth] + sums[0]
            other[...] = total[depth:] + sums[1]

    anywhere = pl.BlockSpec(memory_space=pl.ANY)
    whole = pl.BlockSpec(memory_space=pltpu.VMEM)
    shape = jax.ShapeDtypeStruct((depth, slab), jnp.float32)
    olds = () if before is None else tuple(before)
    return pl.pallas_call(
        kernel,
        out_shape=[shape, shape],
        in_specs=[anywhere] * (1 + places + 2 * count + len(olds)),
        out_specs=[whole, whole],
        scratch_shapes=[
            pltpu.VMEM((count, 2 * depth, window), jnp.bfloat16),
            pltpu.VMEM((count, window, slab), jnp.bfloat16),
            pltpu.VMEM((2, depth, slab), jnp.float32),
            pltpu.SemaphoreType.DMA((count, 2)),
            pltpu.SemaphoreType.DMA((count, 2)),
            pltpu.SemaphoreType.DMA((2,)),
        ],
        compiler_params=pltpu.CompilerParams(vmem_limit_bytes=MEMORY),
        cost_estimate=cost,
    )(tokens, *fars, *[p for pair in pieces for p, _ in pair], *olds)


def paired(mesh):
    n_outer = mesh.shape["outer"]
    n_node = mesh.shape["node"]
    orders = [[1, 2], [2, 1]]

    def core_swap(value):
        return lax.ppermute(value, "outer", [(o, o ^ 1) for o in range(n_outer)])

    def outer_swap(value, stage):
        return lax.ppermute(
            value, "outer", [(o, o ^ (1 << orders[o % 2][stage])) for o in range(n_outer)]
        )

    def node_shift(value, step):
        return lax.ppermute(value, "node", [(n, (n + step) % n_node) for n in range(n_node)])

    def place_of(o):
        bits = o >> 1
        return jnp.where(o % 2 == 0, bits, (bits >> 1) + 2 * (bits % 2))

    def on_device(tokens, cotangent, weight_codes, weight_scales, weight_bits, grad_bits):
        o = lax.axis_index("outer")
        width = tokens.shape[1]
        rows = width // n_outer
        share = rows // n_node
        node_rows = weight_codes.shape[0]
        window = (rows + 127) // 128 * 128
        edge = window - rows
        masks = (3, 1, 2, 0)

        def column(mask, o, mine):
            base = o if mine else o ^ 1
            which = base ^ jnp.where(
                base % 2 == 0, relative_of(orders, 0, mask), relative_of(orders, 1, mask)
            )
            return which // 2 * node_rows + which % 2 * (node_rows - window)

        def take(source, mask):
            return lax.dynamic_slice_in_dim(source, column(mask, o, False), window, 1)

        cot_far = core_swap(cotangent)
        leave = take(after(tokens, cotangent), 3)
        source = after(tokens, leave)
        far3 = core_swap(leave)
        fars = [far3] + [core_swap(take(source, mask)) for mask in masks[1:]]

        def columns(*masks):
            return lambda: [column(mask, lax.axis_index("outer"), True) for mask in masks]

        (first,) = grad_blocks(
            columns(3), tokens, fars[:1], cotangent, cot_far, [jnp.bfloat16], LONG
        )
        came3 = outer_swap(first, 0)

        part = rows // 2

        def side_of(o):
            return jnp.where(o % 2 == 0, o >> 1, o >> 2) % 2

        start = o % 2 * rows + side_of(o) * part
        held = rotate(
            dequantize(
                lax.dynamic_slice_in_dim(after(weight_codes, first), start, part),
                lax.dynamic_slice_in_dim(weight_scales, start, part),
            ),
            weight_bits,
        ).astype(jnp.bfloat16)
        swap0 = outer_swap(held, 0)
        ahead = node_shift(held, 1)

        def position():
            return lax.axis_index("outer") % 2 * edge, lax.axis_index("node")

        def out_position(step):
            o = lax.axis_index("outer")
            n = lax.axis_index("node")
            core = o % 2
            node = lax.rem(n + n_node - step, n_node)
            bits = place_of((node * 2 + core) ^ (o - core))
            slot = jnp.where(bits == 3, 0, jnp.where(bits == 1, 1, jnp.where(bits == 2, 2, 3)))
            start = node * node_rows + core * (node_rows - window)
            rows_at = [core * edge + side * part for side in (side_of(o), 1 - side_of(o))]
            return start, slot, rows_at

        def product(steps, pieces, before, later_than, cost):
            source = after(tokens, later_than)
            return output_part(out_position, steps, source, fars, pieces, before, part, cost)

        second, keep2, keep0 = grad_blocks(
            columns(*masks[1:]), after(tokens, held), fars[1:], cotangent, cot_far,
            [jnp.bfloat16, jnp.float32, jnp.float32], LONGER,
        )
        came1 = outer_swap(after(second, came3), 0)
        passed = add_blocks(keep2, came3)
        came2 = outer_swap(passed, 1)
        behind = node_shift(after(held, passed), n_node - 1)
        early = product((0,), [((held, 0), (swap0, 0))], None, passed, LONGER)
        ahead, *early = lax.optimization_barrier((ahead, *early))
        relay = node_shift(ahead, 1)
        came2, *early = lax.optimization_barrier((came2, *early))
        joined = join(ahead, behind)
        own, *sends = cut_shares(position, after(keep0, joined), came1, came2, rows, share)
        arrived = [node_shift(sends[step - 1], step) for step in range(1, n_node)]
        grad_rotated = finish_grad(own, arrived, grad_bits.reshape(1, -1))

        swap13 = outer_swap(after(joined, *sends), 0)
        swap2 = outer_swap(after(relay, *sends), 0)
        sums = product(
            (1, 3), [((ahead, 0), (swap13, 0)), ((behind, 0), (swap13, part))], early, swap13, LONG
        )
        own_part, other_part = product((2,), [((relay, 0), (swap2, 0))], sums, swap2, SMALL)
        output = round_sum(own_part, core_swap(other_part), tokens.dtype)
        return output, grad_rotated

    return on_device


def general(mesh):
    n_outer = mesh.shape["outer"]
    n_node = mesh.shape["node"]
    n_bits = n_outer.bit_length() - 1
    orders = [list(range(1, n_bits)), [2, 1] + list(range(3, n_bits))]

    def outer_swap(value, stage):
        pairs = []
        for o in range(n_outer):
            pairs.append((o, o ^ (1 if stage is None else 1 << orders[o % 2][stage])))
        return lax.ppermute(value, "outer", pairs)

    def node_shift(value, step):
        return lax.ppermute(value, "node", [(n, (n + step) % n_node) for n in range(n_node)])

    def on_device(tokens, cotangent, weight_codes, weight_scales, weight_bits, grad_bits):
        o = lax.axis_index("outer")
        n = lax.axis_index("node")
        core = o % 2
        width = tokens.shape[1]
        slab = cotangent.shape[1]

        part = weight_codes.shape[0] // 4
        side = jnp.where(core == 0, (o >> orders[0][0]) % 2, (o >> orders[1][0]) % 2)
        mate_side = jnp.where(core == 0, (o >> orders[1][0]) % 2, (o >> orders[0][0]) % 2)
        quarter = core * 2 + side
        start = quarter * part
        held = rotate(
            dequantize(
                lax.dynamic_slice_in_dim(weight_codes, start, part),
                lax.dynamic_slice_in_dim(weight_scales, start, part),
            ),
            weight_bits,
        ).astype(jnp.bfloat16)

        total = lax.dot_general(
            tokens, cotangent, (((0,), (0,)), ((), ())), preferred_element_type=jnp.float32
        ).astype(jnp.bfloat16)
        rows = width // n_outer
        blocks = {}

        def own(d):
            return lax.dynamic_slice_in_dim(total, (o ^ d) * rows, rows)

        def relative(mask):
            found = [0, 0]
            for c in range(2):
                for j, bit in enumerate(orders[c]):
                    if mask >> j & 1:
                        found[c] |= 1 << bit
            return jnp.where(core == 0, found[0], found[1])

        n_rest = n_bits - 1
        sums = {}
        for mask in reversed(range(2**n_rest)):
            partner = jnp.where(core == 0, relative_of(orders, 1, mask), relative_of(orders, 0, mask))
            came = outer_swap(own(partner ^ 1), None)
            sums[mask] = own(relative(mask)).astype(jnp.float32) + came.astype(jnp.float32)
        for stage in range(n_rest):
            low = 1 << stage
            for mask in sorted([m for m in sums if m & low], reverse=True):
                came = outer_swap(sums.pop(mask).astype(jnp.bfloat16), stage)
                sums[mask ^ low] = sums[mask ^ low] + came.astype(jnp.float32)
        mine = sums[0]
        share = rows // n_node
        send = mine.astype(jnp.bfloat16)
        grad = lax.dynamic_slice_in_dim(mine, n * share, share)
        for step in range(1, n_node):
            piece = lax.dynamic_slice_in_dim(send, (n + step) % n_node * share, share)
            grad = grad + node_shift(piece, step).astype(jnp.float32)
        grad_rotated = rotate(grad, grad_bits)

        weight = jnp.zeros((width, slab), jnp.bfloat16)
        node_rows = weight_codes.shape[0]
        for step in range(n_node):
            base = (n - step) % n_node * node_rows
            across = outer_swap(held, 0)
            mate = outer_swap(held, None)
            mate_across = outer_swap(across, None)
            pieces = [
                (held, core * 2 + side),
                (across, core * 2 + 1 - side),
                (mate, (1 - core) * 2 + mate_side),
                (mate_across, (1 - core) * 2 + 1 - mate_side),
            ]
            for value, place in pieces:
                weight = lax.dynamic_update_slice_in_dim(weight, value, base + place * part, 0)
            if step < n_node - 1:
                held = node_shift(held, 1)
        output = jnp.dot(tokens, weight, preferred_element_type=jnp.float32).astype(jnp.bfloat16)
        return output, grad_rotated

    return on_device


def solution(mesh):
    n_outer = mesh.shape["outer"]
    n_node = mesh.shape["node"]
    on_device = paired(mesh) if n_outer == 8 and n_node == 4 else general(mesh)
    return jax.shard_map(
        on_device,
        mesh=mesh,
        in_specs=(
            P(("outer", "node"), None),
            P(("outer", "node"), None),
            P("node", None),
            P("node", None),
            P(),
            P(),
        ),
        out_specs=(P(("outer", "node"), None), P(("outer", "node"), None)),
        check_vma=False,
    )
```

```python
import math

import jax
import jax.numpy as jnp
import numpy as np
from jax import lax
from jax.experimental import pallas as pl
from jax.experimental.pallas import tpu as pltpu
from jax.sharding import PartitionSpec as P


def sylvester():
    row_index = np.arange(128).reshape(128, 1)
    column_index = np.arange(128).reshape(1, 128)
    parity = np.zeros((128, 128))
    for level in range(7):
        parity = parity + row_index // 2**level % 2 * (column_index // 2**level % 2)
    return 1.0 - 2.0 * (parity % 2)


def rotate(values, bits):
    width = values.shape[1]
    signs = (2 * bits - 1).astype(jnp.float32)
    table = np.kron(np.eye(width // 128), sylvester()) / math.sqrt(128.0)
    return jnp.dot(
        values * signs,
        jnp.asarray(table, jnp.float32),
        precision=lax.Precision.HIGHEST,
    )


def dequantize(codes, scales):
    height, width = codes.shape
    spread = jnp.concatenate(
        [
            jnp.broadcast_to(scales[:, block : block + 1], (height, 128))
            for block in range(width // 128)
        ],
        axis=1,
    )
    return codes.astype(jnp.float32) * spread


def relative_of(orders, core, mask):
    found = 0
    for j, bit in enumerate(orders[core]):
        if mask >> j & 1:
            found |= 1 << bit
    return found


SMALL = pl.CostEstimate(flops=0, bytes_accessed=1024, transcendentals=0)
LONG = pl.CostEstimate(flops=5 * 10**9, bytes_accessed=1024, transcendentals=0)
LONGER = pl.CostEstimate(flops=6 * 10**10, bytes_accessed=1024, transcendentals=0)
MIB = 2**20
MEMORY = 56 * MIB


def after(value, *deps):
    return lax.optimization_barrier((value, *deps))[0]


def tile_of(window):
    return max(128 * k for k in range(1, 6) if window % (128 * k) == 0)


def tile_copies(sources, dests, sems):
    return [
        pltpu.make_async_copy(source, dest, sems.at[i])
        for i, (source, dest) in enumerate(zip(sources, dests))
    ]


def start_all(copies):
    for copy in copies:
        copy.start()


def wait_all(copies):
    for copy in copies:
        copy.wait()


def grad_blocks(columns, tokens, fars, cot, cot_far, kinds, cost):
    count = len(fars)
    depth, slab = cot.shape
    window = fars[0].shape[1]
    tile = tile_of(window)
    tiles = window // tile

    def kernel(tok, cot, cot_far, *refs):
        far_refs, outs = refs[:count], refs[count : 2 * count]
        cots, left, sems, cot_sems, out_sems = refs[2 * count : 2 * count + 5]
        held = refs[2 * count + 5 :]
        first = columns()
        ends = tile_copies([cot, cot_far], [cots.at[0], cots.at[1]], cot_sems)
        start_all(ends)
        copies = {}
        for i in range(count):
            for j in range(tiles):
                near = tok.at[:, pl.ds(pl.multiple_of(first[i] + j * tile, 128), tile)]
                far = far_refs[i].at[:, pl.ds(j * tile, tile)]
                copies[i, j] = tile_copies(
                    [near, far], [left.at[i, j, 0], left.at[i, j, 1]], sems.at[i, j]
                )
                start_all(copies[i, j])
        wait_all(ends)
        mine, theirs = cots[0].T, cots[1].T
        done = []
        for i in range(count):
            for j in range(tiles):
                wait_all(copies[i, j])
                held[i][j] = (
                    jnp.dot(mine, left[i, j, 0], preferred_element_type=jnp.float32)
                    + jnp.dot(theirs, left[i, j, 1], preferred_element_type=jnp.float32)
                ).astype(kinds[i])
                done.append(
                    pltpu.make_async_copy(
                        held[i].at[j], outs[i].at[:, pl.ds(j * tile, tile)], out_sems.at[i, j]
                    )
                )
                done[-1].start()
        wait_all(done)

    anywhere = pl.BlockSpec(memory_space=pl.ANY)
    return pl.pallas_call(
        kernel,
        out_shape=[jax.ShapeDtypeStruct((slab, window), kind) for kind in kinds],
        in_specs=[anywhere] * (3 + count),
        out_specs=[anywhere] * count,
        scratch_shapes=[
            pltpu.VMEM((2, depth, slab), jnp.bfloat16),
            pltpu.VMEM((count, tiles, 2, depth, tile), jnp.bfloat16),
            pltpu.SemaphoreType.DMA((count, tiles, 2)),
            pltpu.SemaphoreType.DMA((2,)),
            pltpu.SemaphoreType.DMA((count, tiles)),
        ]
        + [pltpu.VMEM((tiles, slab, tile), kind) for kind in kinds],
        compiler_params=pltpu.CompilerParams(vmem_limit_bytes=MEMORY),
        cost_estimate=cost,
    )(tokens, cot, cot_far, *fars)


def add_blocks(keep, came):
    slab, window = keep.shape
    tile = tile_of(window)
    tiles = window // tile

    def kernel(keep, came, out, left, right, held, sems, out_sems):
        copies = []
        for j in range(tiles):
            cols = pl.ds(j * tile, tile)
            copies.append(
                tile_copies(
                    [keep.at[:, cols], came.at[:, cols]], [left.at[j], right.at[j]], sems.at[j]
                )
            )
            start_all(copies[j])
        done = []
        for j in range(tiles):
            wait_all(copies[j])
            held[j] = (left[j] + right[j].astype(jnp.float32)).astype(jnp.bfloat16)
            done.append(
                pltpu.make_async_copy(held.at[j], out.at[:, pl.ds(j * tile, tile)], out_sems.at[j])
            )
            done[-1].start()
        wait_all(done)

    anywhere = pl.BlockSpec(memory_space=pl.ANY)
    return pl.pallas_call(
        kernel,
        out_shape=jax.ShapeDtypeStruct((slab, window), jnp.bfloat16),
        in_specs=[anywhere] * 2,
        out_specs=anywhere,
        scratch_shapes=[
            pltpu.VMEM((tiles, slab, tile), jnp.float32),
            pltpu.VMEM((tiles, slab, tile), jnp.bfloat16),
            pltpu.VMEM((tiles, slab, tile), jnp.bfloat16),
            pltpu.SemaphoreType.DMA((tiles, 2)),
            pltpu.SemaphoreType.DMA((tiles,)),
        ],
        compiler_params=pltpu.CompilerParams(vmem_limit_bytes=6 * MIB),
        cost_estimate=SMALL,
    )(keep, came)


def cut_shares(position, keep, came, came2, rows, share):
    slab, window = keep.shape
    tile = tile_of(window)
    tiles = window // tile
    n_share = rows // share

    def kernel(keep, came, came2, own, *refs):
        sends = refs[: n_share - 1]
        left, right, total, own_held, send_held, sems, out_sems = refs[n_share - 1 :]
        copies = []
        for j in range(tiles):
            cols = pl.ds(j * tile, tile)
            copies.append(
                tile_copies(
                    [keep.at[:, cols], came.at[:, cols], came2.at[:, cols]],
                    [left.at[j], right.at[j, 0], right.at[j, 1]],
                    sems.at[j],
                )
            )
            start_all(copies[j])
        for j in range(tiles):
            wait_all(copies[j])
            block = (
                left[j] + right[j, 0].astype(jnp.float32) + right[j, 1].astype(jnp.float32)
            )
            total[j * tile : (j + 1) * tile, :] = block.T
        skip, place = position()
        done = []
        for k in [*range(1, n_share), 0]:
            first = skip + lax.rem(place + k, n_share) * share
            value = total[pl.ds(pl.multiple_of(first, 16), share), :]
            if k == 0:
                own_held[...] = value
                copy = pltpu.make_async_copy(own_held, own, out_sems.at[0])
            else:
                send_held[k - 1] = value.astype(jnp.bfloat16)
                copy = pltpu.make_async_copy(send_held.at[k - 1], sends[k - 1], out_sems.at[k])
            copy.start()
            done.append(copy)
        wait_all(done)

    anywhere = pl.BlockSpec(memory_space=pl.ANY)
    return pl.pallas_call(
        kernel,
        out_shape=[jax.ShapeDtypeStruct((share, slab), jnp.float32)]
        + [jax.ShapeDtypeStruct((share, slab), jnp.bfloat16)] * (n_share - 1),
        in_specs=[anywhere] * 3,
        out_specs=[anywhere] * n_share,
        scratch_shapes=[
            pltpu.VMEM((tiles, slab, tile), jnp.float32),
            pltpu.VMEM((tiles, 2, slab, tile), jnp.bfloat16),
            pltpu.VMEM((window, slab), jnp.float32),
            pltpu.VMEM((share, slab), jnp.float32),
            pltpu.VMEM((n_share - 1, share, slab), jnp.bfloat16),
            pltpu.SemaphoreType.DMA((tiles, 3)),
            pltpu.SemaphoreType.DMA((n_share,)),
        ],
        compiler_params=pltpu.CompilerParams(vmem_limit_bytes=9 * MIB),
        cost_estimate=SMALL,
    )(keep, came, came2)


def join(upper, lower):
    rows, slab = upper.shape

    def kernel(upper, lower, out, held, sems):
        moves = []
        for i, source in enumerate((upper, lower)):
            moves.append(pltpu.make_async_copy(source, held.at[i], sems.at[i, 0]))
            moves[-1].start()
        done = []
        for i in range(2):
            moves[i].wait()
            done.append(
                pltpu.make_async_copy(held.at[i], out.at[pl.ds(i * rows, rows)], sems.at[i, 1])
            )
            done[-1].start()
        for copy in done:
            copy.wait()

    anywhere = pl.BlockSpec(memory_space=pl.ANY)
    return pl.pallas_call(
        kernel,
        out_shape=jax.ShapeDtypeStruct((2 * rows, slab), upper.dtype),
        in_specs=[anywhere, anywhere],
        out_specs=anywhere,
        scratch_shapes=[
            pltpu.VMEM((2, rows, slab), upper.dtype),
            pltpu.SemaphoreType.DMA((2, 2)),
        ],
        compiler_params=pltpu.CompilerParams(vmem_limit_bytes=4 * MIB),
        cost_estimate=SMALL,
    )(upper, lower)


def round_sum(own, came, kind):
    def kernel(own, came, out):
        out[...] = (own[...] + came[...]).astype(kind)

    whole = pl.BlockSpec(memory_space=pltpu.VMEM)
    return pl.pallas_call(
        kernel,
        out_shape=jax.ShapeDtypeStruct(own.shape, kind),
        in_specs=[whole, whole],
        out_specs=whole,
        compiler_params=pltpu.CompilerParams(vmem_limit_bytes=4 * MIB),
        cost_estimate=SMALL,
    )(own, came)


def finish_grad(own, came, bits):
    share, slab = own.shape

    def kernel(own, *refs):
        bits, table, out = refs[-3:]
        total = own[...]
        for ref in refs[:-3]:
            total = total + ref[...].astype(jnp.float32)
        total = total * (2 * bits[...] - 1).astype(jnp.float32)
        result = None
        for _ in range(3):
            part = total.astype(jnp.bfloat16)
            total = total - part.astype(jnp.float32)
            term = jnp.dot(part, table[...], preferred_element_type=jnp.float32)
            result = term if result is None else result + term
        out[...] = result * (1.0 / math.sqrt(128.0))

    table = np.kron(np.eye(slab // 128), sylvester())
    whole = pl.BlockSpec(memory_space=pltpu.VMEM)
    return pl.pallas_call(
        kernel,
        out_shape=jax.ShapeDtypeStruct((share, slab), jnp.float32),
        in_specs=[whole] * (3 + len(came)),
        out_specs=whole,
        compiler_params=pltpu.CompilerParams(vmem_limit_bytes=12 * MIB),
        cost_estimate=LONGER,
    )(own, *came, bits, jnp.asarray(table, jnp.bfloat16))


def output_part(position, tokens, fars, pieces, before, part, cost):
    depth = tokens.shape[0]
    slab = pieces[0][0].shape[1]
    places = len(fars)
    count = len(pieces)
    lead = part // 128 * 128
    width = fars[0].shape[1] - lead
    edge = width - part

    def kernel(tok, *refs):
        windows = refs[:places]
        parts = refs[places : places + count]
        refs = refs[places + count :]
        if before is not None:
            old = refs[:2]
            refs = refs[2:]
        own, other, left, right, held, sems, piece_sems, old_sems, out_sems = refs
        earlier = []
        if before is not None:
            earlier = tile_copies(old, [held.at[0], held.at[1]], old_sems)
            start_all(earlier)
        waits = []
        for i, (_, first, step, other_side) in enumerate(pieces):
            start, place, column, row = position(step, other_side)
            near = pltpu.make_async_copy(
                tok.at[:, pl.ds(pl.multiple_of(start, 128), width)],
                left.at[i, pl.ds(0, depth)],
                sems.at[i, 0],
            )
            near.start()
            cols = pl.ds(pl.multiple_of(column, 128), width)
            copies = [
                pltpu.make_async_copy(
                    window.at[:, cols], left.at[i, pl.ds(depth, depth)], sems.at[i, 1]
                )
                for window in windows
            ]
            for k in range(places):
                pl.when(place == k)(copies[k].start)
            right[i, 0:edge, :] = jnp.zeros((edge, slab), jnp.bfloat16)
            right[i, width - edge : width, :] = jnp.zeros((edge, slab), jnp.bfloat16)
            piece = pltpu.make_async_copy(
                parts[i].at[pl.ds(first, part)],
                right.at[i, pl.ds(pl.multiple_of(row, 16), part)],
                piece_sems.at[i],
            )
            piece.start()
            waits.append([near, copies[0], piece])
        total = None
        for i in range(count):
            wait_all(waits[i])
            term = jnp.dot(left[i], right[i], preferred_element_type=jnp.float32)
            total = term if total is None else total + term
        wait_all(earlier)
        done = []
        for k, out in ((1, other), (0, own)):
            value = total[k * depth : (k + 1) * depth]
            held[k] = value if before is None else value + held[k]
            done.append(pltpu.make_async_copy(held.at[k], out, out_sems.at[k]))
            done[-1].start()
        wait_all(done)

    anywhere = pl.BlockSpec(memory_space=pl.ANY)
    shape = jax.ShapeDtypeStruct((depth, slab), jnp.float32)
    olds = () if before is None else tuple(before)
    return pl.pallas_call(
        kernel,
        out_shape=[shape, shape],
        in_specs=[anywhere] * (1 + places + count + len(olds)),
        out_specs=[anywhere, anywhere],
        scratch_shapes=[
            pltpu.VMEM((count, 2 * depth, width), jnp.bfloat16),
            pltpu.VMEM((count, width, slab), jnp.bfloat16),
            pltpu.VMEM((2, depth, slab), jnp.float32),
            pltpu.SemaphoreType.DMA((count, 2)),
            pltpu.SemaphoreType.DMA((count,)),
            pltpu.SemaphoreType.DMA((2,)),
            pltpu.SemaphoreType.DMA((2,)),
        ],
        compiler_params=pltpu.CompilerParams(vmem_limit_bytes=MEMORY),
        cost_estimate=cost,
    )(tokens, *fars, *[array for array, *_ in pieces], *olds)


def paired(mesh):
    n_outer = mesh.shape["outer"]
    n_node = mesh.shape["node"]
    orders = [[1, 2], [2, 1]]

    def core_swap(value):
        return lax.ppermute(value, "outer", [(o, o ^ 1) for o in range(n_outer)])

    def outer_swap(value, stage):
        return lax.ppermute(
            value, "outer", [(o, o ^ (1 << orders[o % 2][stage])) for o in range(n_outer)]
        )

    def node_shift(value, step):
        return lax.ppermute(value, "node", [(n, (n + step) % n_node) for n in range(n_node)])

    def place_of(o):
        bits = o >> 1
        return jnp.where(o % 2 == 0, bits, (bits >> 1) + 2 * (bits % 2))

    def on_device(tokens, cotangent, weight_codes, weight_scales, weight_bits, grad_bits):
        o = lax.axis_index("outer")
        width = tokens.shape[1]
        rows = width // n_outer
        share = rows // n_node
        node_rows = weight_codes.shape[0]
        window = (rows + 127) // 128 * 128
        edge = window - rows
        masks = (3, 1, 2, 0)

        def column(mask, o, mine):
            base = o if mine else o ^ 1
            which = base ^ jnp.where(
                base % 2 == 0, relative_of(orders, 0, mask), relative_of(orders, 1, mask)
            )
            return which // 2 * node_rows + which % 2 * (node_rows - window)

        def take(source, mask):
            return lax.dynamic_slice_in_dim(source, column(mask, o, False), window, 1)

        cot_far = core_swap(cotangent)
        leave = take(after(tokens, cotangent), 3)
        source = after(tokens, leave)
        far3 = core_swap(leave)
        fars = [far3] + [core_swap(take(source, mask)) for mask in masks[1:]]

        def columns(*masks):
            return lambda: [column(mask, lax.axis_index("outer"), True) for mask in masks]

        (first,) = grad_blocks(
            columns(3), tokens, fars[:1], cotangent, cot_far, [jnp.bfloat16], LONG
        )
        came3 = outer_swap(first, 0)

        part = rows // 2

        def side_of(o):
            return jnp.where(o % 2 == 0, o >> 1, o >> 2) % 2

        start = o % 2 * rows + side_of(o) * part
        held = rotate(
            dequantize(
                lax.dynamic_slice_in_dim(after(weight_codes, first), start, part),
                lax.dynamic_slice_in_dim(after(weight_scales, first), start, part),
            ),
            after(weight_bits, first),
        ).astype(jnp.bfloat16)
        swap0 = outer_swap(held, 0)
        ahead = node_shift(held, 1)

        def position():
            return lax.axis_index("outer") % 2 * edge, lax.axis_index("node")

        def out_position(step, other_side):
            o = lax.axis_index("outer")
            n = lax.axis_index("node")
            core = o % 2
            node = lax.rem(n + n_node - step, n_node)
            side = side_of(o) if other_side == 0 else 1 - side_of(o)
            bits = place_of((node * 2 + core) ^ (o - core))
            place = jnp.where(bits == 3, 0, jnp.where(bits == 1, 1, jnp.where(bits == 2, 2, 3)))
            lead = part // 128 * 128
            start = node * node_rows + core * (node_rows - window) + side * lead
            return start, place, side * lead, core * edge + side * (part - lead)

        def product(pieces, before, later_than, cost):
            source = after(tokens, later_than)
            return output_part(out_position, source, fars, pieces, before, part, cost)

        second, keep2, keep0 = grad_blocks(
            columns(*masks[1:]), after(tokens, held), fars[1:], cotangent, cot_far,
            [jnp.bfloat16, jnp.float32, jnp.float32], LONGER,
        )
        came1 = outer_swap(after(second, came3), 0)
        passed = add_blocks(keep2, came3)
        came2 = outer_swap(passed, 1)
        behind = node_shift(after(held, passed), n_node - 1)
        early = product([(held, 0, 0, 0), (swap0, 0, 0, 1)], None, passed, LONGER)
        ahead, *early = lax.optimization_barrier((ahead, *early))
        relay = node_shift(ahead, 1)
        came2, *early = lax.optimization_barrier((came2, *early))
        joined = join(ahead, behind)
        own, *sends = cut_shares(position, after(keep0, joined), came1, came2, rows, share)
        arrived = [node_shift(sends[step - 1], step) for step in range(1, n_node)]
        grad_rotated = finish_grad(own, arrived, grad_bits.reshape(1, -1))

        swap13 = outer_swap(after(joined, *sends), 0)
        swap2 = outer_swap(after(relay, *sends), 0)
        sums = product(
            [(ahead, 0, 1, 0), (behind, 0, n_node - 1, 0), (relay, 0, 2, 0)],
            early, sends[0], LONG,
        )
        own_part, other_part = product(
            [(swap13, 0, 1, 1), (swap13, part, n_node - 1, 1), (swap2, 0, 2, 1)],
            sums, swap2, SMALL,
        )
        output = round_sum(own_part, core_swap(other_part), tokens.dtype)
        return output, grad_rotated

    return on_device


def general(mesh):
    n_outer = mesh.shape["outer"]
    n_node = mesh.shape["node"]
    n_bits = n_outer.bit_length() - 1
    orders = [list(range(1, n_bits)), [2, 1] + list(range(3, n_bits))]

    def outer_swap(value, stage):
        pairs = []
        for o in range(n_outer):
            pairs.append((o, o ^ (1 if stage is None else 1 << orders[o % 2][stage])))
        return lax.ppermute(value, "outer", pairs)

    def node_shift(value, step):
        return lax.ppermute(value, "node", [(n, (n + step) % n_node) for n in range(n_node)])

    def on_device(tokens, cotangent, weight_codes, weight_scales, weight_bits, grad_bits):
        o = lax.axis_index("outer")
        n = lax.axis_index("node")
        core = o % 2
        width = tokens.shape[1]
        slab = cotangent.shape[1]

        part = weight_codes.shape[0] // 4
        side = jnp.where(core == 0, (o >> orders[0][0]) % 2, (o >> orders[1][0]) % 2)
        mate_side = jnp.where(core == 0, (o >> orders[1][0]) % 2, (o >> orders[0][0]) % 2)
        quarter = core * 2 + side
        start = quarter * part
        held = rotate(
            dequantize(
                lax.dynamic_slice_in_dim(weight_codes, start, part),
                lax.dynamic_slice_in_dim(weight_scales, start, part),
            ),
            weight_bits,
        ).astype(jnp.bfloat16)

        total = lax.dot_general(
            tokens, cotangent, (((0,), (0,)), ((), ())), preferred_element_type=jnp.float32
        ).astype(jnp.bfloat16)
        rows = width // n_outer
        blocks = {}

        def own(d):
            return lax.dynamic_slice_in_dim(total, (o ^ d) * rows, rows)

        def relative(mask):
            found = [0, 0]
            for c in range(2):
                for j, bit in enumerate(orders[c]):
                    if mask >> j & 1:
                        found[c] |= 1 << bit
            return jnp.where(core == 0, found[0], found[1])

        n_rest = n_bits - 1
        sums = {}
        for mask in reversed(range(2**n_rest)):
            partner = jnp.where(core == 0, relative_of(orders, 1, mask), relative_of(orders, 0, mask))
            came = outer_swap(own(partner ^ 1), None)
            sums[mask] = own(relative(mask)).astype(jnp.float32) + came.astype(jnp.float32)
        for stage in range(n_rest):
            low = 1 << stage
            for mask in sorted([m for m in sums if m & low], reverse=True):
                came = outer_swap(sums.pop(mask).astype(jnp.bfloat16), stage)
                sums[mask ^ low] = sums[mask ^ low] + came.astype(jnp.float32)
        mine = sums[0]
        share = rows // n_node
        send = mine.astype(jnp.bfloat16)
        grad = lax.dynamic_slice_in_dim(mine, n * share, share)
        for step in range(1, n_node):
            piece = lax.dynamic_slice_in_dim(send, (n + step) % n_node * share, share)
            grad = grad + node_shift(piece, step).astype(jnp.float32)
        grad_rotated = rotate(grad, grad_bits)

        weight = jnp.zeros((width, slab), jnp.bfloat16)
        node_rows = weight_codes.shape[0]
        for step in range(n_node):
            base = (n - step) % n_node * node_rows
            across = outer_swap(held, 0)
            mate = outer_swap(held, None)
            mate_across = outer_swap(across, None)
            pieces = [
                (held, core * 2 + side),
                (across, core * 2 + 1 - side),
                (mate, (1 - core) * 2 + mate_side),
                (mate_across, (1 - core) * 2 + 1 - mate_side),
            ]
            for value, place in pieces:
                weight = lax.dynamic_update_slice_in_dim(weight, value, base + place * part, 0)
            if step < n_node - 1:
                held = node_shift(held, 1)
        output = jnp.dot(tokens, weight, preferred_element_type=jnp.float32).astype(jnp.bfloat16)
        return output, grad_rotated

    return on_device


def solution(mesh):
    n_outer = mesh.shape["outer"]
    n_node = mesh.shape["node"]
    on_device = paired(mesh) if n_outer == 8 and n_node == 4 else general(mesh)
    return jax.shard_map(
        on_device,
        mesh=mesh,
        in_specs=(
            P(("outer", "node"), None),
            P(("outer", "node"), None),
            P("node", None),
            P("node", None),
            P(),
            P(),
        ),
        out_specs=(P(("outer", "node"), None), P(("outer", "node"), None)),
        check_vma=False,
    )
```

```python
import math

import jax
import jax.numpy as jnp
import numpy as np
from jax import lax
from jax.experimental import pallas as pl
from jax.experimental.pallas import tpu as pltpu
from jax.sharding import PartitionSpec as P


def sylvester():
    row_index = np.arange(128).reshape(128, 1)
    column_index = np.arange(128).reshape(1, 128)
    parity = np.zeros((128, 128))
    for level in range(7):
        parity = parity + row_index // 2**level % 2 * (column_index // 2**level % 2)
    return 1.0 - 2.0 * (parity % 2)


def rotate(values, bits):
    width = values.shape[1]
    signs = (2 * bits - 1).astype(jnp.float32)
    table = np.kron(np.eye(width // 128), sylvester()) / math.sqrt(128.0)
    return jnp.dot(
        values * signs,
        jnp.asarray(table, jnp.float32),
        precision=lax.Precision.HIGHEST,
    )


def dequantize(codes, scales):
    height, width = codes.shape
    spread = jnp.concatenate(
        [
            jnp.broadcast_to(scales[:, block : block + 1], (height, 128))
            for block in range(width // 128)
        ],
        axis=1,
    )
    return codes.astype(jnp.float32) * spread


def relative_of(orders, core, mask):
    found = 0
    for j, bit in enumerate(orders[core]):
        if mask >> j & 1:
            found |= 1 << bit
    return found


SMALL = pl.CostEstimate(flops=0, bytes_accessed=1024, transcendentals=0)
LONG = pl.CostEstimate(flops=5 * 10**9, bytes_accessed=1024, transcendentals=0)
LONGER = pl.CostEstimate(flops=6 * 10**10, bytes_accessed=1024, transcendentals=0)
MIB = 2**20
MEMORY = 56 * MIB


def after(value, *deps):
    return lax.optimization_barrier((value, *deps))[0]


def tile_of(window):
    return max(128 * k for k in range(1, 6) if window % (128 * k) == 0)


def tile_copies(sources, dests, sems):
    return [
        pltpu.make_async_copy(source, dest, sems.at[i])
        for i, (source, dest) in enumerate(zip(sources, dests))
    ]


def start_all(copies):
    for copy in copies:
        copy.start()


def wait_all(copies):
    for copy in copies:
        copy.wait()


def grad_blocks(columns, tokens, fars, cot, cot_far, kinds, cost, added=None):
    count = len(fars)
    depth, slab = cot.shape
    window = fars[0].shape[1]
    tile = tile_of(window)
    tiles = window // tile

    def kernel(tok, cot, cot_far, *refs):
        far_refs, refs = refs[:count], refs[count:]
        if added is not None:
            added_ref, refs = refs[0], refs[1:]
        outs, refs = refs[:count], refs[count:]
        cots, left, more, sems, cot_sems, out_sems, *held = refs
        first = columns()
        ends = tile_copies([cot, cot_far], [cots.at[0], cots.at[1]], cot_sems)
        start_all(ends)
        copies = {}
        for i in range(count):
            for j in range(tiles):
                near = tok.at[:, pl.ds(pl.multiple_of(first[i] + j * tile, 128), tile)]
                far = far_refs[i].at[:, pl.ds(j * tile, tile)]
                sources, dests = [near, far], [left.at[i, j, 0], left.at[i, j, 1]]
                if added is not None:
                    sources.append(added_ref.at[:, pl.ds(j * tile, tile)])
                    dests.append(more.at[j])
                copies[i, j] = tile_copies(sources, dests, sems.at[i, j])
                start_all(copies[i, j])
        wait_all(ends)
        mine, theirs = cots[0].T, cots[1].T
        done = []
        for i in range(count):
            for j in range(tiles):
                wait_all(copies[i, j])
                value = jnp.dot(
                    mine, left[i, j, 0], preferred_element_type=jnp.float32
                ) + jnp.dot(theirs, left[i, j, 1], preferred_element_type=jnp.float32)
                if added is not None:
                    value = value + more[j].astype(jnp.float32)
                held[i][j] = value.astype(kinds[i])
                done.append(
                    pltpu.make_async_copy(
                        held[i].at[j], outs[i].at[:, pl.ds(j * tile, tile)], out_sems.at[i, j]
                    )
                )
                done[-1].start()
        wait_all(done)

    anywhere = pl.BlockSpec(memory_space=pl.ANY)
    extra = [] if added is None else [added]
    return pl.pallas_call(
        kernel,
        out_shape=[jax.ShapeDtypeStruct((slab, window), kind) for kind in kinds],
        in_specs=[anywhere] * (3 + count + len(extra)),
        out_specs=[anywhere] * count,
        scratch_shapes=[
            pltpu.VMEM((2, depth, slab), jnp.bfloat16),
            pltpu.VMEM((count, tiles, 2, depth, tile), jnp.bfloat16),
            pltpu.VMEM((tiles, slab, tile), jnp.bfloat16),
            pltpu.SemaphoreType.DMA((count, tiles, 3)),
            pltpu.SemaphoreType.DMA((2,)),
            pltpu.SemaphoreType.DMA((count, tiles)),
        ]
        + [pltpu.VMEM((tiles, slab, tile), kind) for kind in kinds],
        compiler_params=pltpu.CompilerParams(vmem_limit_bytes=MEMORY),
        cost_estimate=cost,
    )(tokens, cot, cot_far, *fars, *extra)


def add_blocks(keep, came):
    slab, window = keep.shape
    tile = tile_of(window)
    tiles = window // tile

    def kernel(keep, came, out, left, right, held, sems, out_sems):
        copies = []
        for j in range(tiles):
            cols = pl.ds(j * tile, tile)
            copies.append(
                tile_copies(
                    [keep.at[:, cols], came.at[:, cols]], [left.at[j], right.at[j]], sems.at[j]
                )
            )
            start_all(copies[j])
        done = []
        for j in range(tiles):
            wait_all(copies[j])
            held[j] = (left[j] + right[j].astype(jnp.float32)).astype(jnp.bfloat16)
            done.append(
                pltpu.make_async_copy(held.at[j], out.at[:, pl.ds(j * tile, tile)], out_sems.at[j])
            )
            done[-1].start()
        wait_all(done)

    anywhere = pl.BlockSpec(memory_space=pl.ANY)
    return pl.pallas_call(
        kernel,
        out_shape=jax.ShapeDtypeStruct((slab, window), jnp.bfloat16),
        in_specs=[anywhere] * 2,
        out_specs=anywhere,
        scratch_shapes=[
            pltpu.VMEM((tiles, slab, tile), jnp.float32),
            pltpu.VMEM((tiles, slab, tile), jnp.bfloat16),
            pltpu.VMEM((tiles, slab, tile), jnp.bfloat16),
            pltpu.SemaphoreType.DMA((tiles, 2)),
            pltpu.SemaphoreType.DMA((tiles,)),
        ],
        compiler_params=pltpu.CompilerParams(vmem_limit_bytes=6 * MIB),
        cost_estimate=SMALL,
    )(keep, came)


def cut_shares(position, keep, came, rows, share):
    slab, window = keep.shape
    tile = tile_of(window)
    tiles = window // tile
    n_share = rows // share

    def kernel(keep, came, own, *refs):
        sends = refs[: n_share - 1]
        left, right, total, own_held, send_held, sems, out_sems = refs[n_share - 1 :]
        copies = []
        for j in range(tiles):
            cols = pl.ds(j * tile, tile)
            copies.append(
                tile_copies(
                    [keep.at[:, cols], came.at[:, cols]], [left.at[j], right.at[j]], sems.at[j]
                )
            )
            start_all(copies[j])
        for j in range(tiles):
            wait_all(copies[j])
            total[j * tile : (j + 1) * tile, :] = (left[j] + right[j].astype(jnp.float32)).T
        skip, place = position()
        done = []
        for k in [*range(1, n_share), 0]:
            first = skip + lax.rem(place + k, n_share) * share
            value = total[pl.ds(pl.multiple_of(first, 16), share), :]
            if k == 0:
                own_held[...] = value
                copy = pltpu.make_async_copy(own_held, own, out_sems.at[0])
            else:
                send_held[k - 1] = value.astype(jnp.bfloat16)
                copy = pltpu.make_async_copy(send_held.at[k - 1], sends[k - 1], out_sems.at[k])
            copy.start()
            done.append(copy)
        wait_all(done)

    anywhere = pl.BlockSpec(memory_space=pl.ANY)
    return pl.pallas_call(
        kernel,
        out_shape=[jax.ShapeDtypeStruct((share, slab), jnp.float32)]
        + [jax.ShapeDtypeStruct((share, slab), jnp.bfloat16)] * (n_share - 1),
        in_specs=[anywhere] * 2,
        out_specs=[anywhere] * n_share,
        scratch_shapes=[
            pltpu.VMEM((tiles, slab, tile), jnp.float32),
            pltpu.VMEM((tiles, slab, tile), jnp.bfloat16),
            pltpu.VMEM((window, slab), jnp.float32),
            pltpu.VMEM((share, slab), jnp.float32),
            pltpu.VMEM((n_share - 1, share, slab), jnp.bfloat16),
            pltpu.SemaphoreType.DMA((tiles, 2)),
            pltpu.SemaphoreType.DMA((n_share,)),
        ],
        compiler_params=pltpu.CompilerParams(vmem_limit_bytes=9 * MIB),
        cost_estimate=SMALL,
    )(keep, came)


def join(upper, lower):
    rows, slab = upper.shape

    def kernel(upper, lower, out, held, sems):
        moves = []
        for i, source in enumerate((upper, lower)):
            moves.append(pltpu.make_async_copy(source, held.at[i], sems.at[i, 0]))
            moves[-1].start()
        done = []
        for i in range(2):
            moves[i].wait()
            done.append(
                pltpu.make_async_copy(held.at[i], out.at[pl.ds(i * rows, rows)], sems.at[i, 1])
            )
            done[-1].start()
        for copy in done:
            copy.wait()

    anywhere = pl.BlockSpec(memory_space=pl.ANY)
    return pl.pallas_call(
        kernel,
        out_shape=jax.ShapeDtypeStruct((2 * rows, slab), upper.dtype),
        in_specs=[anywhere, anywhere],
        out_specs=anywhere,
        scratch_shapes=[
            pltpu.VMEM((2, rows, slab), upper.dtype),
            pltpu.SemaphoreType.DMA((2, 2)),
        ],
        compiler_params=pltpu.CompilerParams(vmem_limit_bytes=4 * MIB),
        cost_estimate=SMALL,
    )(upper, lower)


def round_sum(own, came, kind):
    def kernel(own, came, out):
        out[...] = (own[...] + came[...]).astype(kind)

    whole = pl.BlockSpec(memory_space=pltpu.VMEM)
    return pl.pallas_call(
        kernel,
        out_shape=jax.ShapeDtypeStruct(own.shape, kind),
        in_specs=[whole, whole],
        out_specs=whole,
        compiler_params=pltpu.CompilerParams(vmem_limit_bytes=4 * MIB),
        cost_estimate=SMALL,
    )(own, came)


def finish_grad(own, came, bits):
    share, slab = own.shape

    def kernel(own, *refs):
        bits, table, out = refs[-3:]
        total = own[...]
        for ref in refs[:-3]:
            total = total + ref[...].astype(jnp.float32)
        total = total * (2 * bits[...] - 1).astype(jnp.float32)
        result = None
        for _ in range(3):
            part = total.astype(jnp.bfloat16)
            total = total - part.astype(jnp.float32)
            term = jnp.dot(part, table[...], preferred_element_type=jnp.float32)
            result = term if result is None else result + term
        out[...] = result * (1.0 / math.sqrt(128.0))

    table = np.kron(np.eye(slab // 128), sylvester())
    whole = pl.BlockSpec(memory_space=pltpu.VMEM)
    return pl.pallas_call(
        kernel,
        out_shape=jax.ShapeDtypeStruct((share, slab), jnp.float32),
        in_specs=[whole] * (3 + len(came)),
        out_specs=whole,
        compiler_params=pltpu.CompilerParams(vmem_limit_bytes=12 * MIB),
        cost_estimate=LONGER,
    )(own, *came, bits, jnp.asarray(table, jnp.bfloat16))


def output_part(position, tokens, fars, pieces, before, part, cost):
    depth = tokens.shape[0]
    slab = pieces[0][0].shape[1]
    places = len(fars)
    count = len(pieces)
    lead = part // 128 * 128
    width = fars[0].shape[1] - lead
    edge = width - part

    def kernel(tok, *refs):
        windows = refs[:places]
        parts = refs[places : places + count]
        refs = refs[places + count :]
        if before is not None:
            old = refs[:2]
            refs = refs[2:]
        own, other, left, right, held, sems, piece_sems, old_sems, out_sems = refs
        earlier = []
        if before is not None:
            earlier = tile_copies(old, [held.at[0], held.at[1]], old_sems)
            start_all(earlier)
        waits = []
        for i, (_, first, step, other_side) in enumerate(pieces):
            start, place, column, row = position(step, other_side)
            near = pltpu.make_async_copy(
                tok.at[:, pl.ds(pl.multiple_of(start, 128), width)],
                left.at[i, pl.ds(0, depth)],
                sems.at[i, 0],
            )
            near.start()
            cols = pl.ds(pl.multiple_of(column, 128), width)
            copies = [
                pltpu.make_async_copy(
                    window.at[:, cols], left.at[i, pl.ds(depth, depth)], sems.at[i, 1]
                )
                for window in windows
            ]
            for k in range(places):
                pl.when(place == k)(copies[k].start)
            right[i, 0:edge, :] = jnp.zeros((edge, slab), jnp.bfloat16)
            right[i, width - edge : width, :] = jnp.zeros((edge, slab), jnp.bfloat16)
            piece = pltpu.make_async_copy(
                parts[i].at[pl.ds(first, part)],
                right.at[i, pl.ds(pl.multiple_of(row, 16), part)],
                piece_sems.at[i],
            )
            piece.start()
            waits.append([near, copies[0], piece])
        total = None
        for i in range(count):
            wait_all(waits[i])
            term = jnp.dot(left[i], right[i], preferred_element_type=jnp.float32)
            total = term if total is None else total + term
        wait_all(earlier)
        done = []
        for k, out in ((1, other), (0, own)):
            value = total[k * depth : (k + 1) * depth]
            held[k] = value if before is None else value + held[k]
            done.append(pltpu.make_async_copy(held.at[k], out, out_sems.at[k]))
            done[-1].start()
        wait_all(done)

    anywhere = pl.BlockSpec(memory_space=pl.ANY)
    shape = jax.ShapeDtypeStruct((depth, slab), jnp.float32)
    olds = () if before is None else tuple(before)
    return pl.pallas_call(
        kernel,
        out_shape=[shape, shape],
        in_specs=[anywhere] * (1 + places + count + len(olds)),
        out_specs=[anywhere, anywhere],
        scratch_shapes=[
            pltpu.VMEM((count, 2 * depth, width), jnp.bfloat16),
            pltpu.VMEM((count, width, slab), jnp.bfloat16),
            pltpu.VMEM((2, depth, slab), jnp.float32),
            pltpu.SemaphoreType.DMA((count, 2)),
            pltpu.SemaphoreType.DMA((count,)),
            pltpu.SemaphoreType.DMA((2,)),
            pltpu.SemaphoreType.DMA((2,)),
        ],
        compiler_params=pltpu.CompilerParams(vmem_limit_bytes=MEMORY),
        cost_estimate=cost,
    )(tokens, *fars, *[array for array, *_ in pieces], *olds)


def paired(mesh):
    n_outer = mesh.shape["outer"]
    n_node = mesh.shape["node"]
    orders = [[1, 2], [2, 1]]

    def core_swap(value):
        return lax.ppermute(value, "outer", [(o, o ^ 1) for o in range(n_outer)])

    def outer_swap(value, stage):
        return lax.ppermute(
            value, "outer", [(o, o ^ (1 << orders[o % 2][stage])) for o in range(n_outer)]
        )

    def node_shift(value, step):
        return lax.ppermute(value, "node", [(n, (n + step) % n_node) for n in range(n_node)])

    def place_of(o):
        bits = o >> 1
        return jnp.where(o % 2 == 0, bits, (bits >> 1) + 2 * (bits % 2))

    def on_device(tokens, cotangent, weight_codes, weight_scales, weight_bits, grad_bits):
        o = lax.axis_index("outer")
        width = tokens.shape[1]
        rows = width // n_outer
        share = rows // n_node
        node_rows = weight_codes.shape[0]
        window = (rows + 127) // 128 * 128
        edge = window - rows
        masks = (3, 1, 2, 0)

        def column(mask, o, mine):
            base = o if mine else o ^ 1
            which = base ^ jnp.where(
                base % 2 == 0, relative_of(orders, 0, mask), relative_of(orders, 1, mask)
            )
            return which // 2 * node_rows + which % 2 * (node_rows - window)

        def take(source, mask):
            return lax.dynamic_slice_in_dim(source, column(mask, o, False), window, 1)

        cot_far = core_swap(cotangent)
        leave = take(after(tokens, cotangent), 3)
        source = after(tokens, leave)
        far3 = core_swap(leave)
        fars = [far3] + [core_swap(take(source, mask)) for mask in masks[1:]]

        def columns(*masks):
            return lambda: [column(mask, lax.axis_index("outer"), True) for mask in masks]

        (first,) = grad_blocks(
            columns(3), tokens, fars[:1], cotangent, cot_far, [jnp.bfloat16], LONG
        )
        came3 = outer_swap(first, 0)

        part = rows // 2

        def side_of(o):
            return jnp.where(o % 2 == 0, o >> 1, o >> 2) % 2

        start = o % 2 * rows + side_of(o) * part
        held = rotate(
            dequantize(
                lax.dynamic_slice_in_dim(after(weight_codes, first), start, part),
                lax.dynamic_slice_in_dim(after(weight_scales, first), start, part),
            ),
            after(weight_bits, first),
        ).astype(jnp.bfloat16)
        swap0 = outer_swap(held, 0)
        ahead = node_shift(held, 1)

        def position():
            return lax.axis_index("outer") % 2 * edge, lax.axis_index("node")

        def out_position(step, other_side):
            o = lax.axis_index("outer")
            n = lax.axis_index("node")
            core = o % 2
            node = lax.rem(n + n_node - step, n_node)
            side = side_of(o) if other_side == 0 else 1 - side_of(o)
            bits = place_of((node * 2 + core) ^ (o - core))
            place = jnp.where(bits == 3, 0, jnp.where(bits == 1, 1, jnp.where(bits == 2, 2, 3)))
            lead = part // 128 * 128
            start = node * node_rows + core * (node_rows - window) + side * lead
            return start, place, side * lead, core * edge + side * (part - lead)

        def product(pieces, before, later_than, cost):
            source = after(tokens, later_than)
            return output_part(out_position, source, fars, pieces, before, part, cost)

        second, keep2 = grad_blocks(
            columns(*masks[1:3]), after(tokens, held), fars[1:3], cotangent, cot_far,
            [jnp.bfloat16, jnp.float32], LONGER,
        )
        came1 = outer_swap(second, 0)
        passed = add_blocks(keep2, came3)
        came2 = outer_swap(passed, 1)
        behind = node_shift(after(held, passed), n_node - 1)
        early = product([(held, 0, 0, 0), (swap0, 0, 0, 1)], None, passed, LONGER)
        ahead, *early = lax.optimization_barrier((ahead, *early))
        relay = node_shift(ahead, 1)
        joined = join(ahead, behind)
        (keep0,) = grad_blocks(
            columns(masks[3]), after(tokens, *early), fars[3:], cotangent, cot_far,
            [jnp.float32], LONGER, came1,
        )
        came2, joined, _ = lax.optimization_barrier((came2, joined, keep0))
        own, *sends = cut_shares(position, keep0, came2, rows, share)
        arrived = [node_shift(sends[step - 1], step) for step in range(1, n_node)]
        grad_rotated = finish_grad(own, arrived, grad_bits.reshape(1, -1))

        swap13 = outer_swap(joined, 0)
        swap2 = outer_swap(after(relay, *sends), 0)
        sums = product(
            [(ahead, 0, 1, 0), (behind, 0, n_node - 1, 0), (relay, 0, 2, 0)],
            early, sends[0], LONG,
        )
        own_part, other_part = product(
            [(swap13, 0, 1, 1), (swap13, part, n_node - 1, 1), (swap2, 0, 2, 1)],
            sums, swap2, SMALL,
        )
        output = round_sum(own_part, core_swap(other_part), tokens.dtype)
        return output, grad_rotated

    return on_device


def general(mesh):
    n_outer = mesh.shape["outer"]
    n_node = mesh.shape["node"]
    n_bits = n_outer.bit_length() - 1
    orders = [list(range(1, n_bits)), [2, 1] + list(range(3, n_bits))]

    def outer_swap(value, stage):
        pairs = []
        for o in range(n_outer):
            pairs.append((o, o ^ (1 if stage is None else 1 << orders[o % 2][stage])))
        return lax.ppermute(value, "outer", pairs)

    def node_shift(value, step):
        return lax.ppermute(value, "node", [(n, (n + step) % n_node) for n in range(n_node)])

    def on_device(tokens, cotangent, weight_codes, weight_scales, weight_bits, grad_bits):
        o = lax.axis_index("outer")
        n = lax.axis_index("node")
        core = o % 2
        width = tokens.shape[1]
        slab = cotangent.shape[1]

        part = weight_codes.shape[0] // 4
        side = jnp.where(core == 0, (o >> orders[0][0]) % 2, (o >> orders[1][0]) % 2)
        mate_side = jnp.where(core == 0, (o >> orders[1][0]) % 2, (o >> orders[0][0]) % 2)
        quarter = core * 2 + side
        start = quarter * part
        held = rotate(
            dequantize(
                lax.dynamic_slice_in_dim(weight_codes, start, part),
                lax.dynamic_slice_in_dim(weight_scales, start, part),
            ),
            weight_bits,
        ).astype(jnp.bfloat16)

        total = lax.dot_general(
            tokens, cotangent, (((0,), (0,)), ((), ())), preferred_element_type=jnp.float32
        ).astype(jnp.bfloat16)
        rows = width // n_outer
        blocks = {}

        def own(d):
            return lax.dynamic_slice_in_dim(total, (o ^ d) * rows, rows)

        def relative(mask):
            found = [0, 0]
            for c in range(2):
                for j, bit in enumerate(orders[c]):
                    if mask >> j & 1:
                        found[c] |= 1 << bit
            return jnp.where(core == 0, found[0], found[1])

        n_rest = n_bits - 1
        sums = {}
        for mask in reversed(range(2**n_rest)):
            partner = jnp.where(core == 0, relative_of(orders, 1, mask), relative_of(orders, 0, mask))
            came = outer_swap(own(partner ^ 1), None)
            sums[mask] = own(relative(mask)).astype(jnp.float32) + came.astype(jnp.float32)
        for stage in range(n_rest):
            low = 1 << stage
            for mask in sorted([m for m in sums if m & low], reverse=True):
                came = outer_swap(sums.pop(mask).astype(jnp.bfloat16), stage)
                sums[mask ^ low] = sums[mask ^ low] + came.astype(jnp.float32)
        mine = sums[0]
        share = rows // n_node
        send = mine.astype(jnp.bfloat16)
        grad = lax.dynamic_slice_in_dim(mine, n * share, share)
        for step in range(1, n_node):
            piece = lax.dynamic_slice_in_dim(send, (n + step) % n_node * share, share)
            grad = grad + node_shift(piece, step).astype(jnp.float32)
        grad_rotated = rotate(grad, grad_bits)

        weight = jnp.zeros((width, slab), jnp.bfloat16)
        node_rows = weight_codes.shape[0]
        for step in range(n_node):
            base = (n - step) % n_node * node_rows
            across = outer_swap(held, 0)
            mate = outer_swap(held, None)
            mate_across = outer_swap(across, None)
            pieces = [
                (held, core * 2 + side),
                (across, core * 2 + 1 - side),
                (mate, (1 - core) * 2 + mate_side),
                (mate_across, (1 - core) * 2 + 1 - mate_side),
            ]
            for value, place in pieces:
                weight = lax.dynamic_update_slice_in_dim(weight, value, base + place * part, 0)
            if step < n_node - 1:
                held = node_shift(held, 1)
        output = jnp.dot(tokens, weight, preferred_element_type=jnp.float32).astype(jnp.bfloat16)
        return output, grad_rotated

    return on_device


def solution(mesh):
    n_outer = mesh.shape["outer"]
    n_node = mesh.shape["node"]
    on_device = paired(mesh) if n_outer == 8 and n_node == 4 else general(mesh)
    return jax.shard_map(
        on_device,
        mesh=mesh,
        in_specs=(
            P(("outer", "node"), None),
            P(("outer", "node"), None),
            P("node", None),
            P("node", None),
            P(),
            P(),
        ),
        out_specs=(P(("outer", "node"), None), P(("outer", "node"), None)),
        check_vma=False,
    )
```

```python
import math

import jax
import jax.numpy as jnp
import numpy as np
from jax import lax
from jax.experimental import pallas as pl
from jax.experimental.pallas import tpu as pltpu
from jax.sharding import PartitionSpec as P


def sylvester():
    row_index = np.arange(128).reshape(128, 1)
    column_index = np.arange(128).reshape(1, 128)
    parity = np.zeros((128, 128))
    for level in range(7):
        parity = parity + row_index // 2**level % 2 * (column_index // 2**level % 2)
    return 1.0 - 2.0 * (parity % 2)


def rotate(values, bits):
    width = values.shape[1]
    signs = (2 * bits - 1).astype(jnp.float32)
    table = np.kron(np.eye(width // 128), sylvester()) / math.sqrt(128.0)
    return jnp.dot(
        values * signs,
        jnp.asarray(table, jnp.float32),
        precision=lax.Precision.HIGHEST,
    )


def dequantize(codes, scales):
    height, width = codes.shape
    spread = jnp.concatenate(
        [
            jnp.broadcast_to(scales[:, block : block + 1], (height, 128))
            for block in range(width // 128)
        ],
        axis=1,
    )
    return codes.astype(jnp.float32) * spread


def relative_of(orders, core, mask):
    found = 0
    for j, bit in enumerate(orders[core]):
        if mask >> j & 1:
            found |= 1 << bit
    return found


SMALL = pl.CostEstimate(flops=0, bytes_accessed=1024, transcendentals=0)
LONG = pl.CostEstimate(flops=5 * 10**9, bytes_accessed=1024, transcendentals=0)
LONGER = pl.CostEstimate(flops=6 * 10**10, bytes_accessed=1024, transcendentals=0)
MIB = 2**20
MEMORY = 56 * MIB


def after(value, *deps):
    return lax.optimization_barrier((value, *deps))[0]


def tile_of(window):
    return max(128 * k for k in range(1, 6) if window % (128 * k) == 0)


def tile_copies(sources, dests, sems):
    return [
        pltpu.make_async_copy(source, dest, sems.at[i])
        for i, (source, dest) in enumerate(zip(sources, dests))
    ]


def start_all(copies):
    for copy in copies:
        copy.start()


def wait_all(copies):
    for copy in copies:
        copy.wait()


def grad_blocks(columns, tokens, fars, cot, cot_far, kinds, cost):
    count = len(fars)
    depth, slab = cot.shape
    window = fars[0].shape[1]
    tile = tile_of(window)
    tiles = window // tile

    def kernel(tok, cot, cot_far, *refs):
        far_refs, outs = refs[:count], refs[count : 2 * count]
        cots, left, sems, cot_sems, out_sems = refs[2 * count : 2 * count + 5]
        held = refs[2 * count + 5 :]
        first = columns()
        ends = tile_copies([cot, cot_far], [cots.at[0], cots.at[1]], cot_sems)
        start_all(ends)
        copies = {}
        for i in range(count):
            for j in range(tiles):
                near = tok.at[:, pl.ds(pl.multiple_of(first[i] + j * tile, 128), tile)]
                far = far_refs[i].at[:, pl.ds(j * tile, tile)]
                copies[i, j] = tile_copies(
                    [near, far], [left.at[i, j, 0], left.at[i, j, 1]], sems.at[i, j]
                )
                start_all(copies[i, j])
        wait_all(ends)
        mine, theirs = cots[0].T, cots[1].T
        done = []
        for i in range(count):
            for j in range(tiles):
                wait_all(copies[i, j])
                held[i][j] = (
                    jnp.dot(mine, left[i, j, 0], preferred_element_type=jnp.float32)
                    + jnp.dot(theirs, left[i, j, 1], preferred_element_type=jnp.float32)
                ).astype(kinds[i])
                done.append(
                    pltpu.make_async_copy(
                        held[i].at[j], outs[i].at[:, pl.ds(j * tile, tile)], out_sems.at[i, j]
                    )
                )
                done[-1].start()
        wait_all(done)

    anywhere = pl.BlockSpec(memory_space=pl.ANY)
    return pl.pallas_call(
        kernel,
        out_shape=[jax.ShapeDtypeStruct((slab, window), kind) for kind in kinds],
        in_specs=[anywhere] * (3 + count),
        out_specs=[anywhere] * count,
        scratch_shapes=[
            pltpu.VMEM((2, depth, slab), jnp.bfloat16),
            pltpu.VMEM((count, tiles, 2, depth, tile), jnp.bfloat16),
            pltpu.SemaphoreType.DMA((count, tiles, 2)),
            pltpu.SemaphoreType.DMA((2,)),
            pltpu.SemaphoreType.DMA((count, tiles)),
        ]
        + [pltpu.VMEM((tiles, slab, tile), kind) for kind in kinds],
        compiler_params=pltpu.CompilerParams(vmem_limit_bytes=MEMORY),
        cost_estimate=cost,
    )(tokens, cot, cot_far, *fars)


def add_blocks(keep, came):
    slab, window = keep.shape
    tile = tile_of(window)
    tiles = window // tile

    def kernel(keep, came, out, left, right, held, sems, out_sems):
        copies = []
        for j in range(tiles):
            cols = pl.ds(j * tile, tile)
            copies.append(
                tile_copies(
                    [keep.at[:, cols], came.at[:, cols]], [left.at[j], right.at[j]], sems.at[j]
                )
            )
            start_all(copies[j])
        done = []
        for j in range(tiles):
            wait_all(copies[j])
            held[j] = (left[j] + right[j].astype(jnp.float32)).astype(jnp.bfloat16)
            done.append(
                pltpu.make_async_copy(held.at[j], out.at[:, pl.ds(j * tile, tile)], out_sems.at[j])
            )
            done[-1].start()
        wait_all(done)

    anywhere = pl.BlockSpec(memory_space=pl.ANY)
    return pl.pallas_call(
        kernel,
        out_shape=jax.ShapeDtypeStruct((slab, window), jnp.bfloat16),
        in_specs=[anywhere] * 2,
        out_specs=anywhere,
        scratch_shapes=[
            pltpu.VMEM((tiles, slab, tile), jnp.float32),
            pltpu.VMEM((tiles, slab, tile), jnp.bfloat16),
            pltpu.VMEM((tiles, slab, tile), jnp.bfloat16),
            pltpu.SemaphoreType.DMA((tiles, 2)),
            pltpu.SemaphoreType.DMA((tiles,)),
        ],
        compiler_params=pltpu.CompilerParams(vmem_limit_bytes=MEMORY),
        cost_estimate=SMALL,
    )(keep, came)


def cut_shares(position, keep, came, came2, rows, share):
    slab, window = keep.shape
    tile = tile_of(window)
    tiles = window // tile
    n_share = rows // share

    def kernel(keep, came, came2, own, *refs):
        sends = refs[: n_share - 1]
        left, right, total, own_held, send_held, sems, out_sems = refs[n_share - 1 :]
        copies = []
        for j in range(tiles):
            cols = pl.ds(j * tile, tile)
            copies.append(
                tile_copies(
                    [keep.at[:, cols], came.at[:, cols], came2.at[:, cols]],
                    [left.at[j], right.at[j, 0], right.at[j, 1]],
                    sems.at[j],
                )
            )
            start_all(copies[j])
        for j in range(tiles):
            wait_all(copies[j])
            block = (
                left[j] + right[j, 0].astype(jnp.float32) + right[j, 1].astype(jnp.float32)
            )
            total[j * tile : (j + 1) * tile, :] = block.T
        skip, place = position()
        done = []
        for k in [*range(1, n_share), 0]:
            first = skip + lax.rem(place + k, n_share) * share
            value = total[pl.ds(pl.multiple_of(first, 16), share), :]
            if k == 0:
                own_held[...] = value
                copy = pltpu.make_async_copy(own_held, own, out_sems.at[0])
            else:
                send_held[k - 1] = value.astype(jnp.bfloat16)
                copy = pltpu.make_async_copy(send_held.at[k - 1], sends[k - 1], out_sems.at[k])
            copy.start()
            done.append(copy)
        wait_all(done)

    anywhere = pl.BlockSpec(memory_space=pl.ANY)
    return pl.pallas_call(
        kernel,
        out_shape=[jax.ShapeDtypeStruct((share, slab), jnp.float32)]
        + [jax.ShapeDtypeStruct((share, slab), jnp.bfloat16)] * (n_share - 1),
        in_specs=[anywhere] * 3,
        out_specs=[anywhere] * n_share,
        scratch_shapes=[
            pltpu.VMEM((tiles, slab, tile), jnp.float32),
            pltpu.VMEM((tiles, 2, slab, tile), jnp.bfloat16),
            pltpu.VMEM((window, slab), jnp.float32),
            pltpu.VMEM((share, slab), jnp.float32),
            pltpu.VMEM((n_share - 1, share, slab), jnp.bfloat16),
            pltpu.SemaphoreType.DMA((tiles, 3)),
            pltpu.SemaphoreType.DMA((n_share,)),
        ],
        compiler_params=pltpu.CompilerParams(vmem_limit_bytes=9 * MIB),
        cost_estimate=SMALL,
    )(keep, came, came2)


def join(upper, lower):
    rows, slab = upper.shape

    def kernel(upper, lower, out, held, sems):
        moves = []
        for i, source in enumerate((upper, lower)):
            moves.append(pltpu.make_async_copy(source, held.at[i], sems.at[i, 0]))
            moves[-1].start()
        done = []
        for i in range(2):
            moves[i].wait()
            done.append(
                pltpu.make_async_copy(held.at[i], out.at[pl.ds(i * rows, rows)], sems.at[i, 1])
            )
            done[-1].start()
        for copy in done:
            copy.wait()

    anywhere = pl.BlockSpec(memory_space=pl.ANY)
    return pl.pallas_call(
        kernel,
        out_shape=jax.ShapeDtypeStruct((2 * rows, slab), upper.dtype),
        in_specs=[anywhere, anywhere],
        out_specs=anywhere,
        scratch_shapes=[
            pltpu.VMEM((2, rows, slab), upper.dtype),
            pltpu.SemaphoreType.DMA((2, 2)),
        ],
        compiler_params=pltpu.CompilerParams(vmem_limit_bytes=4 * MIB),
        cost_estimate=SMALL,
    )(upper, lower)


def round_sum(own, came, kind):
    def kernel(own, came, out):
        out[...] = (own[...] + came[...]).astype(kind)

    whole = pl.BlockSpec(memory_space=pltpu.VMEM)
    return pl.pallas_call(
        kernel,
        out_shape=jax.ShapeDtypeStruct(own.shape, kind),
        in_specs=[whole, whole],
        out_specs=whole,
        compiler_params=pltpu.CompilerParams(vmem_limit_bytes=4 * MIB),
        cost_estimate=SMALL,
    )(own, came)


def finish_grad(own, came, bits):
    share, slab = own.shape

    def kernel(own, *refs):
        bits, table, out = refs[-3:]
        total = own[...]
        for ref in refs[:-3]:
            total = total + ref[...].astype(jnp.float32)
        total = total * (2 * bits[...] - 1).astype(jnp.float32)
        result = None
        for _ in range(3):
            part = total.astype(jnp.bfloat16)
            total = total - part.astype(jnp.float32)
            term = jnp.dot(part, table[...], preferred_element_type=jnp.float32)
            result = term if result is None else result + term
        out[...] = result * (1.0 / math.sqrt(128.0))

    table = np.kron(np.eye(slab // 128), sylvester())
    whole = pl.BlockSpec(memory_space=pltpu.VMEM)
    return pl.pallas_call(
        kernel,
        out_shape=jax.ShapeDtypeStruct((share, slab), jnp.float32),
        in_specs=[whole] * (3 + len(came)),
        out_specs=whole,
        compiler_params=pltpu.CompilerParams(vmem_limit_bytes=12 * MIB),
        cost_estimate=LONGER,
    )(own, *came, bits, jnp.asarray(table, jnp.bfloat16))


def output_part(position, tokens, fars, pieces, before, part, cost):
    depth = tokens.shape[0]
    slab = pieces[0][0].shape[1]
    places = len(fars)
    count = len(pieces)
    lead = part // 128 * 128
    width = fars[0].shape[1] - lead
    edge = width - part

    def kernel(tok, *refs):
        windows = refs[:places]
        parts = refs[places : places + count]
        refs = refs[places + count :]
        if before is not None:
            old = refs[:2]
            refs = refs[2:]
        own, other, left, right, held, sems, piece_sems, old_sems, out_sems = refs
        earlier = []
        if before is not None:
            earlier = tile_copies(old, [held.at[0], held.at[1]], old_sems)
            start_all(earlier)
        waits = []
        for i, (_, first, step, other_side) in enumerate(pieces):
            start, place, column, row = position(step, other_side)
            near = pltpu.make_async_copy(
                tok.at[:, pl.ds(pl.multiple_of(start, 128), width)],
                left.at[i, pl.ds(0, depth)],
                sems.at[i, 0],
            )
            near.start()
            cols = pl.ds(pl.multiple_of(column, 128), width)
            copies = [
                pltpu.make_async_copy(
                    window.at[:, cols], left.at[i, pl.ds(depth, depth)], sems.at[i, 1]
                )
                for window in windows
            ]
            for k in range(places):
                pl.when(place == k)(copies[k].start)
            right[i, 0:edge, :] = jnp.zeros((edge, slab), jnp.bfloat16)
            right[i, width - edge : width, :] = jnp.zeros((edge, slab), jnp.bfloat16)
            piece = pltpu.make_async_copy(
                parts[i].at[pl.ds(first, part)],
                right.at[i, pl.ds(pl.multiple_of(row, 16), part)],
                piece_sems.at[i],
            )
            piece.start()
            waits.append([near, copies[0], piece])
        total = None
        for i in range(count):
            wait_all(waits[i])
            term = jnp.dot(left[i], right[i], preferred_element_type=jnp.float32)
            total = term if total is None else total + term
        wait_all(earlier)
        done = []
        for k, out in ((1, other), (0, own)):
            value = total[k * depth : (k + 1) * depth]
            held[k] = value if before is None else value + held[k]
            done.append(pltpu.make_async_copy(held.at[k], out, out_sems.at[k]))
            done[-1].start()
        wait_all(done)

    anywhere = pl.BlockSpec(memory_space=pl.ANY)
    shape = jax.ShapeDtypeStruct((depth, slab), jnp.float32)
    olds = () if before is None else tuple(before)
    return pl.pallas_call(
        kernel,
        out_shape=[shape, shape],
        in_specs=[anywhere] * (1 + places + count + len(olds)),
        out_specs=[anywhere, anywhere],
        scratch_shapes=[
            pltpu.VMEM((count, 2 * depth, width), jnp.bfloat16),
            pltpu.VMEM((count, width, slab), jnp.bfloat16),
            pltpu.VMEM((2, depth, slab), jnp.float32),
            pltpu.SemaphoreType.DMA((count, 2)),
            pltpu.SemaphoreType.DMA((count,)),
            pltpu.SemaphoreType.DMA((2,)),
            pltpu.SemaphoreType.DMA((2,)),
        ],
        compiler_params=pltpu.CompilerParams(vmem_limit_bytes=MEMORY),
        cost_estimate=cost,
    )(tokens, *fars, *[array for array, *_ in pieces], *olds)


def paired(mesh):
    n_outer = mesh.shape["outer"]
    n_node = mesh.shape["node"]
    orders = [[1, 2], [2, 1]]

    def core_swap(value):
        return lax.ppermute(value, "outer", [(o, o ^ 1) for o in range(n_outer)])

    def outer_swap(value, stage):
        return lax.ppermute(
            value, "outer", [(o, o ^ (1 << orders[o % 2][stage])) for o in range(n_outer)]
        )

    def node_shift(value, step):
        return lax.ppermute(value, "node", [(n, (n + step) % n_node) for n in range(n_node)])

    def place_of(o):
        bits = o >> 1
        return jnp.where(o % 2 == 0, bits, (bits >> 1) + 2 * (bits % 2))

    def on_device(tokens, cotangent, weight_codes, weight_scales, weight_bits, grad_bits):
        o = lax.axis_index("outer")
        width = tokens.shape[1]
        rows = width // n_outer
        share = rows // n_node
        node_rows = weight_codes.shape[0]
        window = (rows + 127) // 128 * 128
        edge = window - rows
        masks = (3, 1, 2, 0)

        def column(mask, o, mine):
            base = o if mine else o ^ 1
            which = base ^ jnp.where(
                base % 2 == 0, relative_of(orders, 0, mask), relative_of(orders, 1, mask)
            )
            return which // 2 * node_rows + which % 2 * (node_rows - window)

        def take(source, mask):
            return lax.dynamic_slice_in_dim(source, column(mask, o, False), window, 1)

        cot_far = core_swap(cotangent)
        leave = take(after(tokens, cotangent), 3)
        source = after(tokens, leave)
        far3 = core_swap(leave)
        fars = [far3] + [core_swap(take(source, mask)) for mask in masks[1:]]

        def columns(*masks):
            return lambda: [column(mask, lax.axis_index("outer"), True) for mask in masks]

        (first,) = grad_blocks(
            columns(3), tokens, fars[:1], cotangent, cot_far, [jnp.bfloat16], LONG
        )
        came3 = outer_swap(first, 0)

        part = rows // 2

        def side_of(o):
            return jnp.where(o % 2 == 0, o >> 1, o >> 2) % 2

        start = o % 2 * rows + side_of(o) * part
        held = rotate(
            dequantize(
                lax.dynamic_slice_in_dim(after(weight_codes, first), start, part),
                lax.dynamic_slice_in_dim(after(weight_scales, first), start, part),
            ),
            after(weight_bits, first),
        ).astype(jnp.bfloat16)
        swap0 = outer_swap(held, 0)
        ahead = node_shift(held, 1)

        def position():
            return lax.axis_index("outer") % 2 * edge, lax.axis_index("node")

        def out_position(step, other_side):
            o = lax.axis_index("outer")
            n = lax.axis_index("node")
            core = o % 2
            node = lax.rem(n + n_node - step, n_node)
            side = side_of(o) if other_side == 0 else 1 - side_of(o)
            bits = place_of((node * 2 + core) ^ (o - core))
            place = jnp.where(bits == 3, 0, jnp.where(bits == 1, 1, jnp.where(bits == 2, 2, 3)))
            lead = part // 128 * 128
            start = node * node_rows + core * (node_rows - window) + side * lead
            return start, place, side * lead, core * edge + side * (part - lead)

        def product(pieces, before, later_than, cost):
            source = after(tokens, later_than)
            return output_part(out_position, source, fars, pieces, before, part, cost)

        second, keep2 = grad_blocks(
            columns(*masks[1:3]), after(tokens, held), fars[1:3], cotangent, cot_far,
            [jnp.bfloat16, jnp.float32], LONGER,
        )
        came1 = outer_swap(second, 0)
        passed = add_blocks(keep2, came3)
        came2 = outer_swap(passed, 1)
        behind = node_shift(after(held, passed), n_node - 1)
        early = product([(held, 0, 0, 0), (swap0, 0, 0, 1)], None, passed, LONGER)
        ahead, *early = lax.optimization_barrier((ahead, *early))
        relay = node_shift(ahead, 1)
        (keep0,) = grad_blocks(
            columns(masks[3]), after(tokens, *early), fars[3:], cotangent, cot_far,
            [jnp.float32], SMALL,
        )
        joined = join(after(ahead, keep0), behind)
        came2, joined, _ = lax.optimization_barrier((came2, joined, keep0))
        own, *sends = cut_shares(position, keep0, came1, came2, rows, share)
        arrived = [node_shift(sends[step - 1], step) for step in range(1, n_node)]
        grad_rotated = finish_grad(own, arrived, grad_bits.reshape(1, -1))

        swap13 = outer_swap(joined, 0)
        swap2 = outer_swap(after(relay, *sends), 0)
        sums = product(
            [(ahead, 0, 1, 0), (behind, 0, n_node - 1, 0), (relay, 0, 2, 0)],
            early, sends[0], LONG,
        )
        own_part, other_part = product(
            [(swap13, 0, 1, 1), (swap13, part, n_node - 1, 1), (swap2, 0, 2, 1)],
            sums, swap2, SMALL,
        )
        output = round_sum(own_part, core_swap(other_part), tokens.dtype)
        return output, grad_rotated

    return on_device


def general(mesh):
    n_outer = mesh.shape["outer"]
    n_node = mesh.shape["node"]
    n_bits = n_outer.bit_length() - 1
    orders = [list(range(1, n_bits)), [2, 1] + list(range(3, n_bits))]

    def outer_swap(value, stage):
        pairs = []
        for o in range(n_outer):
            pairs.append((o, o ^ (1 if stage is None else 1 << orders[o % 2][stage])))
        return lax.ppermute(value, "outer", pairs)

    def node_shift(value, step):
        return lax.ppermute(value, "node", [(n, (n + step) % n_node) for n in range(n_node)])

    def on_device(tokens, cotangent, weight_codes, weight_scales, weight_bits, grad_bits):
        o = lax.axis_index("outer")
        n = lax.axis_index("node")
        core = o % 2
        width = tokens.shape[1]
        slab = cotangent.shape[1]

        part = weight_codes.shape[0] // 4
        side = jnp.where(core == 0, (o >> orders[0][0]) % 2, (o >> orders[1][0]) % 2)
        mate_side = jnp.where(core == 0, (o >> orders[1][0]) % 2, (o >> orders[0][0]) % 2)
        quarter = core * 2 + side
        start = quarter * part
        held = rotate(
            dequantize(
                lax.dynamic_slice_in_dim(weight_codes, start, part),
                lax.dynamic_slice_in_dim(weight_scales, start, part),
            ),
            weight_bits,
        ).astype(jnp.bfloat16)

        total = lax.dot_general(
            tokens, cotangent, (((0,), (0,)), ((), ())), preferred_element_type=jnp.float32
        ).astype(jnp.bfloat16)
        rows = width // n_outer
        blocks = {}

        def own(d):
            return lax.dynamic_slice_in_dim(total, (o ^ d) * rows, rows)

        def relative(mask):
            found = [0, 0]
            for c in range(2):
                for j, bit in enumerate(orders[c]):
                    if mask >> j & 1:
                        found[c] |= 1 << bit
            return jnp.where(core == 0, found[0], found[1])

        n_rest = n_bits - 1
        sums = {}
        for mask in reversed(range(2**n_rest)):
            partner = jnp.where(core == 0, relative_of(orders, 1, mask), relative_of(orders, 0, mask))
            came = outer_swap(own(partner ^ 1), None)
            sums[mask] = own(relative(mask)).astype(jnp.float32) + came.astype(jnp.float32)
        for stage in range(n_rest):
            low = 1 << stage
            for mask in sorted([m for m in sums if m & low], reverse=True):
                came = outer_swap(sums.pop(mask).astype(jnp.bfloat16), stage)
                sums[mask ^ low] = sums[mask ^ low] + came.astype(jnp.float32)
        mine = sums[0]
        share = rows // n_node
        send = mine.astype(jnp.bfloat16)
        grad = lax.dynamic_slice_in_dim(mine, n * share, share)
        for step in range(1, n_node):
            piece = lax.dynamic_slice_in_dim(send, (n + step) % n_node * share, share)
            grad = grad + node_shift(piece, step).astype(jnp.float32)
        grad_rotated = rotate(grad, grad_bits)

        weight = jnp.zeros((width, slab), jnp.bfloat16)
        node_rows = weight_codes.shape[0]
        for step in range(n_node):
            base = (n - step) % n_node * node_rows
            across = outer_swap(held, 0)
            mate = outer_swap(held, None)
            mate_across = outer_swap(across, None)
            pieces = [
                (held, core * 2 + side),
                (across, core * 2 + 1 - side),
                (mate, (1 - core) * 2 + mate_side),
                (mate_across, (1 - core) * 2 + 1 - mate_side),
            ]
            for value, place in pieces:
                weight = lax.dynamic_update_slice_in_dim(weight, value, base + place * part, 0)
            if step < n_node - 1:
                held = node_shift(held, 1)
        output = jnp.dot(tokens, weight, preferred_element_type=jnp.float32).astype(jnp.bfloat16)
        return output, grad_rotated

    return on_device


def solution(mesh):
    n_outer = mesh.shape["outer"]
    n_node = mesh.shape["node"]
    on_device = paired(mesh) if n_outer == 8 and n_node == 4 else general(mesh)
    return jax.shard_map(
        on_device,
        mesh=mesh,
        in_specs=(
            P(("outer", "node"), None),
            P(("outer", "node"), None),
            P("node", None),
            P("node", None),
            P(),
            P(),
        ),
        out_specs=(P(("outer", "node"), None), P(("outer", "node"), None)),
        check_vma=False,
    )
```

```python
import math

import jax
import jax.numpy as jnp
import numpy as np
from jax import lax
from jax.experimental import pallas as pl
from jax.experimental.pallas import tpu as pltpu
from jax.sharding import PartitionSpec as P


def sylvester():
    row_index = np.arange(128).reshape(128, 1)
    column_index = np.arange(128).reshape(1, 128)
    parity = np.zeros((128, 128))
    for level in range(7):
        parity = parity + row_index // 2**level % 2 * (column_index // 2**level % 2)
    return 1.0 - 2.0 * (parity % 2)


def rotate(values, bits):
    width = values.shape[1]
    signs = (2 * bits - 1).astype(jnp.float32)
    table = np.kron(np.eye(width // 128), sylvester()) / math.sqrt(128.0)
    return jnp.dot(
        values * signs,
        jnp.asarray(table, jnp.float32),
        precision=lax.Precision.HIGHEST,
    )


def dequantize(codes, scales):
    height, width = codes.shape
    spread = jnp.concatenate(
        [
            jnp.broadcast_to(scales[:, block : block + 1], (height, 128))
            for block in range(width // 128)
        ],
        axis=1,
    )
    return codes.astype(jnp.float32) * spread


def relative_of(orders, core, mask):
    found = 0
    for j, bit in enumerate(orders[core]):
        if mask >> j & 1:
            found |= 1 << bit
    return found


SMALL = pl.CostEstimate(flops=0, bytes_accessed=1024, transcendentals=0)
LONG = pl.CostEstimate(flops=5 * 10**9, bytes_accessed=1024, transcendentals=0)
MIDDLE = pl.CostEstimate(flops=8 * 10**9, bytes_accessed=1024, transcendentals=0)
LONGER = pl.CostEstimate(flops=6 * 10**10, bytes_accessed=1024, transcendentals=0)
MIB = 2**20
MEMORY = 56 * MIB


def after(value, *deps):
    return lax.optimization_barrier((value, *deps))[0]


def tile_of(window):
    return max(128 * k for k in range(1, 6) if window % (128 * k) == 0)


def tile_copies(sources, dests, sems):
    return [
        pltpu.make_async_copy(source, dest, sems.at[i])
        for i, (source, dest) in enumerate(zip(sources, dests))
    ]


def start_all(copies):
    for copy in copies:
        copy.start()


def wait_all(copies):
    for copy in copies:
        copy.wait()


def grad_blocks(columns, tokens, fars, cot, cot_far, kinds, cost):
    count = len(fars)
    depth, slab = cot.shape
    window = fars[0].shape[1]
    tile = tile_of(window)
    tiles = window // tile

    def kernel(tok, cot, cot_far, *refs):
        far_refs, outs = refs[:count], refs[count : 2 * count]
        cots, left, sems, cot_sems, out_sems = refs[2 * count : 2 * count + 5]
        held = refs[2 * count + 5 :]
        first = columns()
        ends = tile_copies([cot, cot_far], [cots.at[0], cots.at[1]], cot_sems)
        start_all(ends)
        copies = {}
        for i in range(count):
            for j in range(tiles):
                near = tok.at[:, pl.ds(pl.multiple_of(first[i] + j * tile, 128), tile)]
                far = far_refs[i].at[:, pl.ds(j * tile, tile)]
                copies[i, j] = tile_copies(
                    [near, far], [left.at[i, j, 0], left.at[i, j, 1]], sems.at[i, j]
                )
                start_all(copies[i, j])
        wait_all(ends)
        mine, theirs = cots[0].T, cots[1].T
        done = []
        for i in range(count):
            for j in range(tiles):
                wait_all(copies[i, j])
                held[i][j] = (
                    jnp.dot(mine, left[i, j, 0], preferred_element_type=jnp.float32)
                    + jnp.dot(theirs, left[i, j, 1], preferred_element_type=jnp.float32)
                ).astype(kinds[i])
                done.append(
                    pltpu.make_async_copy(
                        held[i].at[j], outs[i].at[:, pl.ds(j * tile, tile)], out_sems.at[i, j]
                    )
                )
                done[-1].start()
        wait_all(done)

    anywhere = pl.BlockSpec(memory_space=pl.ANY)
    return pl.pallas_call(
        kernel,
        out_shape=[jax.ShapeDtypeStruct((slab, window), kind) for kind in kinds],
        in_specs=[anywhere] * (3 + count),
        out_specs=[anywhere] * count,
        scratch_shapes=[
            pltpu.VMEM((2, depth, slab), jnp.bfloat16),
            pltpu.VMEM((count, tiles, 2, depth, tile), jnp.bfloat16),
            pltpu.SemaphoreType.DMA((count, tiles, 2)),
            pltpu.SemaphoreType.DMA((2,)),
            pltpu.SemaphoreType.DMA((count, tiles)),
        ]
        + [pltpu.VMEM((tiles, slab, tile), kind) for kind in kinds],
        compiler_params=pltpu.CompilerParams(vmem_limit_bytes=MEMORY),
        cost_estimate=cost,
    )(tokens, cot, cot_far, *fars)


def add_blocks(keep, came):
    slab, window = keep.shape
    tile = tile_of(window)
    tiles = window // tile

    def kernel(keep, came, out, left, right, held, sems, out_sems):
        copies = []
        for j in range(tiles):
            cols = pl.ds(j * tile, tile)
            copies.append(
                tile_copies(
                    [keep.at[:, cols], came.at[:, cols]], [left.at[j], right.at[j]], sems.at[j]
                )
            )
            start_all(copies[j])
        done = []
        for j in range(tiles):
            wait_all(copies[j])
            held[j] = (left[j] + right[j].astype(jnp.float32)).astype(jnp.bfloat16)
            done.append(
                pltpu.make_async_copy(held.at[j], out.at[:, pl.ds(j * tile, tile)], out_sems.at[j])
            )
            done[-1].start()
        wait_all(done)

    anywhere = pl.BlockSpec(memory_space=pl.ANY)
    return pl.pallas_call(
        kernel,
        out_shape=jax.ShapeDtypeStruct((slab, window), jnp.bfloat16),
        in_specs=[anywhere] * 2,
        out_specs=anywhere,
        scratch_shapes=[
            pltpu.VMEM((tiles, slab, tile), jnp.float32),
            pltpu.VMEM((tiles, slab, tile), jnp.bfloat16),
            pltpu.VMEM((tiles, slab, tile), jnp.bfloat16),
            pltpu.SemaphoreType.DMA((tiles, 2)),
            pltpu.SemaphoreType.DMA((tiles,)),
        ],
        compiler_params=pltpu.CompilerParams(vmem_limit_bytes=6 * MIB),
        cost_estimate=SMALL,
    )(keep, came)


def cut_shares(position, keep, came, came2, rows, share):
    slab, window = keep.shape
    tile = tile_of(window)
    tiles = window // tile
    n_share = rows // share

    def kernel(keep, came, came2, own, *refs):
        sends = refs[: n_share - 1]
        left, right, total, own_held, send_held, sems, out_sems = refs[n_share - 1 :]
        copies = []
        for j in range(tiles):
            cols = pl.ds(j * tile, tile)
            copies.append(
                tile_copies(
                    [keep.at[:, cols], came.at[:, cols], came2.at[:, cols]],
                    [left.at[j], right.at[j, 0], right.at[j, 1]],
                    sems.at[j],
                )
            )
            start_all(copies[j])
        for j in range(tiles):
            wait_all(copies[j])
            block = (
                left[j] + right[j, 0].astype(jnp.float32) + right[j, 1].astype(jnp.float32)
            )
            total[j * tile : (j + 1) * tile, :] = block.T
        skip, place = position()
        done = []
        for k in [*range(1, n_share), 0]:
            first = skip + lax.rem(place + k, n_share) * share
            value = total[pl.ds(pl.multiple_of(first, 16), share), :]
            if k == 0:
                own_held[...] = value
                copy = pltpu.make_async_copy(own_held, own, out_sems.at[0])
            else:
                send_held[k - 1] = value.astype(jnp.bfloat16)
                copy = pltpu.make_async_copy(send_held.at[k - 1], sends[k - 1], out_sems.at[k])
            copy.start()
            done.append(copy)
        wait_all(done)

    anywhere = pl.BlockSpec(memory_space=pl.ANY)
    return pl.pallas_call(
        kernel,
        out_shape=[jax.ShapeDtypeStruct((share, slab), jnp.float32)]
        + [jax.ShapeDtypeStruct((share, slab), jnp.bfloat16)] * (n_share - 1),
        in_specs=[anywhere] * 3,
        out_specs=[anywhere] * n_share,
        scratch_shapes=[
            pltpu.VMEM((tiles, slab, tile), jnp.float32),
            pltpu.VMEM((tiles, 2, slab, tile), jnp.bfloat16),
            pltpu.VMEM((window, slab), jnp.float32),
            pltpu.VMEM((share, slab), jnp.float32),
            pltpu.VMEM((n_share - 1, share, slab), jnp.bfloat16),
            pltpu.SemaphoreType.DMA((tiles, 3)),
            pltpu.SemaphoreType.DMA((n_share,)),
        ],
        compiler_params=pltpu.CompilerParams(vmem_limit_bytes=9 * MIB),
        cost_estimate=SMALL,
    )(keep, came, came2)


def join(pieces):
    count = len(pieces)
    rows, slab = pieces[0].shape

    def kernel(*refs):
        out, held, sems = refs[count:]
        moves = tile_copies(refs[:count], [held.at[i] for i in range(count)], sems.at[0])
        start_all(moves)
        done = []
        for i in range(count):
            moves[i].wait()
            done.append(
                pltpu.make_async_copy(held.at[i], out.at[pl.ds(i * rows, rows)], sems.at[1, i])
            )
            done[-1].start()
        wait_all(done)

    anywhere = pl.BlockSpec(memory_space=pl.ANY)
    return pl.pallas_call(
        kernel,
        out_shape=jax.ShapeDtypeStruct((count * rows, slab), pieces[0].dtype),
        in_specs=[anywhere] * count,
        out_specs=anywhere,
        scratch_shapes=[
            pltpu.VMEM((count, rows, slab), pieces[0].dtype),
            pltpu.SemaphoreType.DMA((2, count)),
        ],
        compiler_params=pltpu.CompilerParams(vmem_limit_bytes=4 * MIB),
        cost_estimate=SMALL,
    )(*pieces)


def round_sum(own, came, kind):
    def kernel(own, came, out):
        out[...] = (own[...] + came[...]).astype(kind)

    whole = pl.BlockSpec(memory_space=pltpu.VMEM)
    return pl.pallas_call(
        kernel,
        out_shape=jax.ShapeDtypeStruct(own.shape, kind),
        in_specs=[whole, whole],
        out_specs=whole,
        compiler_params=pltpu.CompilerParams(vmem_limit_bytes=4 * MIB),
        cost_estimate=SMALL,
    )(own, came)


def finish_grad(own, came, bits):
    share, slab = own.shape

    def kernel(own, *refs):
        bits, table, out = refs[-3:]
        total = own[...]
        for ref in refs[:-3]:
            total = total + ref[...].astype(jnp.float32)
        total = total * (2 * bits[...] - 1).astype(jnp.float32)
        result = None
        for _ in range(3):
            part = total.astype(jnp.bfloat16)
            total = total - part.astype(jnp.float32)
            term = jnp.dot(part, table[...], preferred_element_type=jnp.float32)
            result = term if result is None else result + term
        out[...] = result * (1.0 / math.sqrt(128.0))

    table = np.kron(np.eye(slab // 128), sylvester())
    whole = pl.BlockSpec(memory_space=pltpu.VMEM)
    return pl.pallas_call(
        kernel,
        out_shape=jax.ShapeDtypeStruct((share, slab), jnp.float32),
        in_specs=[whole] * (3 + len(came)),
        out_specs=whole,
        compiler_params=pltpu.CompilerParams(vmem_limit_bytes=12 * MIB),
        cost_estimate=LONGER,
    )(own, *came, bits, jnp.asarray(table, jnp.bfloat16))


def output_part(position, tokens, fars, pieces, before, part, cost):
    depth = tokens.shape[0]
    slab = pieces[0][0].shape[1]
    places = len(fars)
    count = len(pieces)
    lead = part // 128 * 128
    width = fars[0].shape[1] - lead
    edge = width - part

    def kernel(tok, *refs):
        windows = refs[:places]
        parts = refs[places : places + count]
        refs = refs[places + count :]
        if before is not None:
            old = refs[:2]
            refs = refs[2:]
        own, other, left, right, held, sems, piece_sems, old_sems, out_sems = refs
        earlier = []
        if before is not None:
            earlier = tile_copies(old, [held.at[0], held.at[1]], old_sems)
            start_all(earlier)
        waits = []
        for i, (_, first, step, other_side) in enumerate(pieces):
            start, place, column, row = position(step, other_side)
            near = pltpu.make_async_copy(
                tok.at[:, pl.ds(pl.multiple_of(start, 128), width)],
                left.at[i, pl.ds(0, depth)],
                sems.at[i, 0],
            )
            near.start()
            cols = pl.ds(pl.multiple_of(column, 128), width)
            copies = [
                pltpu.make_async_copy(
                    window.at[:, cols], left.at[i, pl.ds(depth, depth)], sems.at[i, 1]
                )
                for window in windows
            ]
            for k in range(places):
                pl.when(place == k)(copies[k].start)
            right[i, 0:edge, :] = jnp.zeros((edge, slab), jnp.bfloat16)
            right[i, width - edge : width, :] = jnp.zeros((edge, slab), jnp.bfloat16)
            piece = pltpu.make_async_copy(
                parts[i].at[pl.ds(first, part)],
                right.at[i, pl.ds(pl.multiple_of(row, 16), part)],
                piece_sems.at[i],
            )
            piece.start()
            waits.append([near, copies[0], piece])
        total = None
        for i in range(count):
            wait_all(waits[i])
            term = jnp.dot(left[i], right[i], preferred_element_type=jnp.float32)
            total = term if total is None else total + term
        wait_all(earlier)
        done = []
        for k, out in ((1, other), (0, own)):
            value = total[k * depth : (k + 1) * depth]
            held[k] = value if before is None else value + held[k]
            done.append(pltpu.make_async_copy(held.at[k], out, out_sems.at[k]))
            done[-1].start()
        wait_all(done)

    anywhere = pl.BlockSpec(memory_space=pl.ANY)
    shape = jax.ShapeDtypeStruct((depth, slab), jnp.float32)
    olds = () if before is None else tuple(before)
    return pl.pallas_call(
        kernel,
        out_shape=[shape, shape],
        in_specs=[anywhere] * (1 + places + count + len(olds)),
        out_specs=[anywhere, anywhere],
        scratch_shapes=[
            pltpu.VMEM((count, 2 * depth, width), jnp.bfloat16),
            pltpu.VMEM((count, width, slab), jnp.bfloat16),
            pltpu.VMEM((2, depth, slab), jnp.float32),
            pltpu.SemaphoreType.DMA((count, 2)),
            pltpu.SemaphoreType.DMA((count,)),
            pltpu.SemaphoreType.DMA((2,)),
            pltpu.SemaphoreType.DMA((2,)),
        ],
        compiler_params=pltpu.CompilerParams(vmem_limit_bytes=MEMORY),
        cost_estimate=cost,
    )(tokens, *fars, *[array for array, *_ in pieces], *olds)


def paired(mesh):
    n_outer = mesh.shape["outer"]
    n_node = mesh.shape["node"]
    orders = [[1, 2], [2, 1]]

    def core_swap(value):
        return lax.ppermute(value, "outer", [(o, o ^ 1) for o in range(n_outer)])

    def outer_swap(value, stage):
        return lax.ppermute(
            value, "outer", [(o, o ^ (1 << orders[o % 2][stage])) for o in range(n_outer)]
        )

    def node_shift(value, step):
        return lax.ppermute(value, "node", [(n, (n + step) % n_node) for n in range(n_node)])

    def place_of(o):
        bits = o >> 1
        return jnp.where(o % 2 == 0, bits, (bits >> 1) + 2 * (bits % 2))

    def on_device(tokens, cotangent, weight_codes, weight_scales, weight_bits, grad_bits):
        o = lax.axis_index("outer")
        width = tokens.shape[1]
        rows = width // n_outer
        share = rows // n_node
        node_rows = weight_codes.shape[0]
        window = (rows + 127) // 128 * 128
        edge = window - rows
        masks = (3, 1, 2, 0)

        def column(mask, o, mine):
            base = o if mine else o ^ 1
            which = base ^ jnp.where(
                base % 2 == 0, relative_of(orders, 0, mask), relative_of(orders, 1, mask)
            )
            return which // 2 * node_rows + which % 2 * (node_rows - window)

        def take(source, mask):
            return lax.dynamic_slice_in_dim(source, column(mask, o, False), window, 1)

        cot_far = core_swap(cotangent)
        leave = take(after(tokens, cotangent), 3)
        source = after(tokens, leave)
        far3 = core_swap(leave)
        fars = [far3] + [core_swap(take(source, mask)) for mask in masks[1:]]

        def columns(*masks):
            return lambda: [column(mask, lax.axis_index("outer"), True) for mask in masks]

        (first,) = grad_blocks(
            columns(3), tokens, fars[:1], cotangent, cot_far, [jnp.bfloat16], LONG
        )
        came3 = outer_swap(first, 0)

        part = rows // 2

        def side_of(o):
            return jnp.where(o % 2 == 0, o >> 1, o >> 2) % 2

        start = o % 2 * rows + side_of(o) * part
        held = rotate(
            dequantize(
                lax.dynamic_slice_in_dim(after(weight_codes, first), start, part),
                lax.dynamic_slice_in_dim(after(weight_scales, first), start, part),
            ),
            after(weight_bits, first),
        ).astype(jnp.bfloat16)
        ahead = node_shift(held, 1)

        def position():
            return lax.axis_index("outer") % 2 * edge, lax.axis_index("node")

        def out_position(step, other_side):
            o = lax.axis_index("outer")
            n = lax.axis_index("node")
            core = o % 2
            node = lax.rem(n + n_node - step, n_node)
            side = side_of(o) if other_side == 0 else 1 - side_of(o)
            bits = place_of((node * 2 + core) ^ (o - core))
            place = jnp.where(bits == 3, 0, jnp.where(bits == 1, 1, jnp.where(bits == 2, 2, 3)))
            lead = part // 128 * 128
            start = node * node_rows + core * (node_rows - window) + side * lead
            return start, place, side * lead, core * edge + side * (part - lead)

        def product(pieces, before, later_than, cost):
            source = after(tokens, later_than)
            return output_part(out_position, source, fars, pieces, before, part, cost)

        second, keep2 = grad_blocks(
            columns(*masks[1:3]), after(tokens, held), fars[1:3], cotangent, cot_far,
            [jnp.bfloat16, jnp.float32], LONGER,
        )
        came1 = outer_swap(second, 0)
        passed = add_blocks(keep2, came3)
        came2 = outer_swap(passed, 1)
        behind = node_shift(after(held, passed), n_node - 1)
        early = product([(held, 0, 0, 0)], None, passed, LONGER)
        ahead, *early = lax.optimization_barrier((ahead, *early))
        relay = node_shift(ahead, 1)
        (keep0,) = grad_blocks(
            columns(masks[3]), after(tokens, *early), fars[3:], cotangent, cot_far,
            [jnp.float32], SMALL,
        )
        joined = join([held, ahead, behind])
        came2, joined, _ = lax.optimization_barrier((came2, joined, keep0))
        own, *sends = cut_shares(position, keep0, came1, came2, rows, share)
        arrived = [node_shift(sends[step - 1], step) for step in range(1, n_node)]
        grad_rotated = finish_grad(own, arrived, grad_bits.reshape(1, -1))

        swap013 = outer_swap(joined, 0)
        swap2 = outer_swap(after(relay, *sends), 0)
        sums = product(
            [(ahead, 0, 1, 0), (behind, 0, n_node - 1, 0), (relay, 0, 2, 0)],
            early, sends[0], MIDDLE,
        )
        sums = product([(swap2, 0, 2, 1)], sums, swap2, LONG)
        own_part, other_part = product(
            [(swap013, 0, 0, 1), (swap013, part, 1, 1), (swap013, 2 * part, n_node - 1, 1)],
            sums, swap013, SMALL,
        )
        output = round_sum(own_part, core_swap(other_part), tokens.dtype)
        return output, grad_rotated

    return on_device


def general(mesh):
    n_outer = mesh.shape["outer"]
    n_node = mesh.shape["node"]
    n_bits = n_outer.bit_length() - 1
    orders = [list(range(1, n_bits)), [2, 1] + list(range(3, n_bits))]

    def outer_swap(value, stage):
        pairs = []
        for o in range(n_outer):
            pairs.append((o, o ^ (1 if stage is None else 1 << orders[o % 2][stage])))
        return lax.ppermute(value, "outer", pairs)

    def node_shift(value, step):
        return lax.ppermute(value, "node", [(n, (n + step) % n_node) for n in range(n_node)])

    def on_device(tokens, cotangent, weight_codes, weight_scales, weight_bits, grad_bits):
        o = lax.axis_index("outer")
        n = lax.axis_index("node")
        core = o % 2
        width = tokens.shape[1]
        slab = cotangent.shape[1]

        part = weight_codes.shape[0] // 4
        side = jnp.where(core == 0, (o >> orders[0][0]) % 2, (o >> orders[1][0]) % 2)
        mate_side = jnp.where(core == 0, (o >> orders[1][0]) % 2, (o >> orders[0][0]) % 2)
        quarter = core * 2 + side
        start = quarter * part
        held = rotate(
            dequantize(
                lax.dynamic_slice_in_dim(weight_codes, start, part),
                lax.dynamic_slice_in_dim(weight_scales, start, part),
            ),
            weight_bits,
        ).astype(jnp.bfloat16)

        total = lax.dot_general(
            tokens, cotangent, (((0,), (0,)), ((), ())), preferred_element_type=jnp.float32
        ).astype(jnp.bfloat16)
        rows = width // n_outer
        blocks = {}

        def own(d):
            return lax.dynamic_slice_in_dim(total, (o ^ d) * rows, rows)

        def relative(mask):
            found = [0, 0]
            for c in range(2):
                for j, bit in enumerate(orders[c]):
                    if mask >> j & 1:
                        found[c] |= 1 << bit
            return jnp.where(core == 0, found[0], found[1])

        n_rest = n_bits - 1
        sums = {}
        for mask in reversed(range(2**n_rest)):
            partner = jnp.where(core == 0, relative_of(orders, 1, mask), relative_of(orders, 0, mask))
            came = outer_swap(own(partner ^ 1), None)
            sums[mask] = own(relative(mask)).astype(jnp.float32) + came.astype(jnp.float32)
        for stage in range(n_rest):
            low = 1 << stage
            for mask in sorted([m for m in sums if m & low], reverse=True):
                came = outer_swap(sums.pop(mask).astype(jnp.bfloat16), stage)
                sums[mask ^ low] = sums[mask ^ low] + came.astype(jnp.float32)
        mine = sums[0]
        share = rows // n_node
        send = mine.astype(jnp.bfloat16)
        grad = lax.dynamic_slice_in_dim(mine, n * share, share)
        for step in range(1, n_node):
            piece = lax.dynamic_slice_in_dim(send, (n + step) % n_node * share, share)
            grad = grad + node_shift(piece, step).astype(jnp.float32)
        grad_rotated = rotate(grad, grad_bits)

        weight = jnp.zeros((width, slab), jnp.bfloat16)
        node_rows = weight_codes.shape[0]
        for step in range(n_node):
            base = (n - step) % n_node * node_rows
            across = outer_swap(held, 0)
            mate = outer_swap(held, None)
            mate_across = outer_swap(across, None)
            pieces = [
                (held, core * 2 + side),
                (across, core * 2 + 1 - side),
                (mate, (1 - core) * 2 + mate_side),
                (mate_across, (1 - core) * 2 + 1 - mate_side),
            ]
            for value, place in pieces:
                weight = lax.dynamic_update_slice_in_dim(weight, value, base + place * part, 0)
            if step < n_node - 1:
                held = node_shift(held, 1)
        output = jnp.dot(tokens, weight, preferred_element_type=jnp.float32).astype(jnp.bfloat16)
        return output, grad_rotated

    return on_device


def solution(mesh):
    n_outer = mesh.shape["outer"]
    n_node = mesh.shape["node"]
    on_device = paired(mesh) if n_outer == 8 and n_node == 4 else general(mesh)
    return jax.shard_map(
        on_device,
        mesh=mesh,
        in_specs=(
            P(("outer", "node"), None),
            P(("outer", "node"), None),
            P("node", None),
            P("node", None),
            P(),
            P(),
        ),
        out_specs=(P(("outer", "node"), None), P(("outer", "node"), None)),
        check_vma=False,
    )
```

```python
import math

import jax
import jax.numpy as jnp
import numpy as np
from jax import lax
from jax.experimental import pallas as pl
from jax.experimental.pallas import tpu as pltpu
from jax.sharding import PartitionSpec as P


def sylvester():
    row_index = np.arange(128).reshape(128, 1)
    column_index = np.arange(128).reshape(1, 128)
    parity = np.zeros((128, 128))
    for level in range(7):
        parity = parity + row_index // 2**level % 2 * (column_index // 2**level % 2)
    return 1.0 - 2.0 * (parity % 2)


def rotate(values, bits):
    width = values.shape[1]
    signs = (2 * bits - 1).astype(jnp.float32)
    table = np.kron(np.eye(width // 128), sylvester()) / math.sqrt(128.0)
    return jnp.dot(
        values * signs,
        jnp.asarray(table, jnp.float32),
        precision=lax.Precision.HIGHEST,
    )


def dequantize(codes, scales):
    height, width = codes.shape
    spread = jnp.concatenate(
        [
            jnp.broadcast_to(scales[:, block : block + 1], (height, 128))
            for block in range(width // 128)
        ],
        axis=1,
    )
    return codes.astype(jnp.float32) * spread


def relative_of(orders, core, mask):
    found = 0
    for j, bit in enumerate(orders[core]):
        if mask >> j & 1:
            found |= 1 << bit
    return found


SMALL = pl.CostEstimate(flops=0, bytes_accessed=1024, transcendentals=0)
LONG = pl.CostEstimate(flops=5 * 10**9, bytes_accessed=1024, transcendentals=0)
MIDDLE = pl.CostEstimate(flops=13 * 10**9, bytes_accessed=1024, transcendentals=0)
LONGER = pl.CostEstimate(flops=6 * 10**10, bytes_accessed=1024, transcendentals=0)
MIB = 2**20
MEMORY = 56 * MIB


def after(value, *deps):
    return lax.optimization_barrier((value, *deps))[0]


def tile_of(window):
    return max(128 * k for k in range(1, 6) if window % (128 * k) == 0)


def tile_copies(sources, dests, sems):
    return [
        pltpu.make_async_copy(source, dest, sems.at[i])
        for i, (source, dest) in enumerate(zip(sources, dests))
    ]


def start_all(copies):
    for copy in copies:
        copy.start()


def wait_all(copies):
    for copy in copies:
        copy.wait()


def grad_blocks(columns, tokens, fars, cot, cot_far, kinds, cost):
    count = len(fars)
    depth, slab = cot.shape
    window = fars[0].shape[1]
    tile = tile_of(window)
    tiles = window // tile

    def kernel(tok, cot, cot_far, *refs):
        far_refs, outs = refs[:count], refs[count : 2 * count]
        cots, left, sems, cot_sems, out_sems = refs[2 * count : 2 * count + 5]
        held = refs[2 * count + 5 :]
        first = columns()
        ends = tile_copies([cot, cot_far], [cots.at[0], cots.at[1]], cot_sems)
        start_all(ends)
        copies = {}
        for i in range(count):
            for j in range(tiles):
                near = tok.at[:, pl.ds(pl.multiple_of(first[i] + j * tile, 128), tile)]
                far = far_refs[i].at[:, pl.ds(j * tile, tile)]
                copies[i, j] = tile_copies(
                    [near, far], [left.at[i, j, 0], left.at[i, j, 1]], sems.at[i, j]
                )
                start_all(copies[i, j])
        wait_all(ends)
        mine, theirs = cots[0].T, cots[1].T
        done = []
        for i in range(count):
            for j in range(tiles):
                wait_all(copies[i, j])
                held[i][j] = (
                    jnp.dot(mine, left[i, j, 0], preferred_element_type=jnp.float32)
                    + jnp.dot(theirs, left[i, j, 1], preferred_element_type=jnp.float32)
                ).astype(kinds[i])
                done.append(
                    pltpu.make_async_copy(
                        held[i].at[j], outs[i].at[:, pl.ds(j * tile, tile)], out_sems.at[i, j]
                    )
                )
                done[-1].start()
        wait_all(done)

    anywhere = pl.BlockSpec(memory_space=pl.ANY)
    return pl.pallas_call(
        kernel,
        out_shape=[jax.ShapeDtypeStruct((slab, window), kind) for kind in kinds],
        in_specs=[anywhere] * (3 + count),
        out_specs=[anywhere] * count,
        scratch_shapes=[
            pltpu.VMEM((2, depth, slab), jnp.bfloat16),
            pltpu.VMEM((count, tiles, 2, depth, tile), jnp.bfloat16),
            pltpu.SemaphoreType.DMA((count, tiles, 2)),
            pltpu.SemaphoreType.DMA((2,)),
            pltpu.SemaphoreType.DMA((count, tiles)),
        ]
        + [pltpu.VMEM((tiles, slab, tile), kind) for kind in kinds],
        compiler_params=pltpu.CompilerParams(vmem_limit_bytes=MEMORY),
        cost_estimate=cost,
    )(tokens, cot, cot_far, *fars)


def add_blocks(keep, came):
    slab, window = keep.shape
    tile = tile_of(window)
    tiles = window // tile

    def kernel(keep, came, out, left, right, held, sems, out_sems):
        copies = []
        for j in range(tiles):
            cols = pl.ds(j * tile, tile)
            copies.append(
                tile_copies(
                    [keep.at[:, cols], came.at[:, cols]], [left.at[j], right.at[j]], sems.at[j]
                )
            )
            start_all(copies[j])
        done = []
        for j in range(tiles):
            wait_all(copies[j])
            held[j] = (left[j] + right[j].astype(jnp.float32)).astype(jnp.bfloat16)
            done.append(
                pltpu.make_async_copy(held.at[j], out.at[:, pl.ds(j * tile, tile)], out_sems.at[j])
            )
            done[-1].start()
        wait_all(done)

    anywhere = pl.BlockSpec(memory_space=pl.ANY)
    return pl.pallas_call(
        kernel,
        out_shape=jax.ShapeDtypeStruct((slab, window), jnp.bfloat16),
        in_specs=[anywhere] * 2,
        out_specs=anywhere,
        scratch_shapes=[
            pltpu.VMEM((tiles, slab, tile), jnp.float32),
            pltpu.VMEM((tiles, slab, tile), jnp.bfloat16),
            pltpu.VMEM((tiles, slab, tile), jnp.bfloat16),
            pltpu.SemaphoreType.DMA((tiles, 2)),
            pltpu.SemaphoreType.DMA((tiles,)),
        ],
        compiler_params=pltpu.CompilerParams(vmem_limit_bytes=6 * MIB),
        cost_estimate=SMALL,
    )(keep, came)


def cut_shares(position, keep, came, came2, rows, share):
    slab, window = keep.shape
    tile = tile_of(window)
    tiles = window // tile
    n_share = rows // share

    def kernel(keep, came, came2, own, *refs):
        sends = refs[: n_share - 1]
        left, right, total, own_held, send_held, sems, out_sems = refs[n_share - 1 :]
        copies = []
        for j in range(tiles):
            cols = pl.ds(j * tile, tile)
            copies.append(
                tile_copies(
                    [keep.at[:, cols], came.at[:, cols], came2.at[:, cols]],
                    [left.at[j], right.at[j, 0], right.at[j, 1]],
                    sems.at[j],
                )
            )
            start_all(copies[j])
        for j in range(tiles):
            wait_all(copies[j])
            block = (
                left[j] + right[j, 0].astype(jnp.float32) + right[j, 1].astype(jnp.float32)
            )
            total[j * tile : (j + 1) * tile, :] = block.T
        skip, place = position()
        done = []
        for k in [*range(1, n_share), 0]:
            first = skip + lax.rem(place + k, n_share) * share
            value = total[pl.ds(pl.multiple_of(first, 16), share), :]
            if k == 0:
                own_held[...] = value
                copy = pltpu.make_async_copy(own_held, own, out_sems.at[0])
            else:
                send_held[k - 1] = value.astype(jnp.bfloat16)
                copy = pltpu.make_async_copy(send_held.at[k - 1], sends[k - 1], out_sems.at[k])
            copy.start()
            done.append(copy)
        wait_all(done)

    anywhere = pl.BlockSpec(memory_space=pl.ANY)
    return pl.pallas_call(
        kernel,
        out_shape=[jax.ShapeDtypeStruct((share, slab), jnp.float32)]
        + [jax.ShapeDtypeStruct((share, slab), jnp.bfloat16)] * (n_share - 1),
        in_specs=[anywhere] * 3,
        out_specs=[anywhere] * n_share,
        scratch_shapes=[
            pltpu.VMEM((tiles, slab, tile), jnp.float32),
            pltpu.VMEM((tiles, 2, slab, tile), jnp.bfloat16),
            pltpu.VMEM((window, slab), jnp.float32),
            pltpu.VMEM((share, slab), jnp.float32),
            pltpu.VMEM((n_share - 1, share, slab), jnp.bfloat16),
            pltpu.SemaphoreType.DMA((tiles, 3)),
            pltpu.SemaphoreType.DMA((n_share,)),
        ],
        compiler_params=pltpu.CompilerParams(vmem_limit_bytes=9 * MIB),
        cost_estimate=SMALL,
    )(keep, came, came2)


def join(pieces):
    count = len(pieces)
    rows, slab = pieces[0].shape

    def kernel(*refs):
        out, held, sems = refs[count:]
        moves = tile_copies(refs[:count], [held.at[i] for i in range(count)], sems.at[0])
        start_all(moves)
        done = []
        for i in range(count):
            moves[i].wait()
            done.append(
                pltpu.make_async_copy(held.at[i], out.at[pl.ds(i * rows, rows)], sems.at[1, i])
            )
            done[-1].start()
        wait_all(done)

    anywhere = pl.BlockSpec(memory_space=pl.ANY)
    return pl.pallas_call(
        kernel,
        out_shape=jax.ShapeDtypeStruct((count * rows, slab), pieces[0].dtype),
        in_specs=[anywhere] * count,
        out_specs=anywhere,
        scratch_shapes=[
            pltpu.VMEM((count, rows, slab), pieces[0].dtype),
            pltpu.SemaphoreType.DMA((2, count)),
        ],
        compiler_params=pltpu.CompilerParams(vmem_limit_bytes=4 * MIB),
        cost_estimate=SMALL,
    )(*pieces)


def round_sum(own, came, kind):
    def kernel(own, came, out):
        out[...] = (own[...] + came[...]).astype(kind)

    whole = pl.BlockSpec(memory_space=pltpu.VMEM)
    return pl.pallas_call(
        kernel,
        out_shape=jax.ShapeDtypeStruct(own.shape, kind),
        in_specs=[whole, whole],
        out_specs=whole,
        compiler_params=pltpu.CompilerParams(vmem_limit_bytes=4 * MIB),
        cost_estimate=SMALL,
    )(own, came)


def finish_grad(own, came, bits):
    share, slab = own.shape

    def kernel(own, *refs):
        bits, table, out = refs[-3:]
        total = own[...]
        for ref in refs[:-3]:
            total = total + ref[...].astype(jnp.float32)
        total = total * (2 * bits[...] - 1).astype(jnp.float32)
        result = None
        for _ in range(3):
            part = total.astype(jnp.bfloat16)
            total = total - part.astype(jnp.float32)
            term = jnp.dot(part, table[...], preferred_element_type=jnp.float32)
            result = term if result is None else result + term
        out[...] = result * (1.0 / math.sqrt(128.0))

    table = np.kron(np.eye(slab // 128), sylvester())
    whole = pl.BlockSpec(memory_space=pltpu.VMEM)
    return pl.pallas_call(
        kernel,
        out_shape=jax.ShapeDtypeStruct((share, slab), jnp.float32),
        in_specs=[whole] * (3 + len(came)),
        out_specs=whole,
        compiler_params=pltpu.CompilerParams(vmem_limit_bytes=12 * MIB),
        cost_estimate=LONGER,
    )(own, *came, bits, jnp.asarray(table, jnp.bfloat16))


def output_part(position, tokens, fars, pieces, before, part, cost):
    depth = tokens.shape[0]
    slab = pieces[0][0].shape[1]
    places = len(fars)
    count = len(pieces)
    lead = part // 128 * 128
    width = fars[0].shape[1] - lead
    edge = width - part

    def kernel(tok, *refs):
        windows = refs[:places]
        parts = refs[places : places + count]
        refs = refs[places + count :]
        if before is not None:
            old = refs[:2]
            refs = refs[2:]
        own, other, left, right, held, sems, piece_sems, old_sems, out_sems = refs
        earlier = []
        if before is not None:
            earlier = tile_copies(old, [held.at[0], held.at[1]], old_sems)
            start_all(earlier)
        waits = []
        for i, (_, first, step, other_side) in enumerate(pieces):
            start, place, column, row = position(step, other_side)
            near = pltpu.make_async_copy(
                tok.at[:, pl.ds(pl.multiple_of(start, 128), width)],
                left.at[i, pl.ds(0, depth)],
                sems.at[i, 0],
            )
            near.start()
            cols = pl.ds(pl.multiple_of(column, 128), width)
            copies = [
                pltpu.make_async_copy(
                    window.at[:, cols], left.at[i, pl.ds(depth, depth)], sems.at[i, 1]
                )
                for window in windows
            ]
            for k in range(places):
                pl.when(place == k)(copies[k].start)
            right[i, 0:edge, :] = jnp.zeros((edge, slab), jnp.bfloat16)
            right[i, width - edge : width, :] = jnp.zeros((edge, slab), jnp.bfloat16)
            piece = pltpu.make_async_copy(
                parts[i].at[pl.ds(first, part)],
                right.at[i, pl.ds(pl.multiple_of(row, 16), part)],
                piece_sems.at[i],
            )
            piece.start()
            waits.append([near, copies[0], piece])
        total = None
        for i in range(count):
            wait_all(waits[i])
            term = jnp.dot(left[i], right[i], preferred_element_type=jnp.float32)
            total = term if total is None else total + term
        wait_all(earlier)
        done = []
        for k, out in ((1, other), (0, own)):
            value = total[k * depth : (k + 1) * depth]
            held[k] = value if before is None else value + held[k]
            done.append(pltpu.make_async_copy(held.at[k], out, out_sems.at[k]))
            done[-1].start()
        wait_all(done)

    anywhere = pl.BlockSpec(memory_space=pl.ANY)
    shape = jax.ShapeDtypeStruct((depth, slab), jnp.float32)
    olds = () if before is None else tuple(before)
    return pl.pallas_call(
        kernel,
        out_shape=[shape, shape],
        in_specs=[anywhere] * (1 + places + count + len(olds)),
        out_specs=[anywhere, anywhere],
        scratch_shapes=[
            pltpu.VMEM((count, 2 * depth, width), jnp.bfloat16),
            pltpu.VMEM((count, width, slab), jnp.bfloat16),
            pltpu.VMEM((2, depth, slab), jnp.float32),
            pltpu.SemaphoreType.DMA((count, 2)),
            pltpu.SemaphoreType.DMA((count,)),
            pltpu.SemaphoreType.DMA((2,)),
            pltpu.SemaphoreType.DMA((2,)),
        ],
        compiler_params=pltpu.CompilerParams(vmem_limit_bytes=MEMORY),
        cost_estimate=cost,
    )(tokens, *fars, *[array for array, *_ in pieces], *olds)


def paired(mesh):
    n_outer = mesh.shape["outer"]
    n_node = mesh.shape["node"]
    orders = [[1, 2], [2, 1]]

    def core_swap(value):
        return lax.ppermute(value, "outer", [(o, o ^ 1) for o in range(n_outer)])

    def outer_swap(value, stage):
        return lax.ppermute(
            value, "outer", [(o, o ^ (1 << orders[o % 2][stage])) for o in range(n_outer)]
        )

    def node_shift(value, step):
        return lax.ppermute(value, "node", [(n, (n + step) % n_node) for n in range(n_node)])

    def place_of(o):
        bits = o >> 1
        return jnp.where(o % 2 == 0, bits, (bits >> 1) + 2 * (bits % 2))

    def on_device(tokens, cotangent, weight_codes, weight_scales, weight_bits, grad_bits):
        o = lax.axis_index("outer")
        width = tokens.shape[1]
        rows = width // n_outer
        share = rows // n_node
        node_rows = weight_codes.shape[0]
        window = (rows + 127) // 128 * 128
        edge = window - rows
        masks = (3, 1, 2, 0)

        def column(mask, o, mine):
            base = o if mine else o ^ 1
            which = base ^ jnp.where(
                base % 2 == 0, relative_of(orders, 0, mask), relative_of(orders, 1, mask)
            )
            return which // 2 * node_rows + which % 2 * (node_rows - window)

        def take(source, mask):
            return lax.dynamic_slice_in_dim(source, column(mask, o, False), window, 1)

        cot_far = core_swap(cotangent)
        leave = take(after(tokens, cotangent), 3)
        source = after(tokens, leave)
        far3 = core_swap(leave)
        fars = [far3] + [core_swap(take(source, mask)) for mask in masks[1:]]

        def columns(*masks):
            return lambda: [column(mask, lax.axis_index("outer"), True) for mask in masks]

        (first,) = grad_blocks(
            columns(3), tokens, fars[:1], cotangent, cot_far, [jnp.bfloat16], LONG
        )
        came3 = outer_swap(first, 0)

        part = rows // 2

        def side_of(o):
            return jnp.where(o % 2 == 0, o >> 1, o >> 2) % 2

        start = o % 2 * rows + side_of(o) * part
        held = rotate(
            dequantize(
                lax.dynamic_slice_in_dim(after(weight_codes, first), start, part),
                lax.dynamic_slice_in_dim(after(weight_scales, first), start, part),
            ),
            after(weight_bits, first),
        ).astype(jnp.bfloat16)
        ahead = node_shift(held, 1)

        def position():
            return lax.axis_index("outer") % 2 * edge, lax.axis_index("node")

        def out_position(step, other_side):
            o = lax.axis_index("outer")
            n = lax.axis_index("node")
            core = o % 2
            node = lax.rem(n + n_node - step, n_node)
            side = side_of(o) if other_side == 0 else 1 - side_of(o)
            bits = place_of((node * 2 + core) ^ (o - core))
            place = jnp.where(bits == 3, 0, jnp.where(bits == 1, 1, jnp.where(bits == 2, 2, 3)))
            lead = part // 128 * 128
            start = node * node_rows + core * (node_rows - window) + side * lead
            return start, place, side * lead, core * edge + side * (part - lead)

        def product(pieces, before, later_than, cost):
            source = after(tokens, later_than)
            return output_part(out_position, source, fars, pieces, before, part, cost)

        second, keep2 = grad_blocks(
            columns(*masks[1:3]), after(tokens, held), fars[1:3], cotangent, cot_far,
            [jnp.bfloat16, jnp.float32], LONGER,
        )
        came1 = outer_swap(second, 0)
        passed = add_blocks(keep2, came3)
        came2 = outer_swap(passed, 1)
        behind = node_shift(after(held, passed), n_node - 1)
        early = product([(held, 0, 0, 0)], None, passed, LONGER)
        ahead, *early = lax.optimization_barrier((ahead, *early))
        relay = node_shift(ahead, 1)
        (keep0,) = grad_blocks(
            columns(masks[3]), after(tokens, *early), fars[3:], cotangent, cot_far,
            [jnp.float32], SMALL,
        )
        joined = join([held, ahead, behind])
        came2, joined, _ = lax.optimization_barrier((came2, joined, keep0))
        own, *sends = cut_shares(position, keep0, came1, came2, rows, share)
        arrived = [node_shift(sends[step - 1], step) for step in range(1, n_node)]
        grad_rotated = finish_grad(own, arrived, grad_bits.reshape(1, -1))

        swap013 = outer_swap(joined, 0)
        sums = product(
            [(ahead, 0, 1, 0), (behind, 0, n_node - 1, 0), (relay, 0, 2, 0)],
            early, sends[0], MIDDLE,
        )
        swap2 = outer_swap(after(relay, swap013), 0)
        sums = product(
            [(swap013, 0, 0, 1), (swap013, part, 1, 1), (swap013, 2 * part, n_node - 1, 1)],
            sums, swap013, MIDDLE,
        )
        own_part, other_part = product([(swap2, 0, 2, 1)], sums, swap2, SMALL)
        output = round_sum(own_part, core_swap(other_part), tokens.dtype)
        return output, grad_rotated

    return on_device


def general(mesh):
    n_outer = mesh.shape["outer"]
    n_node = mesh.shape["node"]
    n_bits = n_outer.bit_length() - 1
    orders = [list(range(1, n_bits)), [2, 1] + list(range(3, n_bits))]

    def outer_swap(value, stage):
        pairs = []
        for o in range(n_outer):
            pairs.append((o, o ^ (1 if stage is None else 1 << orders[o % 2][stage])))
        return lax.ppermute(value, "outer", pairs)

    def node_shift(value, step):
        return lax.ppermute(value, "node", [(n, (n + step) % n_node) for n in range(n_node)])

    def on_device(tokens, cotangent, weight_codes, weight_scales, weight_bits, grad_bits):
        o = lax.axis_index("outer")
        n = lax.axis_index("node")
        core = o % 2
        width = tokens.shape[1]
        slab = cotangent.shape[1]

        part = weight_codes.shape[0] // 4
        side = jnp.where(core == 0, (o >> orders[0][0]) % 2, (o >> orders[1][0]) % 2)
        mate_side = jnp.where(core == 0, (o >> orders[1][0]) % 2, (o >> orders[0][0]) % 2)
        quarter = core * 2 + side
        start = quarter * part
        held = rotate(
            dequantize(
                lax.dynamic_slice_in_dim(weight_codes, start, part),
                lax.dynamic_slice_in_dim(weight_scales, start, part),
            ),
            weight_bits,
        ).astype(jnp.bfloat16)

        total = lax.dot_general(
            tokens, cotangent, (((0,), (0,)), ((), ())), preferred_element_type=jnp.float32
        ).astype(jnp.bfloat16)
        rows = width // n_outer
        blocks = {}

        def own(d):
            return lax.dynamic_slice_in_dim(total, (o ^ d) * rows, rows)

        def relative(mask):
            found = [0, 0]
            for c in range(2):
                for j, bit in enumerate(orders[c]):
                    if mask >> j & 1:
                        found[c] |= 1 << bit
            return jnp.where(core == 0, found[0], found[1])

        n_rest = n_bits - 1
        sums = {}
        for mask in reversed(range(2**n_rest)):
            partner = jnp.where(core == 0, relative_of(orders, 1, mask), relative_of(orders, 0, mask))
            came = outer_swap(own(partner ^ 1), None)
            sums[mask] = own(relative(mask)).astype(jnp.float32) + came.astype(jnp.float32)
        for stage in range(n_rest):
            low = 1 << stage
            for mask in sorted([m for m in sums if m & low], reverse=True):
                came = outer_swap(sums.pop(mask).astype(jnp.bfloat16), stage)
                sums[mask ^ low] = sums[mask ^ low] + came.astype(jnp.float32)
        mine = sums[0]
        share = rows // n_node
        send = mine.astype(jnp.bfloat16)
        grad = lax.dynamic_slice_in_dim(mine, n * share, share)
        for step in range(1, n_node):
            piece = lax.dynamic_slice_in_dim(send, (n + step) % n_node * share, share)
            grad = grad + node_shift(piece, step).astype(jnp.float32)
        grad_rotated = rotate(grad, grad_bits)

        weight = jnp.zeros((width, slab), jnp.bfloat16)
        node_rows = weight_codes.shape[0]
        for step in range(n_node):
            base = (n - step) % n_node * node_rows
            across = outer_swap(held, 0)
            mate = outer_swap(held, None)
            mate_across = outer_swap(across, None)
            pieces = [
                (held, core * 2 + side),
                (across, core * 2 + 1 - side),
                (mate, (1 - core) * 2 + mate_side),
                (mate_across, (1 - core) * 2 + 1 - mate_side),
            ]
            for value, place in pieces:
                weight = lax.dynamic_update_slice_in_dim(weight, value, base + place * part, 0)
            if step < n_node - 1:
                held = node_shift(held, 1)
        output = jnp.dot(tokens, weight, preferred_element_type=jnp.float32).astype(jnp.bfloat16)
        return output, grad_rotated

    return on_device


def solution(mesh):
    n_outer = mesh.shape["outer"]
    n_node = mesh.shape["node"]
    on_device = paired(mesh) if n_outer == 8 and n_node == 4 else general(mesh)
    return jax.shard_map(
        on_device,
        mesh=mesh,
        in_specs=(
            P(("outer", "node"), None),
            P(("outer", "node"), None),
            P("node", None),
            P("node", None),
            P(),
            P(),
        ),
        out_specs=(P(("outer", "node"), None), P(("outer", "node"), None)),
        check_vma=False,
    )
```

```python
import math

import jax
import jax.numpy as jnp
import numpy as np
from jax import lax
from jax.experimental import pallas as pl
from jax.experimental.pallas import tpu as pltpu
from jax.sharding import PartitionSpec as P


def sylvester():
    row_index = np.arange(128).reshape(128, 1)
    column_index = np.arange(128).reshape(1, 128)
    parity = np.zeros((128, 128))
    for level in range(7):
        parity = parity + row_index // 2**level % 2 * (column_index // 2**level % 2)
    return 1.0 - 2.0 * (parity % 2)


def rotate(values, bits):
    width = values.shape[1]
    signs = (2 * bits - 1).astype(jnp.float32)
    table = np.kron(np.eye(width // 128), sylvester()) / math.sqrt(128.0)
    return jnp.dot(
        values * signs,
        jnp.asarray(table, jnp.float32),
        precision=lax.Precision.HIGHEST,
    )


def dequantize(codes, scales):
    height, width = codes.shape
    spread = jnp.concatenate(
        [
            jnp.broadcast_to(scales[:, block : block + 1], (height, 128))
            for block in range(width // 128)
        ],
        axis=1,
    )
    return codes.astype(jnp.float32) * spread


def relative_of(orders, core, mask):
    found = 0
    for j, bit in enumerate(orders[core]):
        if mask >> j & 1:
            found |= 1 << bit
    return found


SMALL = pl.CostEstimate(flops=0, bytes_accessed=1024, transcendentals=0)
LONG = pl.CostEstimate(flops=5 * 10**9, bytes_accessed=1024, transcendentals=0)
MIDDLE = pl.CostEstimate(flops=8 * 10**9, bytes_accessed=1024, transcendentals=0)
MORE = pl.CostEstimate(flops=15 * 10**9, bytes_accessed=1024, transcendentals=0)
LONGER = pl.CostEstimate(flops=6 * 10**10, bytes_accessed=1024, transcendentals=0)
MIB = 2**20
MEMORY = 56 * MIB


def after(value, *deps):
    return lax.optimization_barrier((value, *deps))[0]


def tile_of(window):
    return max(128 * k for k in range(1, 6) if window % (128 * k) == 0)


def tile_copies(sources, dests, sems):
    return [
        pltpu.make_async_copy(source, dest, sems.at[i])
        for i, (source, dest) in enumerate(zip(sources, dests))
    ]


def start_all(copies):
    for copy in copies:
        copy.start()


def wait_all(copies):
    for copy in copies:
        copy.wait()


def grad_blocks(columns, tokens, fars, cot, cot_far, kinds, cost):
    count = len(fars)
    depth, slab = cot.shape
    window = fars[0].shape[1]
    tile = tile_of(window)
    tiles = window // tile

    def kernel(tok, cot, cot_far, *refs):
        far_refs, outs = refs[:count], refs[count : 2 * count]
        cots, left, sems, cot_sems, out_sems = refs[2 * count : 2 * count + 5]
        held = refs[2 * count + 5 :]
        first = columns()
        ends = tile_copies([cot, cot_far], [cots.at[0], cots.at[1]], cot_sems)
        start_all(ends)
        copies = {}
        for i in range(count):
            for j in range(tiles):
                near = tok.at[:, pl.ds(pl.multiple_of(first[i] + j * tile, 128), tile)]
                far = far_refs[i].at[:, pl.ds(j * tile, tile)]
                copies[i, j] = tile_copies(
                    [near, far], [left.at[i, j, 0], left.at[i, j, 1]], sems.at[i, j]
                )
                start_all(copies[i, j])
        wait_all(ends)
        mine, theirs = cots[0].T, cots[1].T
        done = []
        for i in range(count):
            for j in range(tiles):
                wait_all(copies[i, j])
                held[i][j] = (
                    jnp.dot(mine, left[i, j, 0], preferred_element_type=jnp.float32)
                    + jnp.dot(theirs, left[i, j, 1], preferred_element_type=jnp.float32)
                ).astype(kinds[i])
                done.append(
                    pltpu.make_async_copy(
                        held[i].at[j], outs[i].at[:, pl.ds(j * tile, tile)], out_sems.at[i, j]
                    )
                )
                done[-1].start()
        wait_all(done)

    anywhere = pl.BlockSpec(memory_space=pl.ANY)
    return pl.pallas_call(
        kernel,
        out_shape=[jax.ShapeDtypeStruct((slab, window), kind) for kind in kinds],
        in_specs=[anywhere] * (3 + count),
        out_specs=[anywhere] * count,
        scratch_shapes=[
            pltpu.VMEM((2, depth, slab), jnp.bfloat16),
            pltpu.VMEM((count, tiles, 2, depth, tile), jnp.bfloat16),
            pltpu.SemaphoreType.DMA((count, tiles, 2)),
            pltpu.SemaphoreType.DMA((2,)),
            pltpu.SemaphoreType.DMA((count, tiles)),
        ]
        + [pltpu.VMEM((tiles, slab, tile), kind) for kind in kinds],
        compiler_params=pltpu.CompilerParams(vmem_limit_bytes=MEMORY),
        cost_estimate=cost,
    )(tokens, cot, cot_far, *fars)


def add_blocks(keep, came):
    slab, window = keep.shape
    tile = tile_of(window)
    tiles = window // tile

    def kernel(keep, came, out, left, right, held, sems, out_sems):
        copies = []
        for j in range(tiles):
            cols = pl.ds(j * tile, tile)
            copies.append(
                tile_copies(
                    [keep.at[:, cols], came.at[:, cols]], [left.at[j], right.at[j]], sems.at[j]
                )
            )
            start_all(copies[j])
        done = []
        for j in range(tiles):
            wait_all(copies[j])
            held[j] = (left[j] + right[j].astype(jnp.float32)).astype(jnp.bfloat16)
            done.append(
                pltpu.make_async_copy(held.at[j], out.at[:, pl.ds(j * tile, tile)], out_sems.at[j])
            )
            done[-1].start()
        wait_all(done)

    anywhere = pl.BlockSpec(memory_space=pl.ANY)
    return pl.pallas_call(
        kernel,
        out_shape=jax.ShapeDtypeStruct((slab, window), jnp.bfloat16),
        in_specs=[anywhere] * 2,
        out_specs=anywhere,
        scratch_shapes=[
            pltpu.VMEM((tiles, slab, tile), jnp.float32),
            pltpu.VMEM((tiles, slab, tile), jnp.bfloat16),
            pltpu.VMEM((tiles, slab, tile), jnp.bfloat16),
            pltpu.SemaphoreType.DMA((tiles, 2)),
            pltpu.SemaphoreType.DMA((tiles,)),
        ],
        compiler_params=pltpu.CompilerParams(vmem_limit_bytes=6 * MIB),
        cost_estimate=SMALL,
    )(keep, came)


def cut_shares(position, keep, came, came2, rows, share):
    slab, window = keep.shape
    tile = tile_of(window)
    tiles = window // tile
    n_share = rows // share

    def kernel(keep, came, came2, own, *refs):
        sends = refs[: n_share - 1]
        left, right, total, own_held, send_held, sems, out_sems = refs[n_share - 1 :]
        copies = []
        for j in range(tiles):
            cols = pl.ds(j * tile, tile)
            copies.append(
                tile_copies(
                    [keep.at[:, cols], came.at[:, cols], came2.at[:, cols]],
                    [left.at[j], right.at[j, 0], right.at[j, 1]],
                    sems.at[j],
                )
            )
            start_all(copies[j])
        for j in range(tiles):
            wait_all(copies[j])
            block = (
                left[j] + right[j, 0].astype(jnp.float32) + right[j, 1].astype(jnp.float32)
            )
            total[j * tile : (j + 1) * tile, :] = block.T
        skip, place = position()
        done = []
        for k in [*range(1, n_share), 0]:
            first = skip + lax.rem(place + k, n_share) * share
            value = total[pl.ds(pl.multiple_of(first, 16), share), :]
            if k == 0:
                own_held[...] = value
                copy = pltpu.make_async_copy(own_held, own, out_sems.at[0])
            else:
                send_held[k - 1] = value.astype(jnp.bfloat16)
                copy = pltpu.make_async_copy(send_held.at[k - 1], sends[k - 1], out_sems.at[k])
            copy.start()
            done.append(copy)
        wait_all(done)

    anywhere = pl.BlockSpec(memory_space=pl.ANY)
    return pl.pallas_call(
        kernel,
        out_shape=[jax.ShapeDtypeStruct((share, slab), jnp.float32)]
        + [jax.ShapeDtypeStruct((share, slab), jnp.bfloat16)] * (n_share - 1),
        in_specs=[anywhere] * 3,
        out_specs=[anywhere] * n_share,
        scratch_shapes=[
            pltpu.VMEM((tiles, slab, tile), jnp.float32),
            pltpu.VMEM((tiles, 2, slab, tile), jnp.bfloat16),
            pltpu.VMEM((window, slab), jnp.float32),
            pltpu.VMEM((share, slab), jnp.float32),
            pltpu.VMEM((n_share - 1, share, slab), jnp.bfloat16),
            pltpu.SemaphoreType.DMA((tiles, 3)),
            pltpu.SemaphoreType.DMA((n_share,)),
        ],
        compiler_params=pltpu.CompilerParams(vmem_limit_bytes=9 * MIB),
        cost_estimate=SMALL,
    )(keep, came, came2)


def join(pieces):
    count = len(pieces)
    rows, slab = pieces[0].shape

    def kernel(*refs):
        out, held, sems = refs[count:]
        moves = tile_copies(refs[:count], [held.at[i] for i in range(count)], sems.at[0])
        start_all(moves)
        done = []
        for i in range(count):
            moves[i].wait()
            done.append(
                pltpu.make_async_copy(held.at[i], out.at[pl.ds(i * rows, rows)], sems.at[1, i])
            )
            done[-1].start()
        wait_all(done)

    anywhere = pl.BlockSpec(memory_space=pl.ANY)
    return pl.pallas_call(
        kernel,
        out_shape=jax.ShapeDtypeStruct((count * rows, slab), pieces[0].dtype),
        in_specs=[anywhere] * count,
        out_specs=anywhere,
        scratch_shapes=[
            pltpu.VMEM((count, rows, slab), pieces[0].dtype),
            pltpu.SemaphoreType.DMA((2, count)),
        ],
        compiler_params=pltpu.CompilerParams(vmem_limit_bytes=4 * MIB),
        cost_estimate=SMALL,
    )(*pieces)


def round_sum(own, came, kind):
    def kernel(own, came, out):
        out[...] = (own[...] + came[...]).astype(kind)

    whole = pl.BlockSpec(memory_space=pltpu.VMEM)
    return pl.pallas_call(
        kernel,
        out_shape=jax.ShapeDtypeStruct(own.shape, kind),
        in_specs=[whole, whole],
        out_specs=whole,
        compiler_params=pltpu.CompilerParams(vmem_limit_bytes=4 * MIB),
        cost_estimate=SMALL,
    )(own, came)


def finish_grad(own, came, bits):
    share, slab = own.shape

    def kernel(own, *refs):
        bits, table, out = refs[-3:]
        total = own[...]
        for ref in refs[:-3]:
            total = total + ref[...].astype(jnp.float32)
        total = total * (2 * bits[...] - 1).astype(jnp.float32)
        result = None
        for _ in range(3):
            part = total.astype(jnp.bfloat16)
            total = total - part.astype(jnp.float32)
            term = jnp.dot(part, table[...], preferred_element_type=jnp.float32)
            result = term if result is None else result + term
        out[...] = result * (1.0 / math.sqrt(128.0))

    table = np.kron(np.eye(slab // 128), sylvester())
    whole = pl.BlockSpec(memory_space=pltpu.VMEM)
    return pl.pallas_call(
        kernel,
        out_shape=jax.ShapeDtypeStruct((share, slab), jnp.float32),
        in_specs=[whole] * (3 + len(came)),
        out_specs=whole,
        compiler_params=pltpu.CompilerParams(vmem_limit_bytes=12 * MIB),
        cost_estimate=LONGER,
    )(own, *came, bits, jnp.asarray(table, jnp.bfloat16))


def output_part(position, tokens, fars, pieces, before, part, cost):
    depth = tokens.shape[0]
    slab = pieces[0][0].shape[1]
    places = len(fars)
    count = len(pieces)
    lead = part // 128 * 128
    width = fars[0].shape[1] - lead
    edge = width - part

    def kernel(tok, *refs):
        windows = refs[:places]
        parts = refs[places : places + count]
        refs = refs[places + count :]
        if before is not None:
            old = refs[:2]
            refs = refs[2:]
        own, other, left, right, held, sems, piece_sems, old_sems, out_sems = refs
        earlier = []
        if before is not None:
            earlier = tile_copies(old, [held.at[0], held.at[1]], old_sems)
            start_all(earlier)
        waits = []
        for i, (_, first, step, other_side) in enumerate(pieces):
            start, place, column, row = position(step, other_side)
            near = pltpu.make_async_copy(
                tok.at[:, pl.ds(pl.multiple_of(start, 128), width)],
                left.at[i, pl.ds(0, depth)],
                sems.at[i, 0],
            )
            near.start()
            cols = pl.ds(pl.multiple_of(column, 128), width)
            copies = [
                pltpu.make_async_copy(
                    window.at[:, cols], left.at[i, pl.ds(depth, depth)], sems.at[i, 1]
                )
                for window in windows
            ]
            for k in range(places):
                pl.when(place == k)(copies[k].start)
            right[i, 0:edge, :] = jnp.zeros((edge, slab), jnp.bfloat16)
            right[i, width - edge : width, :] = jnp.zeros((edge, slab), jnp.bfloat16)
            piece = pltpu.make_async_copy(
                parts[i].at[pl.ds(first, part)],
                right.at[i, pl.ds(pl.multiple_of(row, 16), part)],
                piece_sems.at[i],
            )
            piece.start()
            waits.append([near, copies[0], piece])
        total = None
        for i in range(count):
            wait_all(waits[i])
            term = jnp.dot(left[i], right[i], preferred_element_type=jnp.float32)
            total = term if total is None else total + term
        wait_all(earlier)
        done = []
        for k, out in ((1, other), (0, own)):
            value = total[k * depth : (k + 1) * depth]
            held[k] = value if before is None else value + held[k]
            done.append(pltpu.make_async_copy(held.at[k], out, out_sems.at[k]))
            done[-1].start()
        wait_all(done)

    anywhere = pl.BlockSpec(memory_space=pl.ANY)
    shape = jax.ShapeDtypeStruct((depth, slab), jnp.float32)
    olds = () if before is None else tuple(before)
    return pl.pallas_call(
        kernel,
        out_shape=[shape, shape],
        in_specs=[anywhere] * (1 + places + count + len(olds)),
        out_specs=[anywhere, anywhere],
        scratch_shapes=[
            pltpu.VMEM((count, 2 * depth, width), jnp.bfloat16),
            pltpu.VMEM((count, width, slab), jnp.bfloat16),
            pltpu.VMEM((2, depth, slab), jnp.float32),
            pltpu.SemaphoreType.DMA((count, 2)),
            pltpu.SemaphoreType.DMA((count,)),
            pltpu.SemaphoreType.DMA((2,)),
            pltpu.SemaphoreType.DMA((2,)),
        ],
        compiler_params=pltpu.CompilerParams(vmem_limit_bytes=MEMORY),
        cost_estimate=cost,
    )(tokens, *fars, *[array for array, *_ in pieces], *olds)


def paired(mesh):
    n_outer = mesh.shape["outer"]
    n_node = mesh.shape["node"]
    orders = [[1, 2], [2, 1]]

    def core_swap(value):
        return lax.ppermute(value, "outer", [(o, o ^ 1) for o in range(n_outer)])

    def outer_swap(value, stage):
        return lax.ppermute(
            value, "outer", [(o, o ^ (1 << orders[o % 2][stage])) for o in range(n_outer)]
        )

    def node_shift(value, step):
        return lax.ppermute(value, "node", [(n, (n + step) % n_node) for n in range(n_node)])

    def place_of(o):
        bits = o >> 1
        return jnp.where(o % 2 == 0, bits, (bits >> 1) + 2 * (bits % 2))

    def on_device(tokens, cotangent, weight_codes, weight_scales, weight_bits, grad_bits):
        o = lax.axis_index("outer")
        width = tokens.shape[1]
        rows = width // n_outer
        share = rows // n_node
        node_rows = weight_codes.shape[0]
        window = (rows + 127) // 128 * 128
        edge = window - rows
        masks = (3, 1, 2, 0)

        def column(mask, o, mine):
            base = o if mine else o ^ 1
            which = base ^ jnp.where(
                base % 2 == 0, relative_of(orders, 0, mask), relative_of(orders, 1, mask)
            )
            return which // 2 * node_rows + which % 2 * (node_rows - window)

        def take(source, mask):
            return lax.dynamic_slice_in_dim(source, column(mask, o, False), window, 1)

        cot_far = core_swap(cotangent)
        leave = take(after(tokens, cotangent), 3)
        source = after(tokens, leave)
        far3 = core_swap(leave)
        fars = [far3] + [core_swap(take(source, mask)) for mask in masks[1:]]

        def columns(*masks):
            return lambda: [column(mask, lax.axis_index("outer"), True) for mask in masks]

        (first,) = grad_blocks(
            columns(3), tokens, fars[:1], cotangent, cot_far, [jnp.bfloat16], LONG
        )
        came3 = outer_swap(first, 0)

        part = rows // 2

        def side_of(o):
            return jnp.where(o % 2 == 0, o >> 1, o >> 2) % 2

        start = o % 2 * rows + side_of(o) * part
        held = rotate(
            dequantize(
                lax.dynamic_slice_in_dim(after(weight_codes, first), start, part),
                lax.dynamic_slice_in_dim(after(weight_scales, first), start, part),
            ),
            after(weight_bits, first),
        ).astype(jnp.bfloat16)
        swap0 = outer_swap(held, 0)
        ahead = node_shift(held, 1)

        def position():
            return lax.axis_index("outer") % 2 * edge, lax.axis_index("node")

        def out_position(step, other_side):
            o = lax.axis_index("outer")
            n = lax.axis_index("node")
            core = o % 2
            node = lax.rem(n + n_node - step, n_node)
            side = side_of(o) if other_side == 0 else 1 - side_of(o)
            bits = place_of((node * 2 + core) ^ (o - core))
            place = jnp.where(bits == 3, 0, jnp.where(bits == 1, 1, jnp.where(bits == 2, 2, 3)))
            lead = part // 128 * 128
            start = node * node_rows + core * (node_rows - window) + side * lead
            return start, place, side * lead, core * edge + side * (part - lead)

        def product(pieces, before, later_than, cost):
            source = after(tokens, later_than)
            return output_part(out_position, source, fars, pieces, before, part, cost)

        second, keep2 = grad_blocks(
            columns(*masks[1:3]), after(tokens, held), fars[1:3], cotangent, cot_far,
            [jnp.bfloat16, jnp.float32], LONGER,
        )
        came1 = outer_swap(second, 0)
        passed = add_blocks(keep2, came3)
        came2 = outer_swap(passed, 1)
        behind = node_shift(after(held, passed), n_node - 1)
        early = product([(held, 0, 0, 0), (swap0, 0, 0, 1)], None, passed, LONGER)
        ahead, *early = lax.optimization_barrier((ahead, *early))
        relay = node_shift(ahead, 1)
        (keep0,) = grad_blocks(
            columns(masks[3]), after(tokens, *early), fars[3:], cotangent, cot_far,
            [jnp.float32], SMALL,
        )
        joined = join([ahead, behind])
        came2, joined, _ = lax.optimization_barrier((came2, joined, keep0))
        own, *sends = cut_shares(position, keep0, came1, came2, rows, share)
        arrived = [node_shift(sends[step - 1], step) for step in range(1, n_node)]
        grad_rotated = finish_grad(own, arrived, grad_bits.reshape(1, -1))

        swap13 = outer_swap(joined, 0)
        sums = product(
            [(ahead, 0, 1, 0), (behind, 0, n_node - 1, 0), (relay, 0, 2, 0)],
            early, sends[0], MIDDLE,
        )
        swap2 = outer_swap(after(relay, swap13), 0)
        sums = product(
            [(swap13, 0, 1, 1), (swap13, part, n_node - 1, 1)],
            sums, swap13, MORE,
        )
        own_part, other_part = product([(swap2, 0, 2, 1)], sums, swap2, SMALL)
        output = round_sum(own_part, core_swap(other_part), tokens.dtype)
        return output, grad_rotated

    return on_device


def general(mesh):
    n_outer = mesh.shape["outer"]
    n_node = mesh.shape["node"]
    n_bits = n_outer.bit_length() - 1
    orders = [list(range(1, n_bits)), [2, 1] + list(range(3, n_bits))]

    def outer_swap(value, stage):
        pairs = []
        for o in range(n_outer):
            pairs.append((o, o ^ (1 if stage is None else 1 << orders[o % 2][stage])))
        return lax.ppermute(value, "outer", pairs)

    def node_shift(value, step):
        return lax.ppermute(value, "node", [(n, (n + step) % n_node) for n in range(n_node)])

    def on_device(tokens, cotangent, weight_codes, weight_scales, weight_bits, grad_bits):
        o = lax.axis_index("outer")
        n = lax.axis_index("node")
        core = o % 2
        width = tokens.shape[1]
        slab = cotangent.shape[1]

        part = weight_codes.shape[0] // 4
        side = jnp.where(core == 0, (o >> orders[0][0]) % 2, (o >> orders[1][0]) % 2)
        mate_side = jnp.where(core == 0, (o >> orders[1][0]) % 2, (o >> orders[0][0]) % 2)
        quarter = core * 2 + side
        start = quarter * part
        held = rotate(
            dequantize(
                lax.dynamic_slice_in_dim(weight_codes, start, part),
                lax.dynamic_slice_in_dim(weight_scales, start, part),
            ),
            weight_bits,
        ).astype(jnp.bfloat16)

        total = lax.dot_general(
            tokens, cotangent, (((0,), (0,)), ((), ())), preferred_element_type=jnp.float32
        ).astype(jnp.bfloat16)
        rows = width // n_outer
        blocks = {}

        def own(d):
            return lax.dynamic_slice_in_dim(total, (o ^ d) * rows, rows)

        def relative(mask):
            found = [0, 0]
            for c in range(2):
                for j, bit in enumerate(orders[c]):
                    if mask >> j & 1:
                        found[c] |= 1 << bit
            return jnp.where(core == 0, found[0], found[1])

        n_rest = n_bits - 1
        sums = {}
        for mask in reversed(range(2**n_rest)):
            partner = jnp.where(core == 0, relative_of(orders, 1, mask), relative_of(orders, 0, mask))
            came = outer_swap(own(partner ^ 1), None)
            sums[mask] = own(relative(mask)).astype(jnp.float32) + came.astype(jnp.float32)
        for stage in range(n_rest):
            low = 1 << stage
            for mask in sorted([m for m in sums if m & low], reverse=True):
                came = outer_swap(sums.pop(mask).astype(jnp.bfloat16), stage)
                sums[mask ^ low] = sums[mask ^ low] + came.astype(jnp.float32)
        mine = sums[0]
        share = rows // n_node
        send = mine.astype(jnp.bfloat16)
        grad = lax.dynamic_slice_in_dim(mine, n * share, share)
        for step in range(1, n_node):
            piece = lax.dynamic_slice_in_dim(send, (n + step) % n_node * share, share)
            grad = grad + node_shift(piece, step).astype(jnp.float32)
        grad_rotated = rotate(grad, grad_bits)

        weight = jnp.zeros((width, slab), jnp.bfloat16)
        node_rows = weight_codes.shape[0]
        for step in range(n_node):
            base = (n - step) % n_node * node_rows
            across = outer_swap(held, 0)
            mate = outer_swap(held, None)
            mate_across = outer_swap(across, None)
            pieces = [
                (held, core * 2 + side),
                (across, core * 2 + 1 - side),
                (mate, (1 - core) * 2 + mate_side),
                (mate_across, (1 - core) * 2 + 1 - mate_side),
            ]
            for value, place in pieces:
                weight = lax.dynamic_update_slice_in_dim(weight, value, base + place * part, 0)
            if step < n_node - 1:
                held = node_shift(held, 1)
        output = jnp.dot(tokens, weight, preferred_element_type=jnp.float32).astype(jnp.bfloat16)
        return output, grad_rotated

    return on_device


def solution(mesh):
    n_outer = mesh.shape["outer"]
    n_node = mesh.shape["node"]
    on_device = paired(mesh) if n_outer == 8 and n_node == 4 else general(mesh)
    return jax.shard_map(
        on_device,
        mesh=mesh,
        in_specs=(
            P(("outer", "node"), None),
            P(("outer", "node"), None),
            P("node", None),
            P("node", None),
            P(),
            P(),
        ),
        out_specs=(P(("outer", "node"), None), P(("outer", "node"), None)),
        check_vma=False,
    )
```

```python
import math

import jax
import jax.numpy as jnp
import numpy as np
from jax import lax
from jax.experimental import pallas as pl
from jax.experimental.pallas import tpu as pltpu
from jax.sharding import PartitionSpec as P


def sylvester():
    row_index = np.arange(128).reshape(128, 1)
    column_index = np.arange(128).reshape(1, 128)
    parity = np.zeros((128, 128))
    for level in range(7):
        parity = parity + row_index // 2**level % 2 * (column_index // 2**level % 2)
    return 1.0 - 2.0 * (parity % 2)


def rotate(values, bits):
    width = values.shape[1]
    signs = (2 * bits - 1).astype(jnp.float32)
    table = np.kron(np.eye(width // 128), sylvester()) / math.sqrt(128.0)
    return jnp.dot(
        values * signs,
        jnp.asarray(table, jnp.float32),
        precision=lax.Precision.HIGHEST,
    )


def dequantize(codes, scales):
    height, width = codes.shape
    spread = jnp.concatenate(
        [
            jnp.broadcast_to(scales[:, block : block + 1], (height, 128))
            for block in range(width // 128)
        ],
        axis=1,
    )
    return codes.astype(jnp.float32) * spread


def relative_of(orders, core, mask):
    found = 0
    for j, bit in enumerate(orders[core]):
        if mask >> j & 1:
            found |= 1 << bit
    return found


SMALL = pl.CostEstimate(flops=0, bytes_accessed=1024, transcendentals=0)
LONG = pl.CostEstimate(flops=5 * 10**9, bytes_accessed=1024, transcendentals=0)
MIDDLE = pl.CostEstimate(flops=8 * 10**9, bytes_accessed=1024, transcendentals=0)
MORE = pl.CostEstimate(flops=15 * 10**9, bytes_accessed=1024, transcendentals=0)
LONGER = pl.CostEstimate(flops=6 * 10**10, bytes_accessed=1024, transcendentals=0)
MIB = 2**20
MEMORY = 56 * MIB


def after(value, *deps):
    return lax.optimization_barrier((value, *deps))[0]


def tile_of(window):
    return max(128 * k for k in range(1, 6) if window % (128 * k) == 0)


def tile_copies(sources, dests, sems):
    return [
        pltpu.make_async_copy(source, dest, sems.at[i])
        for i, (source, dest) in enumerate(zip(sources, dests))
    ]


def start_all(copies):
    for copy in copies:
        copy.start()


def wait_all(copies):
    for copy in copies:
        copy.wait()


def grad_blocks(columns, tokens, fars, cot, cot_far, kinds, cost):
    count = len(fars)
    depth, slab = cot.shape
    window = fars[0].shape[1]
    tile = tile_of(window)
    tiles = window // tile

    def kernel(tok, cot, cot_far, *refs):
        far_refs, outs = refs[:count], refs[count : 2 * count]
        cots, left, sems, cot_sems, out_sems = refs[2 * count : 2 * count + 5]
        held = refs[2 * count + 5 :]
        first = columns()
        ends = tile_copies([cot, cot_far], [cots.at[0], cots.at[1]], cot_sems)
        start_all(ends)
        copies = {}
        for i in range(count):
            for j in range(tiles):
                near = tok.at[:, pl.ds(pl.multiple_of(first[i] + j * tile, 128), tile)]
                far = far_refs[i].at[:, pl.ds(j * tile, tile)]
                copies[i, j] = tile_copies(
                    [near, far], [left.at[i, j, 0], left.at[i, j, 1]], sems.at[i, j]
                )
                start_all(copies[i, j])
        wait_all(ends)
        mine, theirs = cots[0].T, cots[1].T
        done = []
        for i in range(count):
            for j in range(tiles):
                wait_all(copies[i, j])
                held[i][j] = (
                    jnp.dot(mine, left[i, j, 0], preferred_element_type=jnp.float32)
                    + jnp.dot(theirs, left[i, j, 1], preferred_element_type=jnp.float32)
                ).astype(kinds[i])
                done.append(
                    pltpu.make_async_copy(
                        held[i].at[j], outs[i].at[:, pl.ds(j * tile, tile)], out_sems.at[i, j]
                    )
                )
                done[-1].start()
        wait_all(done)

    anywhere = pl.BlockSpec(memory_space=pl.ANY)
    return pl.pallas_call(
        kernel,
        out_shape=[jax.ShapeDtypeStruct((slab, window), kind) for kind in kinds],
        in_specs=[anywhere] * (3 + count),
        out_specs=[anywhere] * count,
        scratch_shapes=[
            pltpu.VMEM((2, depth, slab), jnp.bfloat16),
            pltpu.VMEM((count, tiles, 2, depth, tile), jnp.bfloat16),
            pltpu.SemaphoreType.DMA((count, tiles, 2)),
            pltpu.SemaphoreType.DMA((2,)),
            pltpu.SemaphoreType.DMA((count, tiles)),
        ]
        + [pltpu.VMEM((tiles, slab, tile), kind) for kind in kinds],
        compiler_params=pltpu.CompilerParams(vmem_limit_bytes=MEMORY),
        cost_estimate=cost,
    )(tokens, cot, cot_far, *fars)


def add_blocks(keep, came):
    slab, window = keep.shape
    tile = tile_of(window)
    tiles = window // tile

    def kernel(keep, came, out, left, right, held, sems, out_sems):
        copies = []
        for j in range(tiles):
            cols = pl.ds(j * tile, tile)
            copies.append(
                tile_copies(
                    [keep.at[:, cols], came.at[:, cols]], [left.at[j], right.at[j]], sems.at[j]
                )
            )
            start_all(copies[j])
        done = []
        for j in range(tiles):
            wait_all(copies[j])
            held[j] = (left[j] + right[j].astype(jnp.float32)).astype(jnp.bfloat16)
            done.append(
                pltpu.make_async_copy(held.at[j], out.at[:, pl.ds(j * tile, tile)], out_sems.at[j])
            )
            done[-1].start()
        wait_all(done)

    anywhere = pl.BlockSpec(memory_space=pl.ANY)
    return pl.pallas_call(
        kernel,
        out_shape=jax.ShapeDtypeStruct((slab, window), jnp.bfloat16),
        in_specs=[anywhere] * 2,
        out_specs=anywhere,
        scratch_shapes=[
            pltpu.VMEM((tiles, slab, tile), jnp.float32),
            pltpu.VMEM((tiles, slab, tile), jnp.bfloat16),
            pltpu.VMEM((tiles, slab, tile), jnp.bfloat16),
            pltpu.SemaphoreType.DMA((tiles, 2)),
            pltpu.SemaphoreType.DMA((tiles,)),
        ],
        compiler_params=pltpu.CompilerParams(vmem_limit_bytes=6 * MIB),
        cost_estimate=SMALL,
    )(keep, came)


def cut_shares(position, keep, came, came2, rows, share):
    slab, window = keep.shape
    tile = tile_of(window)
    tiles = window // tile
    n_share = rows // share

    def kernel(keep, came, came2, own, *refs):
        sends = refs[: n_share - 1]
        left, right, total, own_held, send_held, sems, out_sems = refs[n_share - 1 :]
        copies = []
        for j in range(tiles):
            cols = pl.ds(j * tile, tile)
            copies.append(
                tile_copies(
                    [keep.at[:, cols], came.at[:, cols], came2.at[:, cols]],
                    [left.at[j], right.at[j, 0], right.at[j, 1]],
                    sems.at[j],
                )
            )
            start_all(copies[j])
        for j in range(tiles):
            wait_all(copies[j])
            block = (
                left[j] + right[j, 0].astype(jnp.float32) + right[j, 1].astype(jnp.float32)
            )
            total[j * tile : (j + 1) * tile, :] = block.T
        skip, place = position()
        done = []
        for k in [*range(1, n_share), 0]:
            first = skip + lax.rem(place + k, n_share) * share
            value = total[pl.ds(pl.multiple_of(first, 16), share), :]
            if k == 0:
                own_held[...] = value
                copy = pltpu.make_async_copy(own_held, own, out_sems.at[0])
            else:
                send_held[k - 1] = value.astype(jnp.bfloat16)
                copy = pltpu.make_async_copy(send_held.at[k - 1], sends[k - 1], out_sems.at[k])
            copy.start()
            done.append(copy)
        wait_all(done)

    anywhere = pl.BlockSpec(memory_space=pl.ANY)
    return pl.pallas_call(
        kernel,
        out_shape=[jax.ShapeDtypeStruct((share, slab), jnp.float32)]
        + [jax.ShapeDtypeStruct((share, slab), jnp.bfloat16)] * (n_share - 1),
        in_specs=[anywhere] * 3,
        out_specs=[anywhere] * n_share,
        scratch_shapes=[
            pltpu.VMEM((tiles, slab, tile), jnp.float32),
            pltpu.VMEM((tiles, 2, slab, tile), jnp.bfloat16),
            pltpu.VMEM((window, slab), jnp.float32),
            pltpu.VMEM((share, slab), jnp.float32),
            pltpu.VMEM((n_share - 1, share, slab), jnp.bfloat16),
            pltpu.SemaphoreType.DMA((tiles, 3)),
            pltpu.SemaphoreType.DMA((n_share,)),
        ],
        compiler_params=pltpu.CompilerParams(vmem_limit_bytes=9 * MIB),
        cost_estimate=SMALL,
    )(keep, came, came2)


def join(pieces):
    count = len(pieces)
    rows, slab = pieces[0].shape

    def kernel(*refs):
        out, held, sems = refs[count:]
        moves = tile_copies(refs[:count], [held.at[i] for i in range(count)], sems.at[0])
        start_all(moves)
        done = []
        for i in range(count):
            moves[i].wait()
            done.append(
                pltpu.make_async_copy(held.at[i], out.at[pl.ds(i * rows, rows)], sems.at[1, i])
            )
            done[-1].start()
        wait_all(done)

    anywhere = pl.BlockSpec(memory_space=pl.ANY)
    return pl.pallas_call(
        kernel,
        out_shape=jax.ShapeDtypeStruct((count * rows, slab), pieces[0].dtype),
        in_specs=[anywhere] * count,
        out_specs=anywhere,
        scratch_shapes=[
            pltpu.VMEM((count, rows, slab), pieces[0].dtype),
            pltpu.SemaphoreType.DMA((2, count)),
        ],
        compiler_params=pltpu.CompilerParams(vmem_limit_bytes=4 * MIB),
        cost_estimate=SMALL,
    )(*pieces)


def round_sum(own, came, kind):
    def kernel(own, came, out):
        out[...] = (own[...] + came[...]).astype(kind)

    whole = pl.BlockSpec(memory_space=pltpu.VMEM)
    return pl.pallas_call(
        kernel,
        out_shape=jax.ShapeDtypeStruct(own.shape, kind),
        in_specs=[whole, whole],
        out_specs=whole,
        compiler_params=pltpu.CompilerParams(vmem_limit_bytes=4 * MIB),
        cost_estimate=SMALL,
    )(own, came)


def finish_grad(own, came, bits):
    share, slab = own.shape

    def kernel(own, *refs):
        bits, table, out = refs[-3:]
        total = own[...]
        for ref in refs[:-3]:
            total = total + ref[...].astype(jnp.float32)
        total = total * (2 * bits[...] - 1).astype(jnp.float32)
        result = None
        for _ in range(3):
            part = total.astype(jnp.bfloat16)
            total = total - part.astype(jnp.float32)
            term = jnp.dot(part, table[...], preferred_element_type=jnp.float32)
            result = term if result is None else result + term
        out[...] = result * (1.0 / math.sqrt(128.0))

    table = np.kron(np.eye(slab // 128), sylvester())
    whole = pl.BlockSpec(memory_space=pltpu.VMEM)
    return pl.pallas_call(
        kernel,
        out_shape=jax.ShapeDtypeStruct((share, slab), jnp.float32),
        in_specs=[whole] * (3 + len(came)),
        out_specs=whole,
        compiler_params=pltpu.CompilerParams(vmem_limit_bytes=12 * MIB),
        cost_estimate=LONGER,
    )(own, *came, bits, jnp.asarray(table, jnp.bfloat16))


def output_part(position, tokens, fars, pieces, before, part, cost):
    depth = tokens.shape[0]
    slab = pieces[0][0].shape[1]
    places = len(fars)
    count = len(pieces)
    lead = part // 128 * 128
    width = fars[0].shape[1] - lead
    edge = width - part

    def kernel(tok, *refs):
        windows = refs[:places]
        parts = refs[places : places + count]
        refs = refs[places + count :]
        if before is not None:
            old = refs[:2]
            refs = refs[2:]
        own, other, left, right, held, sems, piece_sems, old_sems, out_sems = refs
        earlier = []
        if before is not None:
            earlier = tile_copies(old, [held.at[0], held.at[1]], old_sems)
            start_all(earlier)
        waits = []
        for i, (_, first, step, other_side) in enumerate(pieces):
            start, place, column, row = position(step, other_side)
            near = pltpu.make_async_copy(
                tok.at[:, pl.ds(pl.multiple_of(start, 128), width)],
                left.at[i, pl.ds(0, depth)],
                sems.at[i, 0],
            )
            near.start()
            cols = pl.ds(pl.multiple_of(column, 128), width)
            copies = [
                pltpu.make_async_copy(
                    window.at[:, cols], left.at[i, pl.ds(depth, depth)], sems.at[i, 1]
                )
                for window in windows
            ]
            for k in range(places):
                pl.when(place == k)(copies[k].start)
            right[i, 0:edge, :] = jnp.zeros((edge, slab), jnp.bfloat16)
            right[i, width - edge : width, :] = jnp.zeros((edge, slab), jnp.bfloat16)
            piece = pltpu.make_async_copy(
                parts[i].at[pl.ds(first, part)],
                right.at[i, pl.ds(pl.multiple_of(row, 16), part)],
                piece_sems.at[i],
            )
            piece.start()
            waits.append([near, copies[0], piece])
        total = None
        for i in range(count):
            wait_all(waits[i])
            term = jnp.dot(left[i], right[i], preferred_element_type=jnp.float32)
            total = term if total is None else total + term
        wait_all(earlier)
        done = []
        for k, out in ((1, other), (0, own)):
            value = total[k * depth : (k + 1) * depth]
            held[k] = value if before is None else value + held[k]
            done.append(pltpu.make_async_copy(held.at[k], out, out_sems.at[k]))
            done[-1].start()
        wait_all(done)

    anywhere = pl.BlockSpec(memory_space=pl.ANY)
    shape = jax.ShapeDtypeStruct((depth, slab), jnp.float32)
    olds = () if before is None else tuple(before)
    return pl.pallas_call(
        kernel,
        out_shape=[shape, shape],
        in_specs=[anywhere] * (1 + places + count + len(olds)),
        out_specs=[anywhere, anywhere],
        scratch_shapes=[
            pltpu.VMEM((count, 2 * depth, width), jnp.bfloat16),
            pltpu.VMEM((count, width, slab), jnp.bfloat16),
            pltpu.VMEM((2, depth, slab), jnp.float32),
            pltpu.SemaphoreType.DMA((count, 2)),
            pltpu.SemaphoreType.DMA((count,)),
            pltpu.SemaphoreType.DMA((2,)),
            pltpu.SemaphoreType.DMA((2,)),
        ],
        compiler_params=pltpu.CompilerParams(vmem_limit_bytes=MEMORY),
        cost_estimate=cost,
    )(tokens, *fars, *[array for array, *_ in pieces], *olds)


def paired(mesh):
    n_outer = mesh.shape["outer"]
    n_node = mesh.shape["node"]
    orders = [[1, 2], [2, 1]]

    def core_swap(value):
        return lax.ppermute(value, "outer", [(o, o ^ 1) for o in range(n_outer)])

    def outer_swap(value, stage):
        return lax.ppermute(
            value, "outer", [(o, o ^ (1 << orders[o % 2][stage])) for o in range(n_outer)]
        )

    def node_shift(value, step):
        return lax.ppermute(value, "node", [(n, (n + step) % n_node) for n in range(n_node)])

    def place_of(o):
        bits = o >> 1
        return jnp.where(o % 2 == 0, bits, (bits >> 1) + 2 * (bits % 2))

    def on_device(tokens, cotangent, weight_codes, weight_scales, weight_bits, grad_bits):
        o = lax.axis_index("outer")
        width = tokens.shape[1]
        rows = width // n_outer
        share = rows // n_node
        node_rows = weight_codes.shape[0]
        window = (rows + 127) // 128 * 128
        edge = window - rows
        masks = (3, 1, 2, 0)

        def column(mask, o, mine):
            base = o if mine else o ^ 1
            which = base ^ jnp.where(
                base % 2 == 0, relative_of(orders, 0, mask), relative_of(orders, 1, mask)
            )
            return which // 2 * node_rows + which % 2 * (node_rows - window)

        def take(source, mask):
            return lax.dynamic_slice_in_dim(source, column(mask, o, False), window, 1)

        cot_far = core_swap(cotangent)
        leave = take(after(tokens, cotangent), 3)
        source = after(tokens, leave)
        far3 = core_swap(leave)
        fars = [far3] + [core_swap(take(source, mask)) for mask in masks[1:]]

        def columns(*masks):
            return lambda: [column(mask, lax.axis_index("outer"), True) for mask in masks]

        (first,) = grad_blocks(
            columns(3), tokens, fars[:1], cotangent, cot_far, [jnp.bfloat16], LONG
        )
        came3 = outer_swap(first, 0)

        part = rows // 2

        def side_of(o):
            return jnp.where(o % 2 == 0, o >> 1, o >> 2) % 2

        start = o % 2 * rows + side_of(o) * part
        held = rotate(
            dequantize(
                lax.dynamic_slice_in_dim(after(weight_codes, first), start, part),
                lax.dynamic_slice_in_dim(after(weight_scales, first), start, part),
            ),
            after(weight_bits, first),
        ).astype(jnp.bfloat16)
        swap0 = outer_swap(held, 0)
        ahead = node_shift(held, 1)

        def position():
            return lax.axis_index("outer") % 2 * edge, lax.axis_index("node")

        def out_position(step, other_side):
            o = lax.axis_index("outer")
            n = lax.axis_index("node")
            core = o % 2
            node = lax.rem(n + n_node - step, n_node)
            side = side_of(o) if other_side == 0 else 1 - side_of(o)
            bits = place_of((node * 2 + core) ^ (o - core))
            place = jnp.where(bits == 3, 0, jnp.where(bits == 1, 1, jnp.where(bits == 2, 2, 3)))
            lead = part // 128 * 128
            start = node * node_rows + core * (node_rows - window) + side * lead
            return start, place, side * lead, core * edge + side * (part - lead)

        def product(pieces, before, later_than, cost):
            source = after(tokens, later_than)
            return output_part(out_position, source, fars, pieces, before, part, cost)

        second, keep2 = grad_blocks(
            columns(*masks[1:3]), after(tokens, held), fars[1:3], cotangent, cot_far,
            [jnp.bfloat16, jnp.float32], LONGER,
        )
        came1 = outer_swap(second, 0)
        passed = add_blocks(keep2, came3)
        came2 = outer_swap(passed, 1)
        behind = node_shift(after(held, passed), n_node - 1)
        (keep0,) = grad_blocks(
            columns(masks[3]), after(tokens, passed), fars[3:], cotangent, cot_far,
            [jnp.float32], SMALL,
        )
        early = product([(held, 0, 0, 0), (swap0, 0, 0, 1)], None, keep0, LONGER)
        ahead, *early = lax.optimization_barrier((ahead, *early))
        relay = node_shift(ahead, 1)
        joined = join([ahead, behind])
        came2, joined, _ = lax.optimization_barrier((came2, joined, keep0))
        own, *sends = cut_shares(position, keep0, came1, came2, rows, share)
        arrived = [node_shift(sends[step - 1], step) for step in range(1, n_node)]
        grad_rotated = finish_grad(own, arrived, grad_bits.reshape(1, -1))

        swap13 = outer_swap(joined, 0)
        sums = product(
            [(ahead, 0, 1, 0), (behind, 0, n_node - 1, 0), (relay, 0, 2, 0)],
            early, sends[0], MIDDLE,
        )
        swap2 = outer_swap(after(relay, *sends), 0)
        own_part, other_part = product(
            [(swap13, 0, 1, 1), (swap13, part, n_node - 1, 1), (swap2, 0, 2, 1)],
            sums, swap2, SMALL,
        )
        output = round_sum(own_part, core_swap(other_part), tokens.dtype)
        return output, grad_rotated

    return on_device


def general(mesh):
    n_outer = mesh.shape["outer"]
    n_node = mesh.shape["node"]
    n_bits = n_outer.bit_length() - 1
    orders = [list(range(1, n_bits)), [2, 1] + list(range(3, n_bits))]

    def outer_swap(value, stage):
        pairs = []
        for o in range(n_outer):
            pairs.append((o, o ^ (1 if stage is None else 1 << orders[o % 2][stage])))
        return lax.ppermute(value, "outer", pairs)

    def node_shift(value, step):
        return lax.ppermute(value, "node", [(n, (n + step) % n_node) for n in range(n_node)])

    def on_device(tokens, cotangent, weight_codes, weight_scales, weight_bits, grad_bits):
        o = lax.axis_index("outer")
        n = lax.axis_index("node")
        core = o % 2
        width = tokens.shape[1]
        slab = cotangent.shape[1]

        part = weight_codes.shape[0] // 4
        side = jnp.where(core == 0, (o >> orders[0][0]) % 2, (o >> orders[1][0]) % 2)
        mate_side = jnp.where(core == 0, (o >> orders[1][0]) % 2, (o >> orders[0][0]) % 2)
        quarter = core * 2 + side
        start = quarter * part
        held = rotate(
            dequantize(
                lax.dynamic_slice_in_dim(weight_codes, start, part),
                lax.dynamic_slice_in_dim(weight_scales, start, part),
            ),
            weight_bits,
        ).astype(jnp.bfloat16)

        total = lax.dot_general(
            tokens, cotangent, (((0,), (0,)), ((), ())), preferred_element_type=jnp.float32
        ).astype(jnp.bfloat16)
        rows = width // n_outer
        blocks = {}

        def own(d):
            return lax.dynamic_slice_in_dim(total, (o ^ d) * rows, rows)

        def relative(mask):
            found = [0, 0]
            for c in range(2):
                for j, bit in enumerate(orders[c]):
                    if mask >> j & 1:
                        found[c] |= 1 << bit
            return jnp.where(core == 0, found[0], found[1])

        n_rest = n_bits - 1
        sums = {}
        for mask in reversed(range(2**n_rest)):
            partner = jnp.where(core == 0, relative_of(orders, 1, mask), relative_of(orders, 0, mask))
            came = outer_swap(own(partner ^ 1), None)
            sums[mask] = own(relative(mask)).astype(jnp.float32) + came.astype(jnp.float32)
        for stage in range(n_rest):
            low = 1 << stage
            for mask in sorted([m for m in sums if m & low], reverse=True):
                came = outer_swap(sums.pop(mask).astype(jnp.bfloat16), stage)
                sums[mask ^ low] = sums[mask ^ low] + came.astype(jnp.float32)
        mine = sums[0]
        share = rows // n_node
        send = mine.astype(jnp.bfloat16)
        grad = lax.dynamic_slice_in_dim(mine, n * share, share)
        for step in range(1, n_node):
            piece = lax.dynamic_slice_in_dim(send, (n + step) % n_node * share, share)
            grad = grad + node_shift(piece, step).astype(jnp.float32)
        grad_rotated = rotate(grad, grad_bits)

        weight = jnp.zeros((width, slab), jnp.bfloat16)
        node_rows = weight_codes.shape[0]
        for step in range(n_node):
            base = (n - step) % n_node * node_rows
            across = outer_swap(held, 0)
            mate = outer_swap(held, None)
            mate_across = outer_swap(across, None)
            pieces = [
                (held, core * 2 + side),
                (across, core * 2 + 1 - side),
                (mate, (1 - core) * 2 + mate_side),
                (mate_across, (1 - core) * 2 + 1 - mate_side),
            ]
            for value, place in pieces:
                weight = lax.dynamic_update_slice_in_dim(weight, value, base + place * part, 0)
            if step < n_node - 1:
                held = node_shift(held, 1)
        output = jnp.dot(tokens, weight, preferred_element_type=jnp.float32).astype(jnp.bfloat16)
        return output, grad_rotated

    return on_device


def solution(mesh):
    n_outer = mesh.shape["outer"]
    n_node = mesh.shape["node"]
    on_device = paired(mesh) if n_outer == 8 and n_node == 4 else general(mesh)
    return jax.shard_map(
        on_device,
        mesh=mesh,
        in_specs=(
            P(("outer", "node"), None),
            P(("outer", "node"), None),
            P("node", None),
            P("node", None),
            P(),
            P(),
        ),
        out_specs=(P(("outer", "node"), None), P(("outer", "node"), None)),
        check_vma=False,
    )
```

```python
import math

import jax
import jax.numpy as jnp
import numpy as np
from jax import lax
from jax.experimental import pallas as pl
from jax.experimental.pallas import tpu as pltpu
from jax.sharding import PartitionSpec as P


def sylvester():
    row_index = np.arange(128).reshape(128, 1)
    column_index = np.arange(128).reshape(1, 128)
    parity = np.zeros((128, 128))
    for level in range(7):
        parity = parity + row_index // 2**level % 2 * (column_index // 2**level % 2)
    return 1.0 - 2.0 * (parity % 2)


def rotate(values, bits):
    width = values.shape[1]
    signs = (2 * bits - 1).astype(jnp.float32)
    table = np.kron(np.eye(width // 128), sylvester()) / math.sqrt(128.0)
    return jnp.dot(
        values * signs,
        jnp.asarray(table, jnp.float32),
        precision=lax.Precision.HIGHEST,
    )


def dequantize(codes, scales):
    height, width = codes.shape
    spread = jnp.concatenate(
        [
            jnp.broadcast_to(scales[:, block : block + 1], (height, 128))
            for block in range(width // 128)
        ],
        axis=1,
    )
    return codes.astype(jnp.float32) * spread


def relative_of(orders, core, mask):
    found = 0
    for j, bit in enumerate(orders[core]):
        if mask >> j & 1:
            found |= 1 << bit
    return found


SMALL = pl.CostEstimate(flops=0, bytes_accessed=1024, transcendentals=0)
LONG = pl.CostEstimate(flops=5 * 10**9, bytes_accessed=1024, transcendentals=0)
MIDDLE = pl.CostEstimate(flops=8 * 10**9, bytes_accessed=1024, transcendentals=0)
MORE = pl.CostEstimate(flops=15 * 10**9, bytes_accessed=1024, transcendentals=0)
LONGER = pl.CostEstimate(flops=6 * 10**10, bytes_accessed=1024, transcendentals=0)
MIB = 2**20
MEMORY = 56 * MIB


def after(value, *deps):
    return lax.optimization_barrier((value, *deps))[0]


def tile_of(window):
    return max(128 * k for k in range(1, 6) if window % (128 * k) == 0)


def tile_copies(sources, dests, sems):
    return [
        pltpu.make_async_copy(source, dest, sems.at[i])
        for i, (source, dest) in enumerate(zip(sources, dests))
    ]


def start_all(copies):
    for copy in copies:
        copy.start()


def wait_all(copies):
    for copy in copies:
        copy.wait()


def grad_blocks(columns, tokens, fars, cot, cot_far, kinds, cost):
    count = len(fars)
    depth, slab = cot.shape
    window = fars[0].shape[1]
    tile = tile_of(window)
    tiles = window // tile

    def kernel(tok, cot, cot_far, *refs):
        far_refs, outs = refs[:count], refs[count : 2 * count]
        cots, left, sems, cot_sems, out_sems = refs[2 * count : 2 * count + 5]
        held = refs[2 * count + 5 :]
        first = columns()
        ends = tile_copies([cot, cot_far], [cots.at[0], cots.at[1]], cot_sems)
        start_all(ends)
        copies = {}
        for i in range(count):
            for j in range(tiles):
                near = tok.at[:, pl.ds(pl.multiple_of(first[i] + j * tile, 128), tile)]
                far = far_refs[i].at[:, pl.ds(j * tile, tile)]
                copies[i, j] = tile_copies(
                    [near, far], [left.at[i, j, 0], left.at[i, j, 1]], sems.at[i, j]
                )
                start_all(copies[i, j])
        wait_all(ends)
        mine, theirs = cots[0].T, cots[1].T
        done = []
        for i in range(count):
            for j in range(tiles):
                wait_all(copies[i, j])
                held[i][j] = (
                    jnp.dot(mine, left[i, j, 0], preferred_element_type=jnp.float32)
                    + jnp.dot(theirs, left[i, j, 1], preferred_element_type=jnp.float32)
                ).astype(kinds[i])
                done.append(
                    pltpu.make_async_copy(
                        held[i].at[j], outs[i].at[:, pl.ds(j * tile, tile)], out_sems.at[i, j]
                    )
                )
                done[-1].start()
        wait_all(done)

    anywhere = pl.BlockSpec(memory_space=pl.ANY)
    return pl.pallas_call(
        kernel,
        out_shape=[jax.ShapeDtypeStruct((slab, window), kind) for kind in kinds],
        in_specs=[anywhere] * (3 + count),
        out_specs=[anywhere] * count,
        scratch_shapes=[
            pltpu.VMEM((2, depth, slab), jnp.bfloat16),
            pltpu.VMEM((count, tiles, 2, depth, tile), jnp.bfloat16),
            pltpu.SemaphoreType.DMA((count, tiles, 2)),
            pltpu.SemaphoreType.DMA((2,)),
            pltpu.SemaphoreType.DMA((count, tiles)),
        ]
        + [pltpu.VMEM((tiles, slab, tile), kind) for kind in kinds],
        compiler_params=pltpu.CompilerParams(vmem_limit_bytes=MEMORY),
        cost_estimate=cost,
    )(tokens, cot, cot_far, *fars)


def add_blocks(keep, came):
    slab, window = keep.shape
    tile = tile_of(window)
    tiles = window // tile

    def kernel(keep, came, out, left, right, held, sems, out_sems):
        copies = []
        for j in range(tiles):
            cols = pl.ds(j * tile, tile)
            copies.append(
                tile_copies(
                    [keep.at[:, cols], came.at[:, cols]], [left.at[j], right.at[j]], sems.at[j]
                )
            )
            start_all(copies[j])
        done = []
        for j in range(tiles):
            wait_all(copies[j])
            held[j] = (left[j] + right[j].astype(jnp.float32)).astype(jnp.bfloat16)
            done.append(
                pltpu.make_async_copy(held.at[j], out.at[:, pl.ds(j * tile, tile)], out_sems.at[j])
            )
            done[-1].start()
        wait_all(done)

    anywhere = pl.BlockSpec(memory_space=pl.ANY)
    return pl.pallas_call(
        kernel,
        out_shape=jax.ShapeDtypeStruct((slab, window), jnp.bfloat16),
        in_specs=[anywhere] * 2,
        out_specs=anywhere,
        scratch_shapes=[
            pltpu.VMEM((tiles, slab, tile), jnp.float32),
            pltpu.VMEM((tiles, slab, tile), jnp.bfloat16),
            pltpu.VMEM((tiles, slab, tile), jnp.bfloat16),
            pltpu.SemaphoreType.DMA((tiles, 2)),
            pltpu.SemaphoreType.DMA((tiles,)),
        ],
        compiler_params=pltpu.CompilerParams(vmem_limit_bytes=6 * MIB),
        cost_estimate=SMALL,
    )(keep, came)


def cut_shares(position, keep, came, came2, rows, share):
    slab, window = keep.shape
    tile = tile_of(window)
    tiles = window // tile
    n_share = rows // share

    def kernel(keep, came, came2, own, *refs):
        sends = refs[: n_share - 1]
        left, right, total, own_held, send_held, sems, out_sems = refs[n_share - 1 :]
        copies = []
        for j in range(tiles):
            cols = pl.ds(j * tile, tile)
            copies.append(
                tile_copies(
                    [keep.at[:, cols], came.at[:, cols], came2.at[:, cols]],
                    [left.at[j], right.at[j, 0], right.at[j, 1]],
                    sems.at[j],
                )
            )
            start_all(copies[j])
        for j in range(tiles):
            wait_all(copies[j])
            block = (
                left[j] + right[j, 0].astype(jnp.float32) + right[j, 1].astype(jnp.float32)
            )
            total[j * tile : (j + 1) * tile, :] = block.T
        skip, place = position()
        done = []
        for k in [*range(1, n_share), 0]:
            first = skip + lax.rem(place + k, n_share) * share
            value = total[pl.ds(pl.multiple_of(first, 16), share), :]
            if k == 0:
                own_held[...] = value
                copy = pltpu.make_async_copy(own_held, own, out_sems.at[0])
            else:
                send_held[k - 1] = value.astype(jnp.bfloat16)
                copy = pltpu.make_async_copy(send_held.at[k - 1], sends[k - 1], out_sems.at[k])
            copy.start()
            done.append(copy)
        wait_all(done)

    anywhere = pl.BlockSpec(memory_space=pl.ANY)
    return pl.pallas_call(
        kernel,
        out_shape=[jax.ShapeDtypeStruct((share, slab), jnp.float32)]
        + [jax.ShapeDtypeStruct((share, slab), jnp.bfloat16)] * (n_share - 1),
        in_specs=[anywhere] * 3,
        out_specs=[anywhere] * n_share,
        scratch_shapes=[
            pltpu.VMEM((tiles, slab, tile), jnp.float32),
            pltpu.VMEM((tiles, 2, slab, tile), jnp.bfloat16),
            pltpu.VMEM((window, slab), jnp.float32),
            pltpu.VMEM((share, slab), jnp.float32),
            pltpu.VMEM((n_share - 1, share, slab), jnp.bfloat16),
            pltpu.SemaphoreType.DMA((tiles, 3)),
            pltpu.SemaphoreType.DMA((n_share,)),
        ],
        compiler_params=pltpu.CompilerParams(vmem_limit_bytes=9 * MIB),
        cost_estimate=SMALL,
    )(keep, came, came2)


def join(pieces):
    count = len(pieces)
    rows, slab = pieces[0].shape

    def kernel(*refs):
        out, held, sems = refs[count:]
        moves = tile_copies(refs[:count], [held.at[i] for i in range(count)], sems.at[0])
        start_all(moves)
        done = []
        for i in range(count):
            moves[i].wait()
            done.append(
                pltpu.make_async_copy(held.at[i], out.at[pl.ds(i * rows, rows)], sems.at[1, i])
            )
            done[-1].start()
        wait_all(done)

    anywhere = pl.BlockSpec(memory_space=pl.ANY)
    return pl.pallas_call(
        kernel,
        out_shape=jax.ShapeDtypeStruct((count * rows, slab), pieces[0].dtype),
        in_specs=[anywhere] * count,
        out_specs=anywhere,
        scratch_shapes=[
            pltpu.VMEM((count, rows, slab), pieces[0].dtype),
            pltpu.SemaphoreType.DMA((2, count)),
        ],
        compiler_params=pltpu.CompilerParams(vmem_limit_bytes=4 * MIB),
        cost_estimate=SMALL,
    )(*pieces)


def round_sum(own, came, kind):
    def kernel(own, came, out):
        out[...] = (own[...] + came[...]).astype(kind)

    whole = pl.BlockSpec(memory_space=pltpu.VMEM)
    return pl.pallas_call(
        kernel,
        out_shape=jax.ShapeDtypeStruct(own.shape, kind),
        in_specs=[whole, whole],
        out_specs=whole,
        compiler_params=pltpu.CompilerParams(vmem_limit_bytes=4 * MIB),
        cost_estimate=SMALL,
    )(own, came)


def finish_grad(own, came, bits):
    share, slab = own.shape

    def kernel(own, *refs):
        bits, table, out = refs[-3:]
        total = own[...]
        for ref in refs[:-3]:
            total = total + ref[...].astype(jnp.float32)
        total = total * (2 * bits[...] - 1).astype(jnp.float32)
        result = None
        for _ in range(3):
            part = total.astype(jnp.bfloat16)
            total = total - part.astype(jnp.float32)
            term = jnp.dot(part, table[...], preferred_element_type=jnp.float32)
            result = term if result is None else result + term
        out[...] = result * (1.0 / math.sqrt(128.0))

    table = np.kron(np.eye(slab // 128), sylvester())
    whole = pl.BlockSpec(memory_space=pltpu.VMEM)
    return pl.pallas_call(
        kernel,
        out_shape=jax.ShapeDtypeStruct((share, slab), jnp.float32),
        in_specs=[whole] * (3 + len(came)),
        out_specs=whole,
        compiler_params=pltpu.CompilerParams(vmem_limit_bytes=12 * MIB),
        cost_estimate=LONGER,
    )(own, *came, bits, jnp.asarray(table, jnp.bfloat16))


def output_part(position, tokens, fars, pieces, before, part, cost):
    depth = tokens.shape[0]
    slab = pieces[0][0].shape[1]
    places = len(fars)
    count = len(pieces)
    lead = part // 128 * 128
    width = fars[0].shape[1] - lead
    edge = width - part

    def kernel(tok, *refs):
        windows = refs[:places]
        parts = refs[places : places + count]
        refs = refs[places + count :]
        if before is not None:
            old = refs[:2]
            refs = refs[2:]
        own, other, left, right, held, sems, piece_sems, old_sems, out_sems = refs
        earlier = []
        if before is not None:
            earlier = tile_copies(old, [held.at[0], held.at[1]], old_sems)
            start_all(earlier)
        waits = []
        for i, (_, first, step, other_side) in enumerate(pieces):
            start, place, column, row = position(step, other_side)
            near = pltpu.make_async_copy(
                tok.at[:, pl.ds(pl.multiple_of(start, 128), width)],
                left.at[i, pl.ds(0, depth)],
                sems.at[i, 0],
            )
            near.start()
            cols = pl.ds(pl.multiple_of(column, 128), width)
            copies = [
                pltpu.make_async_copy(
                    window.at[:, cols], left.at[i, pl.ds(depth, depth)], sems.at[i, 1]
                )
                for window in windows
            ]
            for k in range(places):
                pl.when(place == k)(copies[k].start)
            right[i, 0:edge, :] = jnp.zeros((edge, slab), jnp.bfloat16)
            right[i, width - edge : width, :] = jnp.zeros((edge, slab), jnp.bfloat16)
            piece = pltpu.make_async_copy(
                parts[i].at[pl.ds(first, part)],
                right.at[i, pl.ds(pl.multiple_of(row, 16), part)],
                piece_sems.at[i],
            )
            piece.start()
            waits.append([near, copies[0], piece])
        total = None
        for i in range(count):
            wait_all(waits[i])
            term = jnp.dot(left[i], right[i], preferred_element_type=jnp.float32)
            total = term if total is None else total + term
        wait_all(earlier)
        done = []
        for k, out in ((1, other), (0, own)):
            value = total[k * depth : (k + 1) * depth]
            held[k] = value if before is None else value + held[k]
            done.append(pltpu.make_async_copy(held.at[k], out, out_sems.at[k]))
            done[-1].start()
        wait_all(done)

    anywhere = pl.BlockSpec(memory_space=pl.ANY)
    shape = jax.ShapeDtypeStruct((depth, slab), jnp.float32)
    olds = () if before is None else tuple(before)
    return pl.pallas_call(
        kernel,
        out_shape=[shape, shape],
        in_specs=[anywhere] * (1 + places + count + len(olds)),
        out_specs=[anywhere, anywhere],
        scratch_shapes=[
            pltpu.VMEM((count, 2 * depth, width), jnp.bfloat16),
            pltpu.VMEM((count, width, slab), jnp.bfloat16),
            pltpu.VMEM((2, depth, slab), jnp.float32),
            pltpu.SemaphoreType.DMA((count, 2)),
            pltpu.SemaphoreType.DMA((count,)),
            pltpu.SemaphoreType.DMA((2,)),
            pltpu.SemaphoreType.DMA((2,)),
        ],
        compiler_params=pltpu.CompilerParams(vmem_limit_bytes=MEMORY),
        cost_estimate=cost,
    )(tokens, *fars, *[array for array, *_ in pieces], *olds)


def paired(mesh):
    n_outer = mesh.shape["outer"]
    n_node = mesh.shape["node"]
    orders = [[1, 2], [2, 1]]

    def core_swap(value):
        return lax.ppermute(value, "outer", [(o, o ^ 1) for o in range(n_outer)])

    def outer_swap(value, stage):
        return lax.ppermute(
            value, "outer", [(o, o ^ (1 << orders[o % 2][stage])) for o in range(n_outer)]
        )

    def node_shift(value, step):
        return lax.ppermute(value, "node", [(n, (n + step) % n_node) for n in range(n_node)])

    def place_of(o):
        bits = o >> 1
        return jnp.where(o % 2 == 0, bits, (bits >> 1) + 2 * (bits % 2))

    def on_device(tokens, cotangent, weight_codes, weight_scales, weight_bits, grad_bits):
        o = lax.axis_index("outer")
        width = tokens.shape[1]
        rows = width // n_outer
        share = rows // n_node
        node_rows = weight_codes.shape[0]
        window = (rows + 127) // 128 * 128
        edge = window - rows
        masks = (3, 1, 2, 0)

        def column(mask, o, mine):
            base = o if mine else o ^ 1
            which = base ^ jnp.where(
                base % 2 == 0, relative_of(orders, 0, mask), relative_of(orders, 1, mask)
            )
            return which // 2 * node_rows + which % 2 * (node_rows - window)

        def take(source, mask):
            return lax.dynamic_slice_in_dim(source, column(mask, o, False), window, 1)

        cot_far = core_swap(cotangent)
        leave = take(after(tokens, cotangent), 3)
        source = after(tokens, leave)
        far3 = core_swap(leave)
        fars = [far3] + [core_swap(take(source, mask)) for mask in masks[1:]]

        def columns(*masks):
            return lambda: [column(mask, lax.axis_index("outer"), True) for mask in masks]

        (first,) = grad_blocks(
            columns(3), tokens, fars[:1], cotangent, cot_far, [jnp.bfloat16], LONG
        )
        came3 = outer_swap(first, 0)

        part = rows // 2

        def side_of(o):
            return jnp.where(o % 2 == 0, o >> 1, o >> 2) % 2

        start = o % 2 * rows + side_of(o) * part
        held = rotate(
            dequantize(
                lax.dynamic_slice_in_dim(after(weight_codes, first), start, part),
                lax.dynamic_slice_in_dim(after(weight_scales, first), start, part),
            ),
            after(weight_bits, first),
        ).astype(jnp.bfloat16)
        swap0 = outer_swap(held, 0)
        ahead = node_shift(held, 1)

        def position():
            return lax.axis_index("outer") % 2 * edge, lax.axis_index("node")

        def out_position(step, other_side):
            o = lax.axis_index("outer")
            n = lax.axis_index("node")
            core = o % 2
            node = lax.rem(n + n_node - step, n_node)
            side = side_of(o) if other_side == 0 else 1 - side_of(o)
            bits = place_of((node * 2 + core) ^ (o - core))
            place = jnp.where(bits == 3, 0, jnp.where(bits == 1, 1, jnp.where(bits == 2, 2, 3)))
            lead = part // 128 * 128
            start = node * node_rows + core * (node_rows - window) + side * lead
            return start, place, side * lead, core * edge + side * (part - lead)

        def product(pieces, before, later_than, cost):
            source = after(tokens, later_than)
            return output_part(out_position, source, fars, pieces, before, part, cost)

        second, keep2 = grad_blocks(
            columns(*masks[1:3]), after(tokens, held), fars[1:3], cotangent, cot_far,
            [jnp.bfloat16, jnp.float32], LONGER,
        )
        came1 = outer_swap(second, 0)
        passed = add_blocks(keep2, came3)
        came2 = outer_swap(passed, 1)
        behind = node_shift(after(held, passed), n_node - 1)
        (keep0,) = grad_blocks(
            columns(masks[3]), after(tokens, passed), fars[3:], cotangent, cot_far,
            [jnp.float32], SMALL,
        )
        early = product([(held, 0, 0, 0), (swap0, 0, 0, 1)], None, keep0, LONGER)
        ahead, *early = lax.optimization_barrier((ahead, *early))
        relay = node_shift(ahead, 1)
        joined = join([ahead, behind])
        came2, joined, _ = lax.optimization_barrier((came2, joined, keep0))
        own, *sends = cut_shares(position, keep0, came1, came2, rows, share)
        order = sorted(range(1, n_node), key=lambda step: abs(2 * step - n_node))
        arrived = [node_shift(sends[step - 1], step) for step in order]
        grad_rotated = finish_grad(own, arrived, grad_bits.reshape(1, -1))

        swap13 = outer_swap(joined, 0)
        sums = product(
            [(ahead, 0, 1, 0), (behind, 0, n_node - 1, 0), (relay, 0, 2, 0)],
            early, sends[0], MIDDLE,
        )
        swap2 = outer_swap(after(relay, *sends), 0)
        own_part, other_part = product(
            [(swap13, 0, 1, 1), (swap13, part, n_node - 1, 1), (swap2, 0, 2, 1)],
            sums, swap2, SMALL,
        )
        output = round_sum(own_part, core_swap(other_part), tokens.dtype)
        return output, grad_rotated

    return on_device


def general(mesh):
    n_outer = mesh.shape["outer"]
    n_node = mesh.shape["node"]
    n_bits = n_outer.bit_length() - 1
    orders = [list(range(1, n_bits)), [2, 1] + list(range(3, n_bits))]

    def outer_swap(value, stage):
        pairs = []
        for o in range(n_outer):
            pairs.append((o, o ^ (1 if stage is None else 1 << orders[o % 2][stage])))
        return lax.ppermute(value, "outer", pairs)

    def node_shift(value, step):
        return lax.ppermute(value, "node", [(n, (n + step) % n_node) for n in range(n_node)])

    def on_device(tokens, cotangent, weight_codes, weight_scales, weight_bits, grad_bits):
        o = lax.axis_index("outer")
        n = lax.axis_index("node")
        core = o % 2
        width = tokens.shape[1]
        slab = cotangent.shape[1]

        part = weight_codes.shape[0] // 4
        side = jnp.where(core == 0, (o >> orders[0][0]) % 2, (o >> orders[1][0]) % 2)
        mate_side = jnp.where(core == 0, (o >> orders[1][0]) % 2, (o >> orders[0][0]) % 2)
        quarter = core * 2 + side
        start = quarter * part
        held = rotate(
            dequantize(
                lax.dynamic_slice_in_dim(weight_codes, start, part),
                lax.dynamic_slice_in_dim(weight_scales, start, part),
            ),
            weight_bits,
        ).astype(jnp.bfloat16)

        total = lax.dot_general(
            tokens, cotangent, (((0,), (0,)), ((), ())), preferred_element_type=jnp.float32
        ).astype(jnp.bfloat16)
        rows = width // n_outer
        blocks = {}

        def own(d):
            return lax.dynamic_slice_in_dim(total, (o ^ d) * rows, rows)

        def relative(mask):
            found = [0, 0]
            for c in range(2):
                for j, bit in enumerate(orders[c]):
                    if mask >> j & 1:
                        found[c] |= 1 << bit
            return jnp.where(core == 0, found[0], found[1])

        n_rest = n_bits - 1
        sums = {}
        for mask in reversed(range(2**n_rest)):
            partner = jnp.where(core == 0, relative_of(orders, 1, mask), relative_of(orders, 0, mask))
            came = outer_swap(own(partner ^ 1), None)
            sums[mask] = own(relative(mask)).astype(jnp.float32) + came.astype(jnp.float32)
        for stage in range(n_rest):
            low = 1 << stage
            for mask in sorted([m for m in sums if m & low], reverse=True):
                came = outer_swap(sums.pop(mask).astype(jnp.bfloat16), stage)
                sums[mask ^ low] = sums[mask ^ low] + came.astype(jnp.float32)
        mine = sums[0]
        share = rows // n_node
        send = mine.astype(jnp.bfloat16)
        grad = lax.dynamic_slice_in_dim(mine, n * share, share)
        for step in range(1, n_node):
            piece = lax.dynamic_slice_in_dim(send, (n + step) % n_node * share, share)
            grad = grad + node_shift(piece, step).astype(jnp.float32)
        grad_rotated = rotate(grad, grad_bits)

        weight = jnp.zeros((width, slab), jnp.bfloat16)
        node_rows = weight_codes.shape[0]
        for step in range(n_node):
            base = (n - step) % n_node * node_rows
            across = outer_swap(held, 0)
            mate = outer_swap(held, None)
            mate_across = outer_swap(across, None)
            pieces = [
                (held, core * 2 + side),
                (across, core * 2 + 1 - side),
                (mate, (1 - core) * 2 + mate_side),
                (mate_across, (1 - core) * 2 + 1 - mate_side),
            ]
            for value, place in pieces:
                weight = lax.dynamic_update_slice_in_dim(weight, value, base + place * part, 0)
            if step < n_node - 1:
                held = node_shift(held, 1)
        output = jnp.dot(tokens, weight, preferred_element_type=jnp.float32).astype(jnp.bfloat16)
        return output, grad_rotated

    return on_device


def solution(mesh):
    n_outer = mesh.shape["outer"]
    n_node = mesh.shape["node"]
    on_device = paired(mesh) if n_outer == 8 and n_node == 4 else general(mesh)
    return jax.shard_map(
        on_device,
        mesh=mesh,
        in_specs=(
            P(("outer", "node"), None),
            P(("outer", "node"), None),
            P("node", None),
            P("node", None),
            P(),
            P(),
        ),
        out_specs=(P(("outer", "node"), None), P(("outer", "node"), None)),
        check_vma=False,
    )
```
